32 devices in a mesh: ens: 2 (over y), pw: 8 (over z, x), band: 2 (over core).
Axes of the slice: x: 2, y: 2, z: 4, core: 2. Of those that a mesh axis runs over, the one named last changes fastest.
Arguments:
- trial_block: bfloat16 [4, 8, 6144], P('ens', 'band', 'pw'), parts along dimension 0, may hold values from -12 to 12
- all_bands: bfloat16 [4, 2048, 6144], P('ens', 'band', 'pw'), parts along dimension 0, may hold values from -0.078125 to 0.078125
- potential: float32 [256, 128, 128], P('ens', 'pw'), parts along dimension 0, may hold values from -8 to 8
- rest_density: float32 [256, 128, 128], P(('ens', 'band'), 'pw'), parts along dimension 0, may hold values from 0.05 to 0.4
- wave_cells: int32 [6144], P('pw'), may hold values from 0 to 262143, as said below
- kinetic: float32 [6144], P('pw'), may hold values from 0.1 to 8.4
- occupation: int32 [16], P(('ens', 'band')), parts along dimension 0, may hold values from 0 to 2
Outputs:
- correction: float32 [4, 8, 6144], P('ens', 'band', 'pw'), parts along dimension 0
- subspace_block: float32 [4, 2048, 8], P('ens', 'band'), parts along dimension 0
- density: float32 [256, 128, 128], P(('ens', 'band'), 'pw'), parts along dimension 0
The draws below stay inside these ranges and needn't reach their ends.
There are 2 independent parts, one for each index of `ens`. The reference program is written for one: setup_inputs(seed, part) draws one part's arguments, and reference() takes and returns one part's arrays. A program takes and returns all parts, laid end to end along the dimension named above; an argument that names none is the same for every part. Nothing has to cross between parts.
Inputs may be any that keep to these rules, and one draw needn't show every extreme that they name: `wave_cells`: within the 768 plane waves of one device the values are distinct, and 0 and 262143 occur among them.
All inputs are finite; a program needn't handle non-finite values.
Results may differ from the reference program's by a relative error of at most 0.0056.
Values may be sent and summed in bfloat16 or wider, within the bound.
No kernel may reach another device: no remote copies, remote signals or barrier semaphores. Data moves between devices by JAX's collectives and lax.ppermute only.
A program may use at most 576 MiB of HBM per device.

```python
import math
import jax
import jax.numpy as jnp
from jax import lax

NA = 128
NB = 128
NC = 128
NBANDS = 2048
NBLK = 8
PW_DEV = 768
NPW = 6144
SLAB = 262144
N_PW = 8


def draw_trial_block(key, part):
    position = jnp.arange(NPW, dtype=jnp.float32) / NPW
    shape_key, scale_key = jax.random.split(jax.random.fold_in(key, 11))
    falloff = 1.0 / jnp.sqrt(1.0 + 9.0 * position)
    scales = jnp.exp(jax.random.uniform(scale_key, (1, NBLK, 1), jnp.float32, math.log(0.3), math.log(3.0)))
    values = jax.random.truncated_normal(shape_key, -4.0, 4.0, (2, NBLK, NPW), jnp.float32)
    return (values * falloff * scales).astype(jnp.bfloat16)


def draw_kinetic(key, part):
    position = jnp.arange(NPW, dtype=jnp.float32) / NPW
    baseline = 0.2 + 4.0 * position
    rough_key = jax.random.fold_in(key, 13)
    rough = jnp.exp(jax.random.uniform(rough_key, (NPW,), jnp.float32, math.log(0.5), math.log(2.0)))
    return baseline * rough


def draw_wave_cells(key, part):
    devices = NPW // PW_DEV
    slots = SLAB

    def one_device(subkey):
        first_key, second_key = jax.random.split(subkey)
        middle = jax.random.permutation(first_key, slots - 2)[:PW_DEV - 2].astype(jnp.int32) + 1
        ends = jnp.array([0, slots - 1], jnp.int32)
        joined = jnp.concatenate([ends, middle])
        return joined[jax.random.permutation(second_key, PW_DEV)]
    device_keys = jax.random.split(jax.random.fold_in(key, 7), devices)
    return jax.vmap(one_device)(device_keys).reshape(-1).astype(jnp.int32)


def with_ends(entries, key, smallest, largest):
    dims = entries.shape
    index_at = [jax.random.randint(jax.random.fold_in(key, axis), (), 0, dims[axis]) for axis in range(len(dims))]
    entries = entries.at[tuple(index_at)].set(smallest)
    longest = dims.index(max(dims))
    index_at[longest] = (index_at[longest] + 1) % dims[longest]
    return entries.at[tuple(index_at)].set(largest)


def block_levels(rng, dims, shards, low, largest):
    loudness, own = 1.0, jax.random.fold_in(rng, 6)
    for dim, parts in shards:
        steps = jnp.exp(jax.random.uniform(jax.random.fold_in(own, dim), (parts,), jnp.float32, low / len(shards), largest / len(shards)))
        loudness = loudness * jnp.repeat(steps, dims[dim] // parts).reshape([-1 if axis == dim else 1 for axis in range(len(dims))])
    return loudness


def normal_values(own_key, shape, deviation, reach, shards=(), kind=jnp.bfloat16):
    result = deviation * jax.random.normal(own_key, shape, jnp.float32)
    if shards:
        result = result * block_levels(own_key, shape, shards, -0.22, 0.18)
    return jnp.clip(result, -reach, reach).astype(kind)


def setup_inputs(seed: int = 0, part: int = 0) -> dict:
    keys = jax.random.split(jax.random.key(seed), 8)
    own_keys = jax.random.split(jax.random.fold_in(keys[7], part), 8)
    return {
        "trial_block": draw_trial_block(jax.random.fold_in(jax.random.fold_in(keys[7], part), 71), part),
        "all_bands": normal_values(own_keys[1], (2, NBANDS, NPW), NPW ** -0.5, 0.078125, ((1, 2), (2, 8))),
        "potential": normal_values(own_keys[2], (NA, NB, NC), 2.0, 8.0, ((1, 8),), jnp.float32),
        "rest_density": jnp.clip(0.05 + 0.35 * jax.random.uniform(own_keys[3], (NA, NB, NC), jnp.float32) ** block_levels(own_keys[3], (NA, NB, NC), ((0, 2), (1, 8)), -0.2, 0.2), 0.05, 0.4),
        "wave_cells": draw_wave_cells(jax.random.fold_in(keys[7], 71), part),
        "kinetic": draw_kinetic(jax.random.fold_in(keys[7], 71), part),
        "occupation": with_ends(jax.random.randint(own_keys[6], (NBLK,), 0, 3), jax.random.fold_in(own_keys[6], 1), 0, 2).astype(jnp.int32),
    }


EPSILON = 1e-6


def inner(left, right):
    contract = (((1,), (1,)), ((), ()))
    first = lax.dot_general(left[0], right[0], contract, preferred_element_type=jnp.float32)
    second = lax.dot_general(left[1], right[1], contract, preferred_element_type=jnp.float32)
    cross_one = lax.dot_general(left[0], right[1], contract, preferred_element_type=jnp.float32)
    cross_two = lax.dot_general(left[1], right[0], contract, preferred_element_type=jnp.float32)
    return jnp.stack([first + second, cross_one - cross_two])


def reference(trial_block, all_bands, potential, rest_density, wave_cells, kinetic, occupation):
    slab_cells = NA * NB * NC // N_PW
    plane_index = jnp.arange(NPW, dtype=jnp.int32)
    cells = (plane_index // PW_DEV) * slab_cells + wave_cells.astype(jnp.int32)
    trial_float = trial_block.astype(jnp.float32)
    weights = occupation.astype(jnp.float32)

    def one_band(total, inputs):
        real_coef, imag_coef, weight = inputs
        real_grid = jnp.zeros((NA * NB * NC,), jnp.float32).at[cells].set(real_coef)
        imag_grid = jnp.zeros((NA * NB * NC,), jnp.float32).at[cells].set(imag_coef)
        grid = lax.complex(real_grid, imag_grid).reshape(NA, NB, NC)
        spatial = jnp.fft.ifftn(grid, norm="ortho")
        power = jnp.real(spatial) * jnp.real(spatial) + jnp.imag(spatial) * jnp.imag(spatial)
        acted = jnp.fft.fftn(spatial * potential, norm="ortho").reshape(-1)[cells]
        return total + weight * power, (jnp.real(acted), jnp.imag(acted))

    start = jnp.zeros((NA, NB, NC), jnp.float32)
    total, (real_applied, imag_applied) = lax.scan(one_band, start, (trial_float[0], trial_float[1], weights))
    density = rest_density + total
    applied = jnp.stack([real_applied, imag_applied])
    action = kinetic * trial_float + applied
    action_half = action.astype(jnp.bfloat16)
    damping = 1.0 / (1.0 + kinetic)
    damped = (action * damping).astype(jnp.bfloat16)
    softened = (trial_float * damping).astype(jnp.bfloat16)
    numerator = jnp.sum(trial_float * action_half.astype(jnp.float32), axis=(0, 2))
    denominator = jnp.sum(trial_float * trial_float, axis=(0, 2))
    rayleigh = numerator / (denominator + EPSILON)
    subspace_block = inner(all_bands, action_half)
    coefficients = inner(all_bands, damped) - rayleigh * inner(all_bands, softened)
    coefficient_half = coefficients.astype(jnp.bfloat16)
    contract = (((0,), (0,)), ((), ()))
    real_real = lax.dot_general(coefficient_half[0], all_bands[0], contract, preferred_element_type=jnp.float32)
    imag_imag = lax.dot_general(coefficient_half[1], all_bands[1], contract, preferred_element_type=jnp.float32)
    imag_real = lax.dot_general(coefficient_half[1], all_bands[0], contract, preferred_element_type=jnp.float32)
    real_imag = lax.dot_general(coefficient_half[0], all_bands[1], contract, preferred_element_type=jnp.float32)
    projected = jnp.stack([real_real - imag_imag, imag_real + real_imag])
    correction = damped.astype(jnp.float32) - rayleigh[None, :, None] * softened.astype(jnp.float32) - projected
    return (correction, subspace_block, density)
```

```python
import functools
import math

import jax
import jax.numpy as jnp
import numpy as np
from jax import lax
from jax.experimental import pallas as pl
from jax.experimental.pallas import tpu as pltpu
from jax.sharding import PartitionSpec as P

EPSILON = 1e-06
HIGHEST = lax.Precision.HIGHEST
BF16 = jnp.bfloat16
F32 = jnp.float32
LANES = 128


def split_pair(values):
    high = values.astype(BF16)
    low = (values - high.astype(np.float64)).astype(BF16)
    return high, low


def wave_tables(devices, rows, width_first, width_second, width_third):
    half = rows // 2
    second = np.arange(width_second)
    steps = np.outer(2 * np.arange(half) + 1, second) % (2 * width_second)
    angles = steps * (math.pi / width_second)
    near = np.concatenate([np.cos(angles), np.sin(angles)])
    blocks = []
    for device in range(devices):
        middle = 2 * rows * device + rows - 1
        turns = (middle * second % (2 * width_second)) * (math.pi / width_second)
        centre = np.stack([np.cos(turns), np.sin(turns)])
        high, low = split_pair(centre)
        blocks.append(np.concatenate([near.astype(BF16), high, low]))
    second_table = np.stack(blocks)
    missing = -second_table.shape[1] % 16
    second_table = np.pad(second_table, ((0, 0), (0, missing), (0, 0)))
    third = np.arange(width_third)
    angles = (np.outer(third, third) % width_third) * (2 * math.pi / width_third)
    factor = 1.0 / math.sqrt(width_second * width_third)
    values = np.concatenate([np.cos(angles), np.sin(angles)]) * factor
    third_table = np.concatenate(split_pair(values), axis=1)
    first = np.arange(width_first)
    angles = (np.outer(first, first) % width_first) * (2 * math.pi / width_first)
    cosines = np.cos(angles) / math.sqrt(width_first)
    sines = np.sin(angles) / math.sqrt(width_first)
    back = np.block([[cosines, -sines], [sines, cosines]]).astype(BF16)
    fore = np.block([[cosines, sines], [-sines, cosines]]).astype(BF16)
    return second_table, third_table, back, fore


def grid_kernel(
    bands,
    waves_ref,
    second_ref,
    third_ref,
    back_ref,
    fore_ref,
    potential_ref,
    rest_ref,
    kinetic_ref,
    occupation_ref,
    sent_ref,
    own_ref,
    other_ref,
    phase_s,
    select_s,
    centre_s,
    coef_s,
    slab_s,
    acted_s,
    density_s,
    energy_s,
    square_s,
):
    devices, _, count = waves_ref.shape
    width_first, rows, width_third = potential_ref.shape
    slab = width_first // devices
    half = rows // 2
    wide = bands * width_third
    me = lax.axis_index("pw")
    side = lax.axis_index("band")
    nt = (((1,), (1,)), ((), ()))
    tn = (((0,), (0,)), ((), ()))
    near = second_ref[me]
    square_s[...] = jnp.zeros_like(square_s)
    energy_s[...] = jnp.zeros_like(energy_s)

    def spread(p, carry):
        waves = waves_ref[p].astype(F32)
        place = waves[2 * bands : 2 * bands + 8].astype(jnp.int32)
        first, second, third = place[0:1], place[1:2], place[2:3]
        line = lax.broadcasted_iota(jnp.int32, (LANES, count), 0)
        pick = jnp.where(line == second, 1.0, 0.0).astype(BF16)
        turn = jnp.dot(near, pick, preferred_element_type=F32)
        pick = jnp.where(line == third, 1.0, 0.0).astype(BF16)
        phase = jnp.dot(third_ref[...], jnp.concatenate([pick, pick]), preferred_element_type=F32)
        phase_s[p] = phase
        centre = turn[rows : rows + 2] + turn[rows + 2 : rows + 4]
        centre_s[p] = centre
        real, imag = waves[:bands], waves[bands : 2 * bands]
        square_s[...] += real * real + imag * imag
        turned_real = real * centre[0:1] - imag * centre[1:2]
        turned_imag = real * centre[1:2] + imag * centre[0:1]
        inside = lax.broadcasted_iota(jnp.int32, (slab, count), 0) == first
        for k in range(rows):
            select_s[p, k * slab : (k + 1) * slab, :] = jnp.where(
                inside, turn[k : k + 1], 0.0
            ).astype(BF16)
        cosines, sines = phase[:width_third], phase[width_third:]
        for n in range(bands):
            a, b = turned_real[n : n + 1], turned_imag[n : n + 1]
            at = n * width_third
            coef_s[at : at + width_third, :] = (a * cosines - b * sines).astype(BF16)
            coef_s[wide + at : wide + at + width_third, :] = (a * sines + b * cosines).astype(BF16)
        planes = lax.dot_general(select_s[p], coef_s[...], nt, preferred_element_type=F32)
        for k in range(half):
            even = planes[k * slab : (k + 1) * slab]
            odd = planes[(half + k) * slab : (half + k + 1) * slab]
            even_real, even_imag = even[:, :wide], even[:, wide:]
            odd_real, odd_imag = odd[:, :wide], odd[:, wide:]
            real_rows = pl.ds(pl.multiple_of(p * slab, slab), slab)
            imag_rows = pl.ds(pl.multiple_of(width_first + p * slab, slab), slab)
            slab_s[half + k, real_rows, :] = (even_real - odd_imag).astype(BF16)
            slab_s[half + k, imag_rows, :] = (even_imag + odd_real).astype(BF16)
            slab_s[half - 1 - k, real_rows, :] = (even_real + odd_imag).astype(BF16)
            slab_s[half - 1 - k, imag_rows, :] = (even_imag - odd_real).astype(BF16)
        return carry

    lax.fori_loop(0, devices, spread, 0)

    weights = [occupation_ref[n].astype(F32) for n in range(bands)]

    def one_row(row):
        spatial = jnp.dot(back_ref[...], slab_s[row], preferred_element_type=F32)
        local = potential_ref[:, row, :]
        density = jnp.zeros((width_first, width_third), F32)
        moved_real, moved_imag = [], []
        for n in range(bands):
            real = spatial[:width_first, n * width_third : (n + 1) * width_third]
            imag = spatial[width_first:, n * width_third : (n + 1) * width_third]
            power = real * real + imag * imag
            density = density + weights[n] * power
            energy = (power * local).reshape(width_first // 8, 8, width_third)
            energy_s[n] += jnp.sum(energy, axis=0)
            moved_real.append((real * local).astype(BF16))
            moved_imag.append((imag * local).astype(BF16))
        density_s[:, row, :] = density
        moved = jnp.concatenate(
            [jnp.concatenate(moved_real, axis=1), jnp.concatenate(moved_imag, axis=1)]
        )
        return jnp.dot(fore_ref[...], moved, preferred_element_type=F32)

    def pair(k, carry):
        plus = one_row(half + k)
        minus = one_row(half - 1 - k)
        total = (plus + minus).astype(BF16)
        gap = plus - minus
        gap_real = gap[width_first:].astype(BF16)
        gap_imag = (-gap[:width_first]).astype(BF16)
        for p in range(devices):
            even_rows = pl.ds(pl.multiple_of(k * slab, slab), slab)
            odd_rows = pl.ds(pl.multiple_of((half + k) * slab, slab), slab)
            mine = slice(p * slab, (p + 1) * slab)
            acted_s[p, even_rows, :wide] = total[mine]
            acted_s[p, even_rows, wide:] = total[width_first + p * slab : width_first + (p + 1) * slab]
            acted_s[p, odd_rows, :wide] = gap_real[mine]
            acted_s[p, odd_rows, wide:] = gap_imag[mine]
        return carry

    lax.fori_loop(0, half, pair, 0)

    share = width_first // 2
    own_ref[...] = density_s[pl.ds(side * share, share)] + rest_ref[...]
    other_ref[...] = density_s[pl.ds((1 - side) * share, share)].astype(BF16)

    waves = waves_ref[me].astype(F32)
    real, imag = waves[:bands], waves[bands : 2 * bands]
    moving = jnp.sum((real * real + imag * imag) * kinetic_ref[...], axis=1, keepdims=True)
    energy = jnp.concatenate(
        [jnp.sum(energy_s[n], axis=(0, 1), keepdims=True) for n in range(bands)]
    )
    numerator = moving + energy
    denominator = jnp.sum(square_s[...], axis=1, keepdims=True) * (1.0 / devices)
    scalars = []
    for value in (numerator, denominator):
        high = value.astype(BF16)
        low = (value - high.astype(F32)).astype(BF16)
        both = jnp.concatenate([high.astype(F32), low.astype(F32)])
        scalars.append(jnp.broadcast_to(both, (2 * bands, LANES)))
    scalars = jnp.concatenate(scalars, axis=1).astype(BF16)

    def collect(p, carry):
        found = lax.dot_general(acted_s[p], select_s[p], tn, preferred_element_type=F32)
        cosines, sines = phase_s[p, :width_third], phase_s[p, width_third:]
        reals, imags = [], []
        for n in range(bands):
            at = n * width_third
            real = found[at : at + width_third]
            imag = found[wide + at : wide + at + width_third]
            reals.append(jnp.sum(real * cosines + imag * sines, axis=0, keepdims=True))
            imags.append(jnp.sum(imag * cosines - real * sines, axis=0, keepdims=True))
        real, imag = jnp.concatenate(reals), jnp.concatenate(imags)
        centre = centre_s[p]
        cosine, sine = centre[0:1], centre[1:2]
        result = jnp.concatenate([real * cosine + imag * sine, imag * cosine - real * sine])
        sent_ref[p, :, :count] = result.astype(BF16)
        sent_ref[p, :, count:] = scalars
        return carry

    lax.fori_loop(0, devices, collect, 0)


def on_grid(waves, potential, rest_density, kinetic, occupation, bands, width_second):
    devices, _, count = waves.shape
    width_first, rows, width_third = potential.shape
    slab = width_first // devices
    wide = bands * width_third
    tables = wave_tables(devices, rows, width_first, width_second, width_third)
    vmem = pl.BlockSpec(memory_space=pltpu.VMEM)
    smem = pl.BlockSpec(memory_space=pltpu.SMEM)
    return pl.pallas_call(
        functools.partial(grid_kernel, bands),
        out_shape=(
            jax.ShapeDtypeStruct((devices, 2 * bands, count + 2 * LANES), BF16),
            jax.ShapeDtypeStruct(rest_density.shape, F32),
            jax.ShapeDtypeStruct(rest_density.shape, BF16),
        ),
        in_specs=[vmem] * 8 + [smem],
        out_specs=(vmem, vmem, vmem),
        scratch_shapes=[
            pltpu.VMEM((devices, 2 * width_third, count), F32),
            pltpu.VMEM((devices, rows * slab, count), BF16),
            pltpu.VMEM((devices, 2, count), F32),
            pltpu.VMEM((2 * wide, count), BF16),
            pltpu.VMEM((rows, 2 * width_first, wide), BF16),
            pltpu.VMEM((devices, rows * slab, 2 * wide), BF16),
            pltpu.VMEM((width_first, rows, width_third), F32),
            pltpu.VMEM((bands, 8, width_third), F32),
            pltpu.VMEM((bands, count), F32),
        ],
        compiler_params=pltpu.CompilerParams(vmem_limit_bytes=56 * 1024 * 1024),
    )(waves, *[jnp.asarray(t) for t in tables], potential, rest_density, kinetic[None], occupation)


def inner_kernel(bands, mine_ref, theirs_ref, trial_ref, partner_ref, kinetic_ref, all_ref, sent_ref, rest_ref):
    count = kinetic_ref.shape[1]
    first = lax.axis_index("band") == 0
    nt = (((1,), (1,)), ((), ()))

    def order(one, two):
        return jnp.concatenate([jnp.where(first, one, two), jnp.where(first, two, one)])

    kinetic = kinetic_ref[...]
    damping = 1.0 / (1.0 + kinetic)
    mine, theirs = mine_ref[...], theirs_ref[...]
    pairs = order(mine[:bands] + 0.0, theirs[:bands]), order(mine[bands:], theirs[bands:])
    sums = (pairs[0] + pairs[1])[:, count:]
    ratio = sums[:, 0:1] / (sums[:, LANES : LANES + 1] + EPSILON)
    halves, dampeds, softs = [], [], []
    for part in range(2):
        trial = order(trial_ref[part].astype(F32), partner_ref[part].astype(F32))
        action = kinetic * trial + pairs[part][:, :count]
        halves.append(action.astype(BF16))
        dampeds.append((action * damping).astype(BF16))
        softs.append((trial * damping).astype(BF16))
    rows = jnp.concatenate(halves + dampeds + softs)
    one = lax.dot_general(rows, all_ref[0], nt, preferred_element_type=F32)
    two = lax.dot_general(rows, all_ref[1], nt, preferred_element_type=F32)
    block = 2 * bands

    def inner(at):
        real = one[at : at + block] + two[at + block : at + 2 * block]
        imag = one[at + block : at + 2 * block] - two[at : at + block]
        return real, imag

    correlation = inner(0)
    damped = inner(2 * block)
    soft = inner(4 * block)
    coefficients = [d - ratio * s for d, s in zip(damped, soft)]
    sent_ref[...] = jnp.concatenate([*correlation, *coefficients]).astype(BF16)
    own_ratio = jnp.where(first, ratio[:bands], ratio[bands:])
    for part in range(2):
        d, s = dampeds[part].astype(F32), softs[part].astype(F32)
        d = jnp.where(first, d[:bands], d[bands:])
        s = jnp.where(first, s[:bands], s[bands:])
        rest_ref[part * bands : (part + 1) * bands] = d - own_ratio * s


def project_kernel(bands, sums_ref, arrived_ref, all_ref, rest_ref, correlation_ref, own_ref, sent_ref):
    block = 2 * bands
    first = lax.axis_index("band") == 0
    total = sums_ref[...].astype(F32) + arrived_ref[...].astype(F32)
    correlation_ref[...] = total[: 2 * block]
    coefficients = total[2 * block :].astype(BF16)
    one = jnp.dot(coefficients, all_ref[0], preferred_element_type=F32)
    two = jnp.dot(coefficients, all_ref[1], preferred_element_type=F32)
    real = one[:block] - two[block:]
    imag = one[block:] + two[:block]
    for part, value in enumerate((real, imag)):
        low, high = value[:bands], value[bands:]
        rows = slice(part * bands, (part + 1) * bands)
        own_ref[rows] = rest_ref[rows] - jnp.where(first, low, high)
        sent_ref[rows] = jnp.where(first, high, low)


def swap(values, axis, bit):
    size = lax.axis_size(axis)
    return lax.ppermute(values, axis, [(i, i ^ bit) for i in range(size)])


def in_waves(trial_block, all_bands, potential, rest_density, wave_cells, kinetic, occupation):
    devices = lax.axis_size("pw")
    _, rows, width_third = potential.shape
    width_second = rows * devices
    _, bands, count = trial_block.shape
    partner = swap(trial_block, "band", 1)
    first = wave_cells // (width_second * width_third)
    second = wave_cells // width_third % width_second
    third = wave_cells % width_third
    place = jnp.stack([first, second, third]).astype(BF16)
    packet = jnp.concatenate([trial_block.reshape(2 * bands, count), place])
    packet = jnp.pad(packet, ((0, -packet.shape[0] % 16), (0, 0)))
    packets = jnp.broadcast_to(packet[None], (devices, *packet.shape))
    waves = lax.all_to_all(packets, "pw", split_axis=0, concat_axis=0, tiled=True)
    partial, density_own, density_other = on_grid(
        waves, potential, rest_density, kinetic, occupation, bands, width_second
    )
    arrived = lax.all_to_all(partial, "pw", split_axis=0, concat_axis=0, tiled=True)
    mine = jnp.sum(arrived.astype(F32), axis=0)
    theirs = swap(mine, "band", 1)
    density = density_own + swap(density_other, "band", 1).astype(F32)
    vmem = pl.BlockSpec(memory_space=pltpu.VMEM)
    states = all_bands.shape[1]
    block = 2 * bands
    params = pltpu.CompilerParams(vmem_limit_bytes=32 * 1024 * 1024)
    sums, rest = pl.pallas_call(
        functools.partial(inner_kernel, bands),
        out_shape=(
            jax.ShapeDtypeStruct((4 * block, states), BF16),
            jax.ShapeDtypeStruct((block, count), F32),
        ),
        in_specs=[vmem] * 6,
        out_specs=(vmem, vmem),
        compiler_params=params,
    )(mine, theirs, trial_block, partner, kinetic[None], all_bands)
    bit = 1
    while 2 * bit < devices:
        sums = sums + swap(sums, "pw", bit)
        bit *= 2
    correlation, own, sent = pl.pallas_call(
        functools.partial(project_kernel, bands),
        out_shape=(
            jax.ShapeDtypeStruct((2 * block, states), F32),
            jax.ShapeDtypeStruct((block, count), F32),
            jax.ShapeDtypeStruct((block, count), F32),
        ),
        in_specs=[vmem] * 4,
        out_specs=(vmem, vmem, vmem),
        compiler_params=params,
    )(sums, swap(sums, "pw", bit), all_bands, rest)
    correction = (own - swap(sent, "band", 1)).reshape(2, bands, count)
    correlation = correlation.reshape(2, block, states).transpose(0, 2, 1)
    return (correction, correlation, density)


def fits(trial_block, potential, mesh):
    devices = mesh.shape["pw"]
    width_first, width_second, width_third = potential.shape[0] // mesh.shape["ens"], *potential.shape[1:]
    slab, rows = width_first // devices, width_second // devices
    bands = trial_block.shape[1] // mesh.shape["band"]
    return (
        mesh.shape["band"] == 2
        and devices >= 2
        and devices & (devices - 1) == 0
        and slab % 16 == 0
        and rows % 16 == 0
        and width_first % LANES == 0
        and width_second == LANES
        and width_third == LANES
        and bands == 4
        and trial_block.shape[2] // devices % LANES == 0
    )


def tables(length):
    positions = jnp.arange(length, dtype=jnp.int32)
    products = positions[:, None] * positions[None, :] % length
    angles = products.astype(jnp.float32) * (2.0 * math.pi / length)
    factor = 1.0 / math.sqrt(length)
    cosines = jnp.cos(angles) * factor
    sines = jnp.sin(angles) * factor
    backward = jnp.stack([jnp.stack([cosines, -sines]), jnp.stack([sines, cosines])])
    forward = jnp.stack([jnp.stack([cosines, sines]), jnp.stack([-sines, cosines])])
    return (backward, forward)


def transform(fields, table, formula):
    return jnp.einsum(formula, table, fields, precision=HIGHEST)


def inner(left, right):
    contract = (((1,), (1,)), ((), ()))
    first = lax.dot_general(left[0], right[0], contract, preferred_element_type=jnp.float32)
    second = lax.dot_general(left[1], right[1], contract, preferred_element_type=jnp.float32)
    cross_one = lax.dot_general(left[0], right[1], contract, preferred_element_type=jnp.float32)
    cross_two = lax.dot_general(left[1], right[0], contract, preferred_element_type=jnp.float32)
    return jnp.stack([first + second, cross_one - cross_two])


def on_device(trial_block, all_bands, potential, rest_density, wave_cells, kinetic, occupation):
    devices = lax.axis_size("pw")
    width_first, rows_second, width_third = potential.shape
    width_second = rows_second * devices
    slab_rows = width_first // devices
    blocks = trial_block.shape[1]
    back_first, fore_first = tables(width_first)
    back_second, fore_second = tables(width_second)
    back_third, fore_third = tables(width_third)
    along_third = "pqkc,qnabc->pnabk"
    along_second = "pqkb,qnabc->pnakc"
    along_first = "pqka,qnabc->pnkbc"
    trial_float = trial_block.astype(jnp.float32)
    filled = jnp.zeros((2, blocks, slab_rows * width_second * width_third), jnp.float32)
    filled = filled.at[:, :, wave_cells].set(trial_float)
    filled = filled.reshape(2, blocks, slab_rows, width_second, width_third)
    filled = transform(filled, back_third, along_third)
    filled = transform(filled, back_second, along_second)
    spatial = transform(
        lax.all_to_all(filled, "pw", split_axis=3, concat_axis=2, tiled=True),
        back_first,
        along_first,
    )
    power = spatial[0] * spatial[0] + spatial[1] * spatial[1]
    acted = transform(spatial * potential, fore_first, along_first)
    returned = lax.all_to_all(acted, "pw", split_axis=2, concat_axis=3, tiled=True)
    columns, power = (returned, power[None])
    columns = transform(columns, fore_second, along_second)
    columns = transform(columns, fore_third, along_third)
    applied = columns.reshape(2, blocks, slab_rows * width_second * width_third)[:, :, wave_cells]
    weights = occupation.astype(jnp.float32)
    density_part = jnp.einsum("n,nabc->abc", weights, power[0], precision=HIGHEST)
    summed_density = lax.psum(density_part.astype(jnp.bfloat16), "band").astype(jnp.float32)
    share = width_first // lax.axis_size("band")
    block_density = lax.dynamic_slice_in_dim(
        summed_density, lax.axis_index("band") * share, share, 0
    )
    density = rest_density + block_density
    action = kinetic * trial_float + applied
    damping = 1.0 / (1.0 + kinetic)
    action_half = action.astype(jnp.bfloat16)
    damped = (action * damping).astype(jnp.bfloat16)
    softened = (trial_float * damping).astype(jnp.bfloat16)
    every_trial, every_action, every_damped, every_softened = (
        lax.all_gather(trial_block, "band", axis=1, tiled=True),
        lax.all_gather(action_half, "band", axis=1, tiled=True),
        lax.all_gather(damped, "band", axis=1, tiled=True),
        lax.all_gather(softened, "band", axis=1, tiled=True),
    )
    trial_wide = every_trial.astype(jnp.float32)
    numerator = jnp.sum(trial_wide * every_action.astype(jnp.float32), axis=(0, 2))
    denominator = jnp.sum(trial_wide * trial_wide, axis=(0, 2))
    correlation = inner(all_bands, every_action)
    correlation, numerator, denominator = lax.psum((correlation, numerator, denominator), "pw")
    rayleigh = numerator / (denominator + EPSILON)
    local_terms = inner(all_bands, every_damped) - rayleigh * inner(all_bands, every_softened)
    coefficients = lax.psum(local_terms, "pw")
    coefficient_half = coefficients.astype(jnp.bfloat16)
    real_piece = coefficient_half[0]
    imag_piece = coefficient_half[1]
    contract = (((0,), (0,)), ((), ()))
    real_real = lax.dot_general(
        real_piece, all_bands[0], contract, preferred_element_type=jnp.float32
    )
    imag_imag = lax.dot_general(
        imag_piece, all_bands[1], contract, preferred_element_type=jnp.float32
    )
    imag_real = lax.dot_general(
        imag_piece, all_bands[0], contract, preferred_element_type=jnp.float32
    )
    real_imag = lax.dot_general(
        real_piece, all_bands[1], contract, preferred_element_type=jnp.float32
    )
    projected = lax.psum_scatter(
        jnp.concatenate(
            [(real_real - imag_imag)[:, None], (imag_real + real_imag)[:, None]], axis=1
        ),
        "band",
        scatter_dimension=0,
        tiled=True,
    )
    own_ratio = lax.dynamic_slice_in_dim(rayleigh, lax.axis_index("band") * blocks, blocks, 0)
    real_correction = (
        damped[0].astype(jnp.float32)
        - own_ratio[:, None] * softened[0].astype(jnp.float32)
        - projected[:, 0]
    )
    imag_correction = (
        damped[1].astype(jnp.float32)
        - own_ratio[:, None] * softened[1].astype(jnp.float32)
        - projected[:, 1]
    )
    correction = jnp.stack([real_correction, imag_correction])
    return (correction, correlation, density)


def solution(mesh):
    placed = (
        P("ens", "band", "pw"),
        P("ens", "band", "pw"),
        P("ens", "pw", None),
        P(("ens", "band"), "pw", None),
        P("pw"),
        P("pw"),
        P(("ens", "band")),
    )
    results = (P("ens", "band", "pw"), P("ens", "band", None), P(("ens", "band"), "pw", None))

    def program(*arguments):
        body = in_waves if fits(arguments[0], arguments[2], mesh) else on_device
        return jax.shard_map(
            body, mesh=mesh, in_specs=placed, out_specs=results, check_vma=False
        )(*arguments)

    return program
```

```python
import functools
import math

import jax
import jax.numpy as jnp
import numpy as np
from jax import lax
from jax.experimental import pallas as pl
from jax.experimental.pallas import tpu as pltpu
from jax.sharding import PartitionSpec as P

EPSILON = 1e-06
HIGHEST = lax.Precision.HIGHEST
BF16 = jnp.bfloat16
F32 = jnp.float32
LANES = 128


def split_pair(values):
    high = values.astype(BF16)
    low = (values - high.astype(np.float64)).astype(BF16)
    return high, low


def wave_tables(devices, rows, width_first, width_second, width_third):
    half = rows // 2
    second = np.arange(width_second)
    steps = np.outer(2 * np.arange(half) + 1, second) % (2 * width_second)
    angles = steps * (math.pi / width_second)
    near = np.concatenate([np.cos(angles), np.sin(angles)])
    blocks = []
    for device in range(devices):
        middle = 2 * rows * device + rows - 1
        turns = (middle * second % (2 * width_second)) * (math.pi / width_second)
        centre = np.stack([np.cos(turns), np.sin(turns)])
        high, low = split_pair(centre)
        blocks.append(np.concatenate([near.astype(BF16), high, low]))
    second_table = np.stack(blocks)
    missing = -second_table.shape[1] % 16
    second_table = np.pad(second_table, ((0, 0), (0, missing), (0, 0)))
    third = np.arange(width_third)
    angles = (np.outer(third, third) % width_third) * (2 * math.pi / width_third)
    factor = 1.0 / math.sqrt(width_second * width_third)
    values = np.concatenate([np.cos(angles), np.sin(angles)]) * factor
    third_table = np.concatenate(split_pair(values), axis=1)
    first = np.arange(width_first)
    angles = (np.outer(first, first) % width_first) * (2 * math.pi / width_first)
    cosines = np.cos(angles) / math.sqrt(width_first)
    sines = np.sin(angles) / math.sqrt(width_first)
    back = np.block([[cosines, -sines], [sines, cosines]]).astype(BF16)
    fore = np.block([[cosines, sines], [-sines, cosines]]).astype(BF16)
    return second_table, third_table, back, fore


def pack_kernel(bands, devices, width_second, width_third, trial_ref, cells_ref, packet_ref):
    cells = cells_ref[...].reshape(1, cells_ref.shape[0])
    first = lax.div(cells, width_second * width_third)
    second = lax.rem(lax.div(cells, width_third), width_second)
    third = lax.rem(cells, width_third)
    unused = jnp.zeros((packet_ref.shape[1] - 2 * bands - 3, cells.shape[1]), jnp.int32)
    place = jnp.concatenate([first, second, third, unused]).astype(F32)
    trial = [trial_ref[part].astype(F32) for part in range(2)]
    packet = jnp.concatenate([*trial, place]).astype(BF16)
    for p in range(devices):
        packet_ref[p] = packet


def grid_kernel(
    bands,
    waves_ref,
    second_ref,
    third_ref,
    back_ref,
    fore_ref,
    potential_ref,
    kinetic_ref,
    occupation_ref,
    partner_ref,
    sent_ref,
    own_ref,
    other_ref,
    phase_s,
    select_s,
    slab_s,
    acted_s,
):
    devices, _, count = waves_ref.shape
    rows, width_first, width_third = potential_ref.shape
    slab = width_first // devices
    half = rows // 2
    share = width_first // 2
    me = lax.axis_index("pw")
    low_side = lax.axis_index("band") == 0
    nt = (((1,), (1,)), ((), ()))
    tn = (((0,), (0,)), ((), ()))
    near = second_ref[me]
    weights = [occupation_ref[n].astype(F32) for n in range(bands)]
    lanes = [slice(n * width_third, (n + 1) * width_third) for n in range(bands)]
    square = jnp.zeros((bands, count), F32)
    energies = [jnp.zeros((8, width_third), F32) for _ in range(bands)]
    centres = []

    for p in range(devices):
        waves = waves_ref[p].astype(F32)
        place = waves[2 * bands : 2 * bands + 8].astype(jnp.int32)
        first, second, third = place[0:1], place[1:2], place[2:3]
        line = lax.broadcasted_iota(jnp.int32, (LANES, count), 0)
        pick = jnp.where(line == second, 1.0, 0.0).astype(BF16)
        turn = jnp.dot(near, pick, preferred_element_type=F32)
        pick = jnp.where(line == third, 1.0, 0.0).astype(BF16)
        phase = jnp.dot(third_ref[...], jnp.concatenate([pick, pick]), preferred_element_type=F32)
        phase_s[p] = phase
        centre = turn[rows : rows + 2] + turn[rows + 2 : rows + 4]
        centres.append(centre)
        real, imag = waves[:bands], waves[bands : 2 * bands]
        square = square + real * real + imag * imag
        turned_real = real * centre[0:1] - imag * centre[1:2]
        turned_imag = real * centre[1:2] + imag * centre[0:1]
        inside = lax.broadcasted_iota(jnp.int32, (slab, count), 0) == first
        for k in range(rows):
            select_s[p, k * slab : (k + 1) * slab, :] = jnp.where(
                inside, turn[k : k + 1], 0.0
            ).astype(BF16)
        cosines, sines = phase[:width_third], phase[width_third:]
        for n in range(bands):
            a, b = turned_real[n : n + 1], turned_imag[n : n + 1]
            turned = jnp.concatenate([a * cosines - b * sines, a * sines + b * cosines]).astype(BF16)
            planes = lax.dot_general(select_s[p], turned, nt, preferred_element_type=F32)
            even, odd = planes[: half * slab], planes[half * slab :]
            even_real, even_imag = even[:, :width_third], even[:, width_third:]
            odd_real, odd_imag = odd[:, :width_third], odd[:, width_third:]
            plus_real = (even_real - odd_imag).astype(BF16)
            plus_imag = (even_imag + odd_real).astype(BF16)
            minus_real = (even_real + odd_imag).astype(BF16)
            minus_imag = (even_imag - odd_real).astype(BF16)
            real_rows = slice(p * slab, (p + 1) * slab)
            imag_rows = slice(width_first + p * slab, width_first + (p + 1) * slab)
            for k in range(half):
                part = slice(k * slab, (k + 1) * slab)
                slab_s[half + k, real_rows, lanes[n]] = plus_real[part]
                slab_s[half + k, imag_rows, lanes[n]] = plus_imag[part]
                slab_s[half - 1 - k, real_rows, lanes[n]] = minus_real[part]
                slab_s[half - 1 - k, imag_rows, lanes[n]] = minus_imag[part]

    group = 2
    for k in range(half):
        densities = [0.0, 0.0]
        for start in range(0, bands, group):
            members = range(start, start + group)
            at = slice(start * width_third, (start + group) * width_third)
            results = []
            for sign, row in enumerate((half + k, half - 1 - k)):
                spatial = jnp.dot(back_ref[...], slab_s[row, :, at], preferred_element_type=F32)
                local = potential_ref[row]
                moved_real, moved_imag = [], []
                for i, n in enumerate(members):
                    real = spatial[:width_first, lanes[i]]
                    imag = spatial[width_first:, lanes[i]]
                    power = real * real + imag * imag
                    densities[sign] = densities[sign] + weights[n] * power
                    energy = (power * local).reshape(width_first // 8, 8, width_third)
                    energies[n] = energies[n] + jnp.sum(energy, axis=0)
                    moved_real.append((real * local).astype(BF16))
                    moved_imag.append((imag * local).astype(BF16))
                moved = jnp.concatenate(
                    [jnp.concatenate(moved_real, axis=1), jnp.concatenate(moved_imag, axis=1)]
                )
                results.append(jnp.dot(fore_ref[...], moved, preferred_element_type=F32))
            plus, minus = results
            total = (plus + minus).astype(BF16)
            gap = plus - minus
            gap_real = gap[width_first:].astype(BF16)
            gap_imag = (-gap[:width_first]).astype(BF16)
            for p in range(devices):
                mine = slice(p * slab, (p + 1) * slab)
                mine_imag = slice(width_first + p * slab, width_first + (p + 1) * slab)
                even_rows = slice(k * slab, (k + 1) * slab)
                odd_rows = slice((half + k) * slab, (half + k + 1) * slab)
                for i, n in enumerate(members):
                    to_real = slice(2 * n * width_third, (2 * n + 1) * width_third)
                    to_imag = slice((2 * n + 1) * width_third, (2 * n + 2) * width_third)
                    acted_s[p, even_rows, to_real] = total[mine, lanes[i]]
                    acted_s[p, even_rows, to_imag] = total[mine_imag, lanes[i]]
                    acted_s[p, odd_rows, to_real] = gap_real[mine, lanes[i]]
                    acted_s[p, odd_rows, to_imag] = gap_imag[mine, lanes[i]]
        for sign, row in enumerate((half + k, half - 1 - k)):
            low, high = densities[sign][:share], densities[sign][share:]
            own_ref[row] = jnp.where(low_side, low, high)
            other_ref[row] = jnp.where(low_side, high, low).astype(BF16)

    waves = waves_ref[me].astype(F32)
    real, imag = waves[:bands], waves[bands : 2 * bands]
    kinetic = kinetic_ref[...].reshape(1, count)
    moving = jnp.sum((real * real + imag * imag) * kinetic, axis=1, keepdims=True)
    energy = jnp.concatenate([jnp.sum(e, axis=(0, 1), keepdims=True) for e in energies])
    numerator = moving + energy
    denominator = jnp.sum(square, axis=1, keepdims=True) * (1.0 / devices)
    scalars = []
    for value in (numerator, denominator):
        high = value.astype(BF16)
        low = (value - high.astype(F32)).astype(BF16)
        both = jnp.concatenate([high.astype(F32), low.astype(F32)])
        scalars.append(jnp.broadcast_to(both, (2 * bands, LANES)))
    scalars = jnp.concatenate(scalars, axis=1).astype(BF16)

    for p in range(devices):
        cosines, sines = phase_s[p, :width_third], phase_s[p, width_third:]
        reals, imags = [], []
        for n in range(bands):
            at = slice(2 * n * width_third, 2 * (n + 1) * width_third)
            found = lax.dot_general(acted_s[p, :, at], select_s[p], tn, preferred_element_type=F32)
            real, imag = found[:width_third], found[width_third:]
            reals.append(
                jnp.sum(real * cosines, axis=0, keepdims=True)
                + jnp.sum(imag * sines, axis=0, keepdims=True)
            )
            imags.append(
                jnp.sum(imag * cosines, axis=0, keepdims=True)
                - jnp.sum(real * sines, axis=0, keepdims=True)
            )
        real, imag = jnp.concatenate(reals), jnp.concatenate(imags)
        cosine, sine = centres[p][0:1], centres[p][1:2]
        result = jnp.concatenate([real * cosine + imag * sine, imag * cosine - real * sine])
        sent_ref[p, :, :count] = result.astype(BF16)
        sent_ref[p, :, count:] = scalars


def on_grid(waves, potential, kinetic, occupation, partner, bands, width_second):
    devices, _, count = waves.shape
    rows, width_first, width_third = potential.shape
    slab = width_first // devices
    tables = wave_tables(devices, rows, width_first, width_second, width_third)
    vmem = pl.BlockSpec(memory_space=pltpu.VMEM)
    smem = pl.BlockSpec(memory_space=pltpu.SMEM)
    planes = (rows, width_first // 2, width_third)
    return pl.pallas_call(
        functools.partial(grid_kernel, bands),
        out_shape=(
            jax.ShapeDtypeStruct((devices, 2 * bands, count + 2 * LANES), BF16),
            jax.ShapeDtypeStruct(planes, F32),
            jax.ShapeDtypeStruct(planes, BF16),
        ),
        in_specs=[vmem] * 7 + [smem, pl.BlockSpec(memory_space=pl.ANY)],
        out_specs=(vmem, vmem, vmem),
        scratch_shapes=[
            pltpu.VMEM((devices, 2 * width_third, count), F32),
            pltpu.VMEM((devices, rows * slab, count), BF16),
            pltpu.VMEM((rows, 2 * width_first, bands * width_third), BF16),
            pltpu.VMEM((devices, rows * slab, 2 * bands * width_third), BF16),
        ],
        compiler_params=pltpu.CompilerParams(vmem_limit_bytes=40 * 1024 * 1024),
    )(waves, *[jnp.asarray(t) for t in tables], potential, kinetic, occupation, partner)


def inner_kernel(bands, mine_ref, theirs_ref, trial_ref, partner_ref, kinetic_ref, all_ref, density_ref, sent_ref, rest_ref):
    count = kinetic_ref.shape[0]
    first = lax.axis_index("band") == 0
    nt = (((1,), (1,)), ((), ()))

    def order(one, two):
        return jnp.concatenate([jnp.where(first, one, two), jnp.where(first, two, one)])

    kinetic = kinetic_ref[...].reshape(1, count)
    damping = 1.0 / (1.0 + kinetic)
    mine, theirs = mine_ref[...], theirs_ref[...]
    pairs = order(mine[:bands], theirs[:bands]), order(mine[bands:], theirs[bands:])
    sums = (pairs[0] + pairs[1])[:, count:]
    ratio = sums[:, 0:1] / (sums[:, LANES : LANES + 1] + EPSILON)
    halves, dampeds, softs = [], [], []
    for part in range(2):
        trial = order(trial_ref[part].astype(F32), partner_ref[part].astype(F32))
        action = kinetic * trial + pairs[part][:, :count]
        halves.append(action.astype(BF16))
        dampeds.append((action * damping).astype(BF16))
        softs.append((trial * damping).astype(BF16))
    rows = jnp.concatenate(halves + dampeds + softs)
    one = lax.dot_general(rows, all_ref[0], nt, preferred_element_type=F32)
    two = lax.dot_general(rows, all_ref[1], nt, preferred_element_type=F32)
    block = 2 * bands

    def inner(at):
        real = one[at : at + block] + two[at + block : at + 2 * block]
        imag = one[at + block : at + 2 * block] - two[at : at + block]
        return real, imag

    correlation = inner(0)
    damped = inner(2 * block)
    soft = inner(4 * block)
    coefficients = [d - ratio * s for d, s in zip(damped, soft)]
    sent_ref[...] = jnp.concatenate([*correlation, *coefficients]).astype(BF16)
    own_ratio = jnp.where(first, ratio[:bands], ratio[bands:])
    for part in range(2):
        d, s = dampeds[part].astype(F32), softs[part].astype(F32)
        d = jnp.where(first, d[:bands], d[bands:])
        s = jnp.where(first, s[:bands], s[bands:])
        rest_ref[part * bands : (part + 1) * bands] = d - own_ratio * s


def project_kernel(bands, sums_ref, arrived_ref, all_ref, rest_ref, correlation_ref, own_ref, sent_ref):
    block = 2 * bands
    first = lax.axis_index("band") == 0
    total = sums_ref[...].astype(F32) + arrived_ref[...].astype(F32)
    correlation_ref[...] = total[: 2 * block]
    coefficients = total[2 * block :].astype(BF16)
    one = jnp.dot(coefficients, all_ref[0], preferred_element_type=F32)
    two = jnp.dot(coefficients, all_ref[1], preferred_element_type=F32)
    real = one[:block] - two[block:]
    imag = one[block:] + two[:block]
    for part, value in enumerate((real, imag)):
        low, high = value[:bands], value[bands:]
        rest = rest_ref[part * bands : (part + 1) * bands]
        own_ref[part] = rest - jnp.where(first, low, high)
        sent_ref[part] = jnp.where(first, high, low)


def swap(values, axis, bit):
    size = lax.axis_size(axis)
    return lax.ppermute(values, axis, [(i, i ^ bit) for i in range(size)])


def in_waves(trial_block, all_bands, potential, rest_density, wave_cells, kinetic, occupation):
    devices = lax.axis_size("pw")
    _, rows, width_third = potential.shape
    width_second = rows * devices
    _, bands, count = trial_block.shape
    states = all_bands.shape[1]
    block = 2 * bands
    vmem = pl.BlockSpec(memory_space=pltpu.VMEM)
    params = pltpu.CompilerParams(vmem_limit_bytes=16 * 1024 * 1024)
    partner = swap(trial_block, "band", 1)
    packets = pl.pallas_call(
        functools.partial(pack_kernel, bands, devices, width_second, width_third),
        out_shape=jax.ShapeDtypeStruct((devices, 16, count), BF16),
        in_specs=[vmem] * 2,
        out_specs=vmem,
        compiler_params=params,
    )(trial_block, wave_cells)
    waves = lax.all_to_all(packets, "pw", split_axis=0, concat_axis=0, tiled=True)
    partial, density_own, density_other = on_grid(
        waves, potential.transpose(1, 0, 2), kinetic, occupation, partner, bands, width_second
    )
    arrived = lax.all_to_all(partial, "pw", split_axis=0, concat_axis=0, tiled=True)
    block_density = density_own + swap(density_other, "band", 1).astype(F32)
    density = rest_density + block_density.transpose(1, 0, 2)
    mine = jnp.sum(arrived.astype(F32), axis=0)
    theirs = swap(mine, "band", 1)
    sums, rest = pl.pallas_call(
        functools.partial(inner_kernel, bands),
        out_shape=(
            jax.ShapeDtypeStruct((4 * block, states), BF16),
            jax.ShapeDtypeStruct((block, count), F32),
        ),
        in_specs=[vmem] * 6 + [pl.BlockSpec(memory_space=pl.ANY)],
        out_specs=(vmem, vmem),
        compiler_params=params,
    )(mine, theirs, trial_block, partner, kinetic, all_bands, density)
    bit = 1
    while 2 * bit < devices:
        sums = sums + swap(sums, "pw", bit)
        bit *= 2
    correlation, own, sent = pl.pallas_call(
        functools.partial(project_kernel, bands),
        out_shape=(
            jax.ShapeDtypeStruct((2 * block, states), F32),
            jax.ShapeDtypeStruct((2, bands, count), F32),
            jax.ShapeDtypeStruct((2, bands, count), F32),
        ),
        in_specs=[vmem] * 4,
        out_specs=(vmem, vmem, vmem),
        compiler_params=params,
    )(sums, swap(sums, "pw", bit), all_bands, rest)
    correction = own - swap(sent, "band", 1)
    correlation = correlation.reshape(2, block, states).transpose(0, 2, 1)
    return (correction, correlation, density)


def fits(trial_block, potential, mesh):
    devices = mesh.shape["pw"]
    width_first, width_second, width_third = potential.shape[0] // mesh.shape["ens"], *potential.shape[1:]
    slab, rows = width_first // devices, width_second // devices
    bands = trial_block.shape[1] // mesh.shape["band"]
    return (
        mesh.shape["band"] == 2
        and devices >= 2
        and devices & (devices - 1) == 0
        and slab % 16 == 0
        and rows % 16 == 0
        and width_first % LANES == 0
        and width_second == LANES
        and width_third == LANES
        and bands == 4
        and trial_block.shape[2] // devices % LANES == 0
    )


def tables(length):
    positions = jnp.arange(length, dtype=jnp.int32)
    products = positions[:, None] * positions[None, :] % length
    angles = products.astype(jnp.float32) * (2.0 * math.pi / length)
    factor = 1.0 / math.sqrt(length)
    cosines = jnp.cos(angles) * factor
    sines = jnp.sin(angles) * factor
    backward = jnp.stack([jnp.stack([cosines, -sines]), jnp.stack([sines, cosines])])
    forward = jnp.stack([jnp.stack([cosines, sines]), jnp.stack([-sines, cosines])])
    return (backward, forward)


def transform(fields, table, formula):
    return jnp.einsum(formula, table, fields, precision=HIGHEST)


def inner(left, right):
    contract = (((1,), (1,)), ((), ()))
    first = lax.dot_general(left[0], right[0], contract, preferred_element_type=jnp.float32)
    second = lax.dot_general(left[1], right[1], contract, preferred_element_type=jnp.float32)
    cross_one = lax.dot_general(left[0], right[1], contract, preferred_element_type=jnp.float32)
    cross_two = lax.dot_general(left[1], right[0], contract, preferred_element_type=jnp.float32)
    return jnp.stack([first + second, cross_one - cross_two])


def on_device(trial_block, all_bands, potential, rest_density, wave_cells, kinetic, occupation):
    devices = lax.axis_size("pw")
    width_first, rows_second, width_third = potential.shape
    width_second = rows_second * devices
    slab_rows = width_first // devices
    blocks = trial_block.shape[1]
    back_first, fore_first = tables(width_first)
    back_second, fore_second = tables(width_second)
    back_third, fore_third = tables(width_third)
    along_third = "pqkc,qnabc->pnabk"
    along_second = "pqkb,qnabc->pnakc"
    along_first = "pqka,qnabc->pnkbc"
    trial_float = trial_block.astype(jnp.float32)
    filled = jnp.zeros((2, blocks, slab_rows * width_second * width_third), jnp.float32)
    filled = filled.at[:, :, wave_cells].set(trial_float)
    filled = filled.reshape(2, blocks, slab_rows, width_second, width_third)
    filled = transform(filled, back_third, along_third)
    filled = transform(filled, back_second, along_second)
    spatial = transform(
        lax.all_to_all(filled, "pw", split_axis=3, concat_axis=2, tiled=True),
        back_first,
        along_first,
    )
    power = spatial[0] * spatial[0] + spatial[1] * spatial[1]
    acted = transform(spatial * potential, fore_first, along_first)
    returned = lax.all_to_all(acted, "pw", split_axis=2, concat_axis=3, tiled=True)
    columns, power = (returned, power[None])
    columns = transform(columns, fore_second, along_second)
    columns = transform(columns, fore_third, along_third)
    applied = columns.reshape(2, blocks, slab_rows * width_second * width_third)[:, :, wave_cells]
    weights = occupation.astype(jnp.float32)
    density_part = jnp.einsum("n,nabc->abc", weights, power[0], precision=HIGHEST)
    summed_density = lax.psum(density_part.astype(jnp.bfloat16), "band").astype(jnp.float32)
    share = width_first // lax.axis_size("band")
    block_density = lax.dynamic_slice_in_dim(
        summed_density, lax.axis_index("band") * share, share, 0
    )
    density = rest_density + block_density
    action = kinetic * trial_float + applied
    damping = 1.0 / (1.0 + kinetic)
    action_half = action.astype(jnp.bfloat16)
    damped = (action * damping).astype(jnp.bfloat16)
    softened = (trial_float * damping).astype(jnp.bfloat16)
    every_trial, every_action, every_damped, every_softened = (
        lax.all_gather(trial_block, "band", axis=1, tiled=True),
        lax.all_gather(action_half, "band", axis=1, tiled=True),
        lax.all_gather(damped, "band", axis=1, tiled=True),
        lax.all_gather(softened, "band", axis=1, tiled=True),
    )
    trial_wide = every_trial.astype(jnp.float32)
    numerator = jnp.sum(trial_wide * every_action.astype(jnp.float32), axis=(0, 2))
    denominator = jnp.sum(trial_wide * trial_wide, axis=(0, 2))
    correlation = inner(all_bands, every_action)
    correlation, numerator, denominator = lax.psum((correlation, numerator, denominator), "pw")
    rayleigh = numerator / (denominator + EPSILON)
    local_terms = inner(all_bands, every_damped) - rayleigh * inner(all_bands, every_softened)
    coefficients = lax.psum(local_terms, "pw")
    coefficient_half = coefficients.astype(jnp.bfloat16)
    real_piece = coefficient_half[0]
    imag_piece = coefficient_half[1]
    contract = (((0,), (0,)), ((), ()))
    real_real = lax.dot_general(
        real_piece, all_bands[0], contract, preferred_element_type=jnp.float32
    )
    imag_imag = lax.dot_general(
        imag_piece, all_bands[1], contract, preferred_element_type=jnp.float32
    )
    imag_real = lax.dot_general(
        imag_piece, all_bands[0], contract, preferred_element_type=jnp.float32
    )
    real_imag = lax.dot_general(
        real_piece, all_bands[1], contract, preferred_element_type=jnp.float32
    )
    projected = lax.psum_scatter(
        jnp.concatenate(
            [(real_real - imag_imag)[:, None], (imag_real + real_imag)[:, None]], axis=1
        ),
        "band",
        scatter_dimension=0,
        tiled=True,
    )
    own_ratio = lax.dynamic_slice_in_dim(rayleigh, lax.axis_index("band") * blocks, blocks, 0)
    real_correction = (
        damped[0].astype(jnp.float32)
        - own_ratio[:, None] * softened[0].astype(jnp.float32)
        - projected[:, 0]
    )
    imag_correction = (
        damped[1].astype(jnp.float32)
        - own_ratio[:, None] * softened[1].astype(jnp.float32)
        - projected[:, 1]
    )
    correction = jnp.stack([real_correction, imag_correction])
    return (correction, correlation, density)


def solution(mesh):
    placed = (
        P("ens", "band", "pw"),
        P("ens", "band", "pw"),
        P("ens", "pw", None),
        P(("ens", "band"), "pw", None),
        P("pw"),
        P("pw"),
        P(("ens", "band")),
    )
    results = (P("ens", "band", "pw"), P("ens", "band", None), P(("ens", "band"), "pw", None))

    def program(*arguments):
        body = in_waves if fits(arguments[0], arguments[2], mesh) else on_device
        return jax.shard_map(
            body, mesh=mesh, in_specs=placed, out_specs=results, check_vma=False
        )(*arguments)

    return program
```

```python
import functools
import math

import jax
import jax.numpy as jnp
import numpy as np
from jax import lax
from jax.experimental import pallas as pl
from jax.experimental.pallas import tpu as pltpu
from jax.sharding import PartitionSpec as P

EPSILON = 1e-06
HIGHEST = lax.Precision.HIGHEST
BF16 = jnp.bfloat16
F32 = jnp.float32
LANES = 128


def split_pair(values):
    high = values.astype(BF16)
    low = (values - high.astype(np.float64)).astype(BF16)
    return high, low


def wave_tables(devices, rows, width_first, width_second, width_third):
    half = rows // 2
    second = np.arange(width_second)
    steps = np.outer(2 * np.arange(half) + 1, second) % (2 * width_second)
    angles = steps * (math.pi / width_second)
    near = np.concatenate([np.cos(angles), np.sin(angles)])
    blocks = []
    for device in range(devices):
        middle = 2 * rows * device + rows - 1
        turns = (middle * second % (2 * width_second)) * (math.pi / width_second)
        centre = np.stack([np.cos(turns), np.sin(turns)])
        high, low = split_pair(centre)
        blocks.append(np.concatenate([near.astype(BF16), high, low]))
    second_table = np.stack(blocks)
    missing = -second_table.shape[1] % 16
    second_table = np.pad(second_table, ((0, 0), (0, missing), (0, 0)))
    third = np.arange(width_third)
    angles = (np.outer(third, third) % width_third) * (2 * math.pi / width_third)
    factor = 1.0 / math.sqrt(width_second * width_third)
    values = np.concatenate([np.cos(angles), np.sin(angles)]) * factor
    third_table = np.concatenate(split_pair(values), axis=1)
    first = np.arange(width_first)
    angles = (np.outer(first, first) % width_first) * (2 * math.pi / width_first)
    cosines = np.cos(angles) / math.sqrt(width_first)
    sines = np.sin(angles) / math.sqrt(width_first)
    back = np.block([[cosines, -sines], [sines, cosines]]).astype(BF16)
    fore = np.block([[cosines, sines], [-sines, cosines]]).astype(BF16)
    return second_table, third_table, back, fore


def pack_kernel(bands, devices, width_second, width_third, trial_ref, cells_ref, packet_ref):
    cells = cells_ref[...].reshape(1, cells_ref.shape[0])
    first = lax.div(cells, width_second * width_third)
    second = lax.rem(lax.div(cells, width_third), width_second)
    third = lax.rem(cells, width_third)
    unused = jnp.zeros((packet_ref.shape[1] - 2 * bands - 3, cells.shape[1]), jnp.int32)
    place = jnp.concatenate([first, second, third, unused]).astype(F32)
    trial = [trial_ref[part].astype(F32) for part in range(2)]
    packet = jnp.concatenate([*trial, place]).astype(BF16)
    for p in range(devices):
        packet_ref[p] = packet


def grid_kernel(
    bands,
    waves_ref,
    second_ref,
    third_ref,
    back_ref,
    fore_ref,
    potential_in,
    kinetic_ref,
    occupation_ref,
    sent_ref,
    own_out,
    other_out,
    phase_s,
    select_s,
    slab_s,
    acted_s,
    potential_ref,
    own_ref,
    other_ref,
    done,
):
    devices, _, count = waves_ref.shape
    fetch = pltpu.make_async_copy(potential_in, potential_ref, done.at[2])
    fetch.start()
    rows, width_first, width_third = potential_ref.shape
    slab = width_first // devices
    half = rows // 2
    share = width_first // 2
    me = lax.axis_index("pw")
    low_side = lax.axis_index("band") == 0
    nt = (((1,), (1,)), ((), ()))
    tn = (((0,), (0,)), ((), ()))
    near = second_ref[me]
    weights = [occupation_ref[n].astype(F32) for n in range(bands)]
    lanes = [slice(n * width_third, (n + 1) * width_third) for n in range(bands)]
    square = jnp.zeros((bands, count), F32)
    energies = [jnp.zeros((8, width_third), F32) for _ in range(bands)]
    centres = []

    for p in range(devices):
        waves = waves_ref[p].astype(F32)
        place = waves[2 * bands : 2 * bands + 8].astype(jnp.int32)
        first, second, third = place[0:1], place[1:2], place[2:3]
        line = lax.broadcasted_iota(jnp.int32, (LANES, count), 0)
        pick = jnp.where(line == second, 1.0, 0.0).astype(BF16)
        turn = jnp.dot(near, pick, preferred_element_type=F32)
        pick = jnp.where(line == third, 1.0, 0.0).astype(BF16)
        phase = jnp.dot(third_ref[...], jnp.concatenate([pick, pick]), preferred_element_type=F32)
        phase_s[p] = phase
        centre = turn[rows : rows + 2] + turn[rows + 2 : rows + 4]
        centres.append(centre)
        real, imag = waves[:bands], waves[bands : 2 * bands]
        square = square + real * real + imag * imag
        turned_real = real * centre[0:1] - imag * centre[1:2]
        turned_imag = real * centre[1:2] + imag * centre[0:1]
        inside = lax.broadcasted_iota(jnp.int32, (slab, count), 0) == first
        for k in range(rows):
            select_s[p, k * slab : (k + 1) * slab, :] = jnp.where(
                inside, turn[k : k + 1], 0.0
            ).astype(BF16)
        cosines, sines = phase[:width_third], phase[width_third:]
        for n in range(bands):
            a, b = turned_real[n : n + 1], turned_imag[n : n + 1]
            turned = jnp.concatenate([a * cosines - b * sines, a * sines + b * cosines]).astype(BF16)
            planes = lax.dot_general(select_s[p], turned, nt, preferred_element_type=F32)
            even, odd = planes[: half * slab], planes[half * slab :]
            even_real, even_imag = even[:, :width_third], even[:, width_third:]
            odd_real, odd_imag = odd[:, :width_third], odd[:, width_third:]
            plus_real = (even_real - odd_imag).astype(BF16)
            plus_imag = (even_imag + odd_real).astype(BF16)
            minus_real = (even_real + odd_imag).astype(BF16)
            minus_imag = (even_imag - odd_real).astype(BF16)
            real_rows = slice(p * slab, (p + 1) * slab)
            imag_rows = slice(width_first + p * slab, width_first + (p + 1) * slab)
            for k in range(half):
                part = slice(k * slab, (k + 1) * slab)
                slab_s[half + k, real_rows, lanes[n]] = plus_real[part]
                slab_s[half + k, imag_rows, lanes[n]] = plus_imag[part]
                slab_s[half - 1 - k, real_rows, lanes[n]] = minus_real[part]
                slab_s[half - 1 - k, imag_rows, lanes[n]] = minus_imag[part]

    fetch.wait()
    group = 2
    for k in range(half):
        densities = [0.0, 0.0]
        for start in range(0, bands, group):
            members = range(start, start + group)
            at = slice(start * width_third, (start + group) * width_third)
            results = []
            for sign, row in enumerate((half + k, half - 1 - k)):
                spatial = jnp.dot(back_ref[...], slab_s[row, :, at], preferred_element_type=F32)
                local = potential_ref[row]
                moved_real, moved_imag = [], []
                for i, n in enumerate(members):
                    real = spatial[:width_first, lanes[i]]
                    imag = spatial[width_first:, lanes[i]]
                    power = real * real + imag * imag
                    densities[sign] = densities[sign] + weights[n] * power
                    energy = (power * local).reshape(width_first // 8, 8, width_third)
                    energies[n] = energies[n] + jnp.sum(energy, axis=0)
                    moved_real.append((real * local).astype(BF16))
                    moved_imag.append((imag * local).astype(BF16))
                moved = jnp.concatenate(
                    [jnp.concatenate(moved_real, axis=1), jnp.concatenate(moved_imag, axis=1)]
                )
                results.append(jnp.dot(fore_ref[...], moved, preferred_element_type=F32))
            plus, minus = results
            total = (plus + minus).astype(BF16)
            gap = plus - minus
            gap_real = gap[width_first:].astype(BF16)
            gap_imag = (-gap[:width_first]).astype(BF16)
            for p in range(devices):
                mine = slice(p * slab, (p + 1) * slab)
                mine_imag = slice(width_first + p * slab, width_first + (p + 1) * slab)
                even_rows = slice(k * slab, (k + 1) * slab)
                odd_rows = slice((half + k) * slab, (half + k + 1) * slab)
                for i, n in enumerate(members):
                    to_real = slice(2 * n * width_third, (2 * n + 1) * width_third)
                    to_imag = slice((2 * n + 1) * width_third, (2 * n + 2) * width_third)
                    acted_s[p, even_rows, to_real] = total[mine, lanes[i]]
                    acted_s[p, even_rows, to_imag] = total[mine_imag, lanes[i]]
                    acted_s[p, odd_rows, to_real] = gap_real[mine, lanes[i]]
                    acted_s[p, odd_rows, to_imag] = gap_imag[mine, lanes[i]]
        for sign, row in enumerate((half + k, half - 1 - k)):
            low, high = densities[sign][:share], densities[sign][share:]
            own_ref[row] = jnp.where(low_side, low, high)
            other_ref[row] = jnp.where(low_side, high, low).astype(BF16)

    stores = [
        pltpu.make_async_copy(own_ref, own_out, done.at[0]),
        pltpu.make_async_copy(other_ref, other_out, done.at[1]),
    ]
    for store in stores:
        store.start()

    waves = waves_ref[me].astype(F32)
    real, imag = waves[:bands], waves[bands : 2 * bands]
    kinetic = kinetic_ref[...].reshape(1, count)
    moving = jnp.sum((real * real + imag * imag) * kinetic, axis=1, keepdims=True)
    energy = jnp.concatenate([jnp.sum(e, axis=(0, 1), keepdims=True) for e in energies])
    numerator = moving + energy
    denominator = jnp.sum(square, axis=1, keepdims=True) * (1.0 / devices)
    scalars = []
    for value in (numerator, denominator):
        high = value.astype(BF16)
        low = (value - high.astype(F32)).astype(BF16)
        both = jnp.concatenate([high.astype(F32), low.astype(F32)])
        scalars.append(jnp.broadcast_to(both, (2 * bands, LANES)))
    scalars = jnp.concatenate(scalars, axis=1).astype(BF16)

    for p in range(devices):
        cosines, sines = phase_s[p, :width_third], phase_s[p, width_third:]
        reals, imags = [], []
        for n in range(bands):
            at = slice(2 * n * width_third, 2 * (n + 1) * width_third)
            found = lax.dot_general(acted_s[p, :, at], select_s[p], tn, preferred_element_type=F32)
            real, imag = found[:width_third], found[width_third:]
            reals.append(
                jnp.sum(real * cosines, axis=0, keepdims=True)
                + jnp.sum(imag * sines, axis=0, keepdims=True)
            )
            imags.append(
                jnp.sum(imag * cosines, axis=0, keepdims=True)
                - jnp.sum(real * sines, axis=0, keepdims=True)
            )
        real, imag = jnp.concatenate(reals), jnp.concatenate(imags)
        cosine, sine = centres[p][0:1], centres[p][1:2]
        result = jnp.concatenate([real * cosine + imag * sine, imag * cosine - real * sine])
        sent_ref[p, :, :count] = result.astype(BF16)
        sent_ref[p, :, count:] = scalars

    for store in stores:
        store.wait()


def on_grid(waves, potential, kinetic, occupation, bands, width_second):
    devices, _, count = waves.shape
    rows, width_first, width_third = potential.shape
    slab = width_first // devices
    tables = wave_tables(devices, rows, width_first, width_second, width_third)
    vmem = pl.BlockSpec(memory_space=pltpu.VMEM)
    smem = pl.BlockSpec(memory_space=pltpu.SMEM)
    anywhere = pl.BlockSpec(memory_space=pl.ANY)
    planes = (rows, width_first // 2, width_third)
    return pl.pallas_call(
        functools.partial(grid_kernel, bands),
        out_shape=(
            jax.ShapeDtypeStruct((devices, 2 * bands, count + 2 * LANES), BF16),
            jax.ShapeDtypeStruct(planes, F32),
            jax.ShapeDtypeStruct(planes, BF16),
        ),
        in_specs=[vmem] * 5 + [anywhere, vmem, smem],
        out_specs=(vmem, anywhere, anywhere),
        scratch_shapes=[
            pltpu.VMEM((devices, 2 * width_third, count), F32),
            pltpu.VMEM((devices, rows * slab, count), BF16),
            pltpu.VMEM((rows, 2 * width_first, bands * width_third), BF16),
            pltpu.VMEM((devices, rows * slab, 2 * bands * width_third), BF16),
            pltpu.VMEM(potential.shape, F32),
            pltpu.VMEM(planes, F32),
            pltpu.VMEM(planes, BF16),
            pltpu.SemaphoreType.DMA((3,)),
        ],
        compiler_params=pltpu.CompilerParams(vmem_limit_bytes=56 * 1024 * 1024),
    )(waves, *[jnp.asarray(t) for t in tables], potential, kinetic, occupation)


def action_kernel(bands, arrived_ref, trial_ref, kinetic_ref, rows_ref, rest_ref):
    devices = arrived_ref.shape[0]
    count = kinetic_ref.shape[0]
    block = 2 * bands
    total = sum(arrived_ref[p].astype(F32) for p in range(devices))
    applied = total[:, :count]
    scalars = total[:bands, count:] + total[bands:, count:]
    ratio = scalars[:, 0:1] / (scalars[:, LANES : LANES + 1] + EPSILON)
    kinetic = kinetic_ref[...].reshape(1, count)
    damping = 1.0 / (1.0 + kinetic)
    trial = jnp.concatenate([trial_ref[part].astype(F32) for part in range(2)])
    action = kinetic * trial + applied
    damped = (action * damping).astype(BF16).astype(F32)
    soft = (trial * damping).astype(BF16).astype(F32)
    both = jnp.concatenate([ratio, ratio])
    rest_ref[...] = damped - both * soft
    high = ratio.astype(BF16).astype(F32)
    pair = jnp.broadcast_to(jnp.concatenate([high, ratio - high]), (block, LANES))
    unused = jnp.zeros((block, count), F32)
    rows = jnp.concatenate([action, damped, soft, unused])
    tail = jnp.concatenate([pair, pair, pair, pair])
    rows_ref[...] = jnp.concatenate([rows, tail], axis=1).astype(BF16)


def inner_kernel(bands, mine_ref, theirs_ref, all_ref, received_ref, sent_ref, passed_ref):
    count = all_ref.shape[2]
    block = 2 * bands
    first = lax.axis_index("band") == 0
    nt = (((1,), (1,)), ((), ()))
    mine, theirs = mine_ref[...].astype(F32), theirs_ref[...].astype(F32)
    low, high = jnp.where(first, mine, theirs), jnp.where(first, theirs, mine)
    pieces = []
    for at in range(0, 3 * block, bands):
        pieces += [low[at : at + bands], high[at : at + bands]]
    pair = pieces[0][:, count:] + pieces[2][:, count:], pieces[1][:, count:] + pieces[3][:, count:]
    ratio = jnp.concatenate(pair)[:, 0:1]
    rows = jnp.concatenate(pieces)[:, :count].astype(BF16)
    one = lax.dot_general(rows, all_ref[0], nt, preferred_element_type=F32)
    two = lax.dot_general(rows, all_ref[1], nt, preferred_element_type=F32)

    def inner(at):
        real = one[at : at + block] + two[at + block : at + 2 * block]
        imag = one[at + block : at + 2 * block] - two[at : at + block]
        return real, imag

    correlation = inner(0)
    damped = inner(2 * block)
    soft = inner(4 * block)
    coefficients = [d - ratio * s for d, s in zip(damped, soft)]
    sent_ref[...] = jnp.concatenate([*correlation, *coefficients]).astype(BF16)


def project_kernel(bands, parts, *refs):
    terms, (all_ref, rest_ref, _, correlation_ref, own_ref, sent_ref) = refs[:parts], refs[parts:]
    block = 2 * bands
    first = lax.axis_index("band") == 0
    total = sum(term[...].astype(F32) for term in terms)
    correlation_ref[...] = total[: 2 * block]
    coefficients = total[2 * block :].astype(BF16)
    one = jnp.dot(coefficients, all_ref[0], preferred_element_type=F32)
    two = jnp.dot(coefficients, all_ref[1], preferred_element_type=F32)
    real = one[:block] - two[block:]
    imag = one[block:] + two[:block]
    for part, value in enumerate((real, imag)):
        low, high = value[:bands], value[bands:]
        rest = rest_ref[part * bands : (part + 1) * bands]
        own_ref[part] = rest - jnp.where(first, low, high)
        sent_ref[part] = jnp.where(first, high, low)


def swap(values, axis, bit):
    size = lax.axis_size(axis)
    return lax.ppermute(values, axis, [(i, i ^ bit) for i in range(size)])


def in_waves(trial_block, all_bands, potential, rest_density, wave_cells, kinetic, occupation):
    devices = lax.axis_size("pw")
    _, rows, width_third = potential.shape
    width_second = rows * devices
    _, bands, count = trial_block.shape
    states = all_bands.shape[1]
    block = 2 * bands
    vmem = pl.BlockSpec(memory_space=pltpu.VMEM)
    anywhere = pl.BlockSpec(memory_space=pl.ANY)
    params = pltpu.CompilerParams(vmem_limit_bytes=16 * 1024 * 1024)
    packets = pl.pallas_call(
        functools.partial(pack_kernel, bands, devices, width_second, width_third),
        out_shape=jax.ShapeDtypeStruct((devices, 16, count), BF16),
        in_specs=[vmem] * 2,
        out_specs=vmem,
        compiler_params=pltpu.CompilerParams(vmem_limit_bytes=56 * 1024 * 1024),
    )(trial_block, wave_cells)
    waves = lax.all_to_all(packets, "pw", split_axis=0, concat_axis=0, tiled=True)
    partial, density_own, density_other = on_grid(
        waves, potential.transpose(1, 0, 2), kinetic, occupation, bands, width_second
    )
    arrived = lax.all_to_all(partial, "pw", split_axis=0, concat_axis=0, tiled=True)
    received = swap(density_other, "band", 1)
    mine, rest = pl.pallas_call(
        functools.partial(action_kernel, bands),
        out_shape=(
            jax.ShapeDtypeStruct((4 * block, count + LANES), BF16),
            jax.ShapeDtypeStruct((block, count), F32),
        ),
        in_specs=[vmem] * 3,
        out_specs=(vmem, vmem),
        compiler_params=params,
    )(arrived, trial_block, kinetic)
    theirs = swap(mine, "band", 1)
    sums, received = pl.pallas_call(
        functools.partial(inner_kernel, bands),
        out_shape=(
            jax.ShapeDtypeStruct((4 * block, states), BF16),
            jax.ShapeDtypeStruct(received.shape, received.dtype),
        ),
        in_specs=[vmem] * 3 + [anywhere],
        out_specs=(vmem, anywhere),
        input_output_aliases={3: 1},
        compiler_params=params,
    )(mine, theirs, all_bands, received)
    density = rest_density + (density_own + received.astype(F32)).transpose(1, 0, 2)
    near = sums + swap(sums, "pw", 1)
    terms = [near] + [swap(near, "pw", step) for step in range(2, devices, 2)]
    correlation, own, sent = pl.pallas_call(
        functools.partial(project_kernel, bands, len(terms)),
        out_shape=(
            jax.ShapeDtypeStruct((2 * block, states), F32),
            jax.ShapeDtypeStruct((2, bands, count), F32),
            jax.ShapeDtypeStruct((2, bands, count), F32),
        ),
        in_specs=[vmem] * (len(terms) + 2) + [anywhere],
        out_specs=(vmem, vmem, vmem),
        compiler_params=params,
    )(*terms, all_bands, rest, density)
    correction = own - swap(sent, "band", 1)
    correlation = correlation.reshape(2, block, states).transpose(0, 2, 1)
    return (correction, correlation, density)


def fits(trial_block, potential, mesh):
    devices = mesh.shape["pw"]
    width_first, width_second, width_third = potential.shape[0] // mesh.shape["ens"], *potential.shape[1:]
    slab, rows = width_first // devices, width_second // devices
    bands = trial_block.shape[1] // mesh.shape["band"]
    return (
        mesh.shape["band"] == 2
        and devices >= 2
        and devices & (devices - 1) == 0
        and slab % 16 == 0
        and rows % 16 == 0
        and width_first % LANES == 0
        and width_second == LANES
        and width_third == LANES
        and bands == 4
        and trial_block.shape[2] // devices % LANES == 0
    )


def tables(length):
    positions = jnp.arange(length, dtype=jnp.int32)
    products = positions[:, None] * positions[None, :] % length
    angles = products.astype(jnp.float32) * (2.0 * math.pi / length)
    factor = 1.0 / math.sqrt(length)
    cosines = jnp.cos(angles) * factor
    sines = jnp.sin(angles) * factor
    backward = jnp.stack([jnp.stack([cosines, -sines]), jnp.stack([sines, cosines])])
    forward = jnp.stack([jnp.stack([cosines, sines]), jnp.stack([-sines, cosines])])
    return (backward, forward)


def transform(fields, table, formula):
    return jnp.einsum(formula, table, fields, precision=HIGHEST)


def inner(left, right):
    contract = (((1,), (1,)), ((), ()))
    first = lax.dot_general(left[0], right[0], contract, preferred_element_type=jnp.float32)
    second = lax.dot_general(left[1], right[1], contract, preferred_element_type=jnp.float32)
    cross_one = lax.dot_general(left[0], right[1], contract, preferred_element_type=jnp.float32)
    cross_two = lax.dot_general(left[1], right[0], contract, preferred_element_type=jnp.float32)
    return jnp.stack([first + second, cross_one - cross_two])


def on_device(trial_block, all_bands, potential, rest_density, wave_cells, kinetic, occupation):
    devices = lax.axis_size("pw")
    width_first, rows_second, width_third = potential.shape
    width_second = rows_second * devices
    slab_rows = width_first // devices
    blocks = trial_block.shape[1]
    back_first, fore_first = tables(width_first)
    back_second, fore_second = tables(width_second)
    back_third, fore_third = tables(width_third)
    along_third = "pqkc,qnabc->pnabk"
    along_second = "pqkb,qnabc->pnakc"
    along_first = "pqka,qnabc->pnkbc"
    trial_float = trial_block.astype(jnp.float32)
    filled = jnp.zeros((2, blocks, slab_rows * width_second * width_third), jnp.float32)
    filled = filled.at[:, :, wave_cells].set(trial_float)
    filled = filled.reshape(2, blocks, slab_rows, width_second, width_third)
    filled = transform(filled, back_third, along_third)
    filled = transform(filled, back_second, along_second)
    spatial = transform(
        lax.all_to_all(filled, "pw", split_axis=3, concat_axis=2, tiled=True),
        back_first,
        along_first,
    )
    power = spatial[0] * spatial[0] + spatial[1] * spatial[1]
    acted = transform(spatial * potential, fore_first, along_first)
    returned = lax.all_to_all(acted, "pw", split_axis=2, concat_axis=3, tiled=True)
    columns, power = (returned, power[None])
    columns = transform(columns, fore_second, along_second)
    columns = transform(columns, fore_third, along_third)
    applied = columns.reshape(2, blocks, slab_rows * width_second * width_third)[:, :, wave_cells]
    weights = occupation.astype(jnp.float32)
    density_part = jnp.einsum("n,nabc->abc", weights, power[0], precision=HIGHEST)
    summed_density = lax.psum(density_part.astype(jnp.bfloat16), "band").astype(jnp.float32)
    share = width_first // lax.axis_size("band")
    block_density = lax.dynamic_slice_in_dim(
        summed_density, lax.axis_index("band") * share, share, 0
    )
    density = rest_density + block_density
    action = kinetic * trial_float + applied
    damping = 1.0 / (1.0 + kinetic)
    action_half = action.astype(jnp.bfloat16)
    damped = (action * damping).astype(jnp.bfloat16)
    softened = (trial_float * damping).astype(jnp.bfloat16)
    every_trial, every_action, every_damped, every_softened = (
        lax.all_gather(trial_block, "band", axis=1, tiled=True),
        lax.all_gather(action_half, "band", axis=1, tiled=True),
        lax.all_gather(damped, "band", axis=1, tiled=True),
        lax.all_gather(softened, "band", axis=1, tiled=True),
    )
    trial_wide = every_trial.astype(jnp.float32)
    numerator = jnp.sum(trial_wide * every_action.astype(jnp.float32), axis=(0, 2))
    denominator = jnp.sum(trial_wide * trial_wide, axis=(0, 2))
    correlation = inner(all_bands, every_action)
    correlation, numerator, denominator = lax.psum((correlation, numerator, denominator), "pw")
    rayleigh = numerator / (denominator + EPSILON)
    local_terms = inner(all_bands, every_damped) - rayleigh * inner(all_bands, every_softened)
    coefficients = lax.psum(local_terms, "pw")
    coefficient_half = coefficients.astype(jnp.bfloat16)
    real_piece = coefficient_half[0]
    imag_piece = coefficient_half[1]
    contract = (((0,), (0,)), ((), ()))
    real_real = lax.dot_general(
        real_piece, all_bands[0], contract, preferred_element_type=jnp.float32
    )
    imag_imag = lax.dot_general(
        imag_piece, all_bands[1], contract, preferred_element_type=jnp.float32
    )
    imag_real = lax.dot_general(
        imag_piece, all_bands[0], contract, preferred_element_type=jnp.float32
    )
    real_imag = lax.dot_general(
        real_piece, all_bands[1], contract, preferred_element_type=jnp.float32
    )
    projected = lax.psum_scatter(
        jnp.concatenate(
            [(real_real - imag_imag)[:, None], (imag_real + real_imag)[:, None]], axis=1
        ),
        "band",
        scatter_dimension=0,
        tiled=True,
    )
    own_ratio = lax.dynamic_slice_in_dim(rayleigh, lax.axis_index("band") * blocks, blocks, 0)
    real_correction = (
        damped[0].astype(jnp.float32)
        - own_ratio[:, None] * softened[0].astype(jnp.float32)
        - projected[:, 0]
    )
    imag_correction = (
        damped[1].astype(jnp.float32)
        - own_ratio[:, None] * softened[1].astype(jnp.float32)
        - projected[:, 1]
    )
    correction = jnp.stack([real_correction, imag_correction])
    return (correction, correlation, density)


def solution(mesh):
    placed = (
        P("ens", "band", "pw"),
        P("ens", "band", "pw"),
        P("ens", "pw", None),
        P(("ens", "band"), "pw", None),
        P("pw"),
        P("pw"),
        P(("ens", "band")),
    )
    results = (P("ens", "band", "pw"), P("ens", "band", None), P(("ens", "band"), "pw", None))

    def program(*arguments):
        body = in_waves if fits(arguments[0], arguments[2], mesh) else on_device
        return jax.shard_map(
            body, mesh=mesh, in_specs=placed, out_specs=results, check_vma=False
        )(*arguments)

    return program
```

```python
import functools
import math

import jax
import jax.numpy as jnp
import numpy as np
from jax import lax
from jax.experimental import pallas as pl
from jax.experimental.pallas import tpu as pltpu
from jax.sharding import PartitionSpec as P

EPSILON = 1e-06
HIGHEST = lax.Precision.HIGHEST
BF16 = jnp.bfloat16
F32 = jnp.float32
LANES = 128


def split_pair(values):
    high = values.astype(BF16)
    low = (values - high.astype(np.float64)).astype(BF16)
    return high, low


def wave_tables(devices, rows, width_first, width_second, width_third):
    half = rows // 2
    second = np.arange(width_second)
    steps = np.outer(2 * np.arange(half) + 1, second) % (2 * width_second)
    angles = steps * (math.pi / width_second)
    near = np.concatenate([np.cos(angles), np.sin(angles)])
    blocks = []
    for device in range(devices):
        middle = 2 * rows * device + rows - 1
        turns = (middle * second % (2 * width_second)) * (math.pi / width_second)
        centre = np.stack([np.cos(turns), np.sin(turns)])
        high, low = split_pair(centre)
        blocks.append(np.concatenate([near.astype(BF16), high, low]))
    second_table = np.stack(blocks)
    missing = -second_table.shape[1] % 16
    second_table = np.pad(second_table, ((0, 0), (0, missing), (0, 0)))
    third = np.arange(width_third)
    angles = np.outer(third[: width_third // 2], third) % width_third * (2 * math.pi / width_third)
    factor = 1.0 / math.sqrt(width_second * width_third)
    values = np.concatenate([np.cos(angles), np.sin(angles)]) * factor
    third_table = np.concatenate(split_pair(values), axis=1)
    first = np.arange(width_first)
    angles = (np.outer(first, first) % width_first) * (2 * math.pi / width_first)
    cosines = np.cos(angles) / math.sqrt(width_first)
    sines = np.sin(angles) / math.sqrt(width_first)
    back = np.block([[cosines, -sines], [sines, cosines]]).astype(BF16)
    fore = np.block([[cosines, sines], [-sines, cosines]]).astype(BF16)
    return second_table, third_table, back, fore


def pack_kernel(bands, devices, width_second, width_third, trial_ref, cells_ref, packet_ref):
    cells = cells_ref[...].reshape(1, cells_ref.shape[0])
    first = lax.div(cells, width_second * width_third)
    second = lax.rem(lax.div(cells, width_third), width_second)
    third = lax.rem(cells, width_third)
    unused = jnp.zeros((packet_ref.shape[1] - 2 * bands - 3, cells.shape[1]), jnp.int32)
    place = jnp.concatenate([first, second, third, unused]).astype(F32)
    trial = [trial_ref[part].astype(F32) for part in range(2)]
    packet = jnp.concatenate([*trial, place]).astype(BF16)
    for p in range(devices):
        packet_ref[p] = packet


def grid_kernel(
    bands,
    waves_ref,
    second_ref,
    third_ref,
    back_ref,
    fore_ref,
    potential_in,
    kinetic_ref,
    occupation_ref,
    sent_ref,
    own_out,
    other_out,
    phase_s,
    select_s,
    slab_s,
    acted_s,
    potential_ref,
    own_ref,
    other_ref,
    done,
):
    devices, _, count = waves_ref.shape
    fetch = pltpu.make_async_copy(potential_in, potential_ref, done.at[2])
    fetch.start()
    rows, width_first, width_third = potential_ref.shape
    slab = width_first // devices
    half = rows // 2
    share = width_first // 2
    me = lax.axis_index("pw")
    low_side = lax.axis_index("band") == 0
    nt = (((1,), (1,)), ((), ()))
    tn = (((0,), (0,)), ((), ()))
    near = second_ref[me]
    fold = width_third // 2
    full = rows * slab
    groups = bands // 2
    low_lanes = lax.broadcasted_iota(jnp.int32, (1, width_third), 1) < fold
    square = jnp.zeros((bands, count), F32)
    energies = [jnp.zeros((8, width_third), F32) for _ in range(groups)]
    weights = [
        jnp.where(
            low_lanes, occupation_ref[2 * g].astype(F32), occupation_ref[2 * g + 1].astype(F32)
        )
        for g in range(groups)
    ]
    centres = []

    for p in range(devices):
        waves = waves_ref[p].astype(F32)
        place = waves[2 * bands : 2 * bands + 8].astype(jnp.int32)
        first, second, third = place[0:1], place[1:2], place[2:3]
        line = lax.broadcasted_iota(jnp.int32, (LANES, count), 0)
        pick = jnp.where(line == second, 1.0, 0.0).astype(BF16)
        turn = jnp.dot(near, pick, preferred_element_type=F32)
        pick = jnp.where(line == third, 1.0, 0.0).astype(BF16)
        phase = jnp.dot(third_ref[...], jnp.concatenate([pick, pick]), preferred_element_type=F32)
        phase_s[p] = phase
        centre = turn[rows : rows + 2] + turn[rows + 2 : rows + 4]
        centres.append(centre)
        real, imag = waves[:bands], waves[bands : 2 * bands]
        square = square + real * real + imag * imag
        turned_real = real * centre[0:1] - imag * centre[1:2]
        turned_imag = real * centre[1:2] + imag * centre[0:1]
        inside = lax.broadcasted_iota(jnp.int32, (slab, count), 0) == first
        sign = jnp.where(lax.rem(third, 2) == 0, 1.0, -1.0)
        near_turn, far_turn = turn[:rows], turn[:rows] * sign
        for k in range(rows):
            at = slice(k * slab, (k + 1) * slab)
            select_s[p, at, :] = jnp.where(inside, near_turn[k : k + 1], 0.0).astype(BF16)
            at = slice(full + k * slab, full + (k + 1) * slab)
            select_s[p, at, :] = jnp.where(inside, far_turn[k : k + 1], 0.0).astype(BF16)
        cosines, sines = phase[:fold], phase[fold:]
        for g in range(groups):
            reals, imags = [], []
            for n in (2 * g, 2 * g + 1):
                a, b = turned_real[n : n + 1], turned_imag[n : n + 1]
                reals.append(a * cosines - b * sines)
                imags.append(a * sines + b * cosines)
            turned = jnp.concatenate(reals + imags).astype(BF16)
            planes = lax.dot_general(select_s[p], turned, nt, preferred_element_type=F32)
            for h in range(2):
                even = planes[h * full : h * full + full // 2]
                odd = planes[h * full + full // 2 : (h + 1) * full]
                even_real, even_imag = even[:, :width_third], even[:, width_third:]
                odd_real, odd_imag = odd[:, :width_third], odd[:, width_third:]
                plus_real = (even_real - odd_imag).astype(BF16)
                plus_imag = (even_imag + odd_real).astype(BF16)
                minus_real = (even_real + odd_imag).astype(BF16)
                minus_imag = (even_imag - odd_real).astype(BF16)
                real_rows = slice(p * slab, (p + 1) * slab)
                imag_rows = slice(width_first + p * slab, width_first + (p + 1) * slab)
                to = slice((2 * g + h) * width_third, (2 * g + h + 1) * width_third)
                for k in range(half):
                    part = slice(k * slab, (k + 1) * slab)
                    slab_s[half + k, real_rows, to] = plus_real[part]
                    slab_s[half + k, imag_rows, to] = plus_imag[part]
                    slab_s[half - 1 - k, real_rows, to] = minus_real[part]
                    slab_s[half - 1 - k, imag_rows, to] = minus_imag[part]

    fetch.wait()
    blocks = [slice(h * width_third, (h + 1) * width_third) for h in range(2)]
    for k in range(half):
        densities = [[0.0, 0.0], [0.0, 0.0]]
        locals_ = []
        for row in (half + k, half - 1 - k):
            values = potential_ref[row]
            other = pltpu.roll(values, fold, 1)
            locals_.append(
                (jnp.where(low_lanes, values, other), jnp.where(low_lanes, other, values))
            )
        for g in range(groups):
            at = slice(2 * g * width_third, (2 * g + 2) * width_third)
            results = []
            for side, row in enumerate((half + k, half - 1 - k)):
                spatial = jnp.dot(back_ref[...], slab_s[row, :, at], preferred_element_type=F32)
                moved_real, moved_imag = [], []
                for h in range(2):
                    local = locals_[side][h]
                    real = spatial[:width_first, blocks[h]]
                    imag = spatial[width_first:, blocks[h]]
                    power = real * real + imag * imag
                    densities[side][h] = densities[side][h] + weights[g] * power
                    energy = (power * local).reshape(width_first // 8, 8, width_third)
                    energies[g] = energies[g] + jnp.sum(energy, axis=0)
                    moved_real.append((real * local).astype(BF16))
                    moved_imag.append((imag * local).astype(BF16))
                moved = jnp.concatenate(
                    [jnp.concatenate(moved_real, axis=1), jnp.concatenate(moved_imag, axis=1)]
                )
                results.append(jnp.dot(fore_ref[...], moved, preferred_element_type=F32))
            plus, minus = results
            total = (plus + minus).astype(BF16)
            gap = plus - minus
            gap_real = gap[width_first:].astype(BF16)
            gap_imag = (-gap[:width_first]).astype(BF16)
            to_real = slice(2 * g * width_third, (2 * g + 1) * width_third)
            to_imag = slice((2 * g + 1) * width_third, (2 * g + 2) * width_third)
            for p in range(devices):
                mine = slice(p * slab, (p + 1) * slab)
                mine_imag = slice(width_first + p * slab, width_first + (p + 1) * slab)
                for h in range(2):
                    even_rows = slice(h * full + k * slab, h * full + (k + 1) * slab)
                    start = h * full + full // 2 + k * slab
                    odd_rows = slice(start, start + slab)
                    acted_s[p, even_rows, to_real] = total[mine, blocks[h]]
                    acted_s[p, even_rows, to_imag] = total[mine_imag, blocks[h]]
                    acted_s[p, odd_rows, to_real] = gap_real[mine, blocks[h]]
                    acted_s[p, odd_rows, to_imag] = gap_imag[mine, blocks[h]]
        for side, row in enumerate((half + k, half - 1 - k)):
            folded = [d + pltpu.roll(d, fold, 1) for d in densities[side]]
            density = jnp.where(low_lanes, *folded)
            low, high = density[:share], density[share:]
            own_ref[row] = jnp.where(low_side, low, high)
            other_ref[row] = jnp.where(low_side, high, low).astype(BF16)

    stores = [
        pltpu.make_async_copy(own_ref, own_out, done.at[0]),
        pltpu.make_async_copy(other_ref, other_out, done.at[1]),
    ]
    for store in stores:
        store.start()

    waves = waves_ref[me].astype(F32)
    real, imag = waves[:bands], waves[bands : 2 * bands]
    kinetic = kinetic_ref[...].reshape(1, count)
    moving = jnp.sum((real * real + imag * imag) * kinetic, axis=1, keepdims=True)
    energy = []
    for values in energies:
        for part in (jnp.where(low_lanes, values, 0.0), jnp.where(low_lanes, 0.0, values)):
            energy.append(jnp.sum(part, axis=(0, 1), keepdims=True))
    energy = jnp.concatenate(energy)
    numerator = moving + energy
    denominator = jnp.sum(square, axis=1, keepdims=True) * (1.0 / devices)
    scalars = []
    for value in (numerator, denominator):
        high = value.astype(BF16)
        low = (value - high.astype(F32)).astype(BF16)
        both = jnp.concatenate([high.astype(F32), low.astype(F32)])
        scalars.append(jnp.broadcast_to(both, (2 * bands, LANES)))
    scalars = jnp.concatenate(scalars, axis=1).astype(BF16)

    for p in range(devices):
        cosines, sines = phase_s[p, :fold], phase_s[p, fold:]
        reals, imags = [], []
        for g in range(groups):
            at = slice(2 * g * width_third, 2 * (g + 1) * width_third)
            found = lax.dot_general(acted_s[p, :, at], select_s[p], tn, preferred_element_type=F32)
            for i in range(2):
                real = found[i * fold : (i + 1) * fold]
                imag = found[width_third + i * fold : width_third + (i + 1) * fold]
                reals.append(
                    jnp.sum(real * cosines, axis=0, keepdims=True)
                    + jnp.sum(imag * sines, axis=0, keepdims=True)
                )
                imags.append(
                    jnp.sum(imag * cosines, axis=0, keepdims=True)
                    - jnp.sum(real * sines, axis=0, keepdims=True)
                )
        real, imag = jnp.concatenate(reals), jnp.concatenate(imags)
        cosine, sine = centres[p][0:1], centres[p][1:2]
        result = jnp.concatenate([real * cosine + imag * sine, imag * cosine - real * sine])
        sent_ref[p, :, :count] = result.astype(BF16)
        sent_ref[p, :, count:] = scalars

    for store in stores:
        store.wait()


def on_grid(waves, potential, kinetic, occupation, bands, width_second):
    devices, _, count = waves.shape
    rows, width_first, width_third = potential.shape
    slab = width_first // devices
    tables = wave_tables(devices, rows, width_first, width_second, width_third)
    vmem = pl.BlockSpec(memory_space=pltpu.VMEM)
    smem = pl.BlockSpec(memory_space=pltpu.SMEM)
    anywhere = pl.BlockSpec(memory_space=pl.ANY)
    planes = (rows, width_first // 2, width_third)
    return pl.pallas_call(
        functools.partial(grid_kernel, bands),
        out_shape=(
            jax.ShapeDtypeStruct((devices, 2 * bands, count + 2 * LANES), BF16),
            jax.ShapeDtypeStruct(planes, F32),
            jax.ShapeDtypeStruct(planes, BF16),
        ),
        in_specs=[vmem] * 5 + [anywhere, vmem, smem],
        out_specs=(vmem, anywhere, anywhere),
        scratch_shapes=[
            pltpu.VMEM((devices, width_third, count), F32),
            pltpu.VMEM((devices, 2 * rows * slab, count), BF16),
            pltpu.VMEM((rows, 2 * width_first, bands * width_third), BF16),
            pltpu.VMEM((devices, 2 * rows * slab, bands * width_third), BF16),
            pltpu.VMEM(potential.shape, F32),
            pltpu.VMEM(planes, F32),
            pltpu.VMEM(planes, BF16),
            pltpu.SemaphoreType.DMA((3,)),
        ],
        compiler_params=pltpu.CompilerParams(vmem_limit_bytes=56 * 1024 * 1024),
    )(waves, *[jnp.asarray(t) for t in tables], potential, kinetic, occupation)


def action_kernel(bands, arrived_ref, trial_ref, kinetic_ref, rows_ref, rest_ref):
    devices = arrived_ref.shape[0]
    count = kinetic_ref.shape[0]
    block = 2 * bands
    total = sum(arrived_ref[p].astype(F32) for p in range(devices))
    applied = total[:, :count]
    scalars = total[:bands, count:] + total[bands:, count:]
    ratio = scalars[:, 0:1] / (scalars[:, LANES : LANES + 1] + EPSILON)
    kinetic = kinetic_ref[...].reshape(1, count)
    damping = 1.0 / (1.0 + kinetic)
    trial = jnp.concatenate([trial_ref[part].astype(F32) for part in range(2)])
    action = kinetic * trial + applied
    damped = (action * damping).astype(BF16).astype(F32)
    soft = (trial * damping).astype(BF16).astype(F32)
    both = jnp.concatenate([ratio, ratio])
    rest_ref[...] = damped - both * soft
    high = ratio.astype(BF16).astype(F32)
    pair = jnp.broadcast_to(jnp.concatenate([high, ratio - high]), (block, LANES))
    unused = jnp.zeros((block, count), F32)
    rows = jnp.concatenate([action, damped, soft, unused])
    tail = jnp.concatenate([pair, pair, pair, pair])
    rows_ref[...] = jnp.concatenate([rows, tail], axis=1).astype(BF16)


def inner_kernel(bands, mine_ref, theirs_ref, all_ref, received_ref, sent_ref, passed_ref):
    count = all_ref.shape[2]
    block = 2 * bands
    first = lax.axis_index("band") == 0
    nt = (((1,), (1,)), ((), ()))
    mine, theirs = mine_ref[...].astype(F32), theirs_ref[...].astype(F32)
    low, high = jnp.where(first, mine, theirs), jnp.where(first, theirs, mine)
    pieces = []
    for at in range(0, 3 * block, bands):
        pieces += [low[at : at + bands], high[at : at + bands]]
    pair = pieces[0][:, count:] + pieces[2][:, count:], pieces[1][:, count:] + pieces[3][:, count:]
    ratio = jnp.concatenate(pair)[:, 0:1]
    rows = jnp.concatenate(pieces)[:, :count].astype(BF16)
    one = lax.dot_general(rows, all_ref[0], nt, preferred_element_type=F32)
    two = lax.dot_general(rows, all_ref[1], nt, preferred_element_type=F32)

    def inner(at):
        real = one[at : at + block] + two[at + block : at + 2 * block]
        imag = one[at + block : at + 2 * block] - two[at : at + block]
        return real, imag

    correlation = inner(0)
    damped = inner(2 * block)
    soft = inner(4 * block)
    coefficients = [d - ratio * s for d, s in zip(damped, soft)]
    sent_ref[...] = jnp.concatenate([*correlation, *coefficients]).astype(BF16)


def project_kernel(bands, parts, *refs):
    terms, (all_ref, rest_ref, _, correlation_ref, own_ref, sent_ref) = refs[:parts], refs[parts:]
    block = 2 * bands
    first = lax.axis_index("band") == 0
    total = sum(term[...].astype(F32) for term in terms)
    correlation_ref[...] = total[: 2 * block]
    coefficients = total[2 * block :].astype(BF16)
    one = jnp.dot(coefficients, all_ref[0], preferred_element_type=F32)
    two = jnp.dot(coefficients, all_ref[1], preferred_element_type=F32)
    real = one[:block] - two[block:]
    imag = one[block:] + two[:block]
    for part, value in enumerate((real, imag)):
        low, high = value[:bands], value[bands:]
        rest = rest_ref[part * bands : (part + 1) * bands]
        own_ref[part] = rest - jnp.where(first, low, high)
        sent_ref[part] = jnp.where(first, high, low)


def swap(values, axis, bit):
    size = lax.axis_size(axis)
    return lax.ppermute(values, axis, [(i, i ^ bit) for i in range(size)])


def in_waves(trial_block, all_bands, potential, rest_density, wave_cells, kinetic, occupation):
    devices = lax.axis_size("pw")
    _, rows, width_third = potential.shape
    width_second = rows * devices
    _, bands, count = trial_block.shape
    states = all_bands.shape[1]
    block = 2 * bands
    vmem = pl.BlockSpec(memory_space=pltpu.VMEM)
    anywhere = pl.BlockSpec(memory_space=pl.ANY)
    params = pltpu.CompilerParams(vmem_limit_bytes=16 * 1024 * 1024)
    packets = pl.pallas_call(
        functools.partial(pack_kernel, bands, devices, width_second, width_third),
        out_shape=jax.ShapeDtypeStruct((devices, 16, count), BF16),
        in_specs=[vmem] * 2,
        out_specs=vmem,
        compiler_params=pltpu.CompilerParams(vmem_limit_bytes=56 * 1024 * 1024),
    )(trial_block, wave_cells)
    waves = lax.all_to_all(packets, "pw", split_axis=0, concat_axis=0, tiled=True)
    partial, density_own, density_other = on_grid(
        waves, potential.transpose(1, 0, 2), kinetic, occupation, bands, width_second
    )
    arrived = lax.all_to_all(partial, "pw", split_axis=0, concat_axis=0, tiled=True)
    received = swap(density_other, "band", 1)
    mine, rest = pl.pallas_call(
        functools.partial(action_kernel, bands),
        out_shape=(
            jax.ShapeDtypeStruct((4 * block, count + LANES), BF16),
            jax.ShapeDtypeStruct((block, count), F32),
        ),
        in_specs=[vmem] * 3,
        out_specs=(vmem, vmem),
        compiler_params=params,
    )(arrived, trial_block, kinetic)
    theirs = swap(mine, "band", 1)
    sums, received = pl.pallas_call(
        functools.partial(inner_kernel, bands),
        out_shape=(
            jax.ShapeDtypeStruct((4 * block, states), BF16),
            jax.ShapeDtypeStruct(received.shape, received.dtype),
        ),
        in_specs=[vmem] * 3 + [anywhere],
        out_specs=(vmem, anywhere),
        input_output_aliases={3: 1},
        compiler_params=params,
    )(mine, theirs, all_bands, received)
    density = rest_density + (density_own + received.astype(F32)).transpose(1, 0, 2)
    near = sums + swap(sums, "pw", 1)
    terms = [near] + [swap(near, "pw", step) for step in range(2, devices, 2)]
    correlation, own, sent = pl.pallas_call(
        functools.partial(project_kernel, bands, len(terms)),
        out_shape=(
            jax.ShapeDtypeStruct((2 * block, states), F32),
            jax.ShapeDtypeStruct((2, bands, count), F32),
            jax.ShapeDtypeStruct((2, bands, count), F32),
        ),
        in_specs=[vmem] * (len(terms) + 2) + [anywhere],
        out_specs=(vmem, vmem, vmem),
        compiler_params=params,
    )(*terms, all_bands, rest, density)
    correction = own - swap(sent, "band", 1)
    correlation = correlation.reshape(2, block, states).transpose(0, 2, 1)
    return (correction, correlation, density)


def fits(trial_block, potential, mesh):
    devices = mesh.shape["pw"]
    width_first, width_second, width_third = potential.shape[0] // mesh.shape["ens"], *potential.shape[1:]
    slab, rows = width_first // devices, width_second // devices
    bands = trial_block.shape[1] // mesh.shape["band"]
    return (
        mesh.shape["band"] == 2
        and devices >= 2
        and devices & (devices - 1) == 0
        and slab % 16 == 0
        and rows % 16 == 0
        and width_first % LANES == 0
        and width_second == LANES
        and width_third == LANES
        and bands == 4
        and trial_block.shape[2] // devices % LANES == 0
    )


def tables(length):
    positions = jnp.arange(length, dtype=jnp.int32)
    products = positions[:, None] * positions[None, :] % length
    angles = products.astype(jnp.float32) * (2.0 * math.pi / length)
    factor = 1.0 / math.sqrt(length)
    cosines = jnp.cos(angles) * factor
    sines = jnp.sin(angles) * factor
    backward = jnp.stack([jnp.stack([cosines, -sines]), jnp.stack([sines, cosines])])
    forward = jnp.stack([jnp.stack([cosines, sines]), jnp.stack([-sines, cosines])])
    return (backward, forward)


def transform(fields, table, formula):
    return jnp.einsum(formula, table, fields, precision=HIGHEST)


def inner(left, right):
    contract = (((1,), (1,)), ((), ()))
    first = lax.dot_general(left[0], right[0], contract, preferred_element_type=jnp.float32)
    second = lax.dot_general(left[1], right[1], contract, preferred_element_type=jnp.float32)
    cross_one = lax.dot_general(left[0], right[1], contract, preferred_element_type=jnp.float32)
    cross_two = lax.dot_general(left[1], right[0], contract, preferred_element_type=jnp.float32)
    return jnp.stack([first + second, cross_one - cross_two])


def on_device(trial_block, all_bands, potential, rest_density, wave_cells, kinetic, occupation):
    devices = lax.axis_size("pw")
    width_first, rows_second, width_third = potential.shape
    width_second = rows_second * devices
    slab_rows = width_first // devices
    blocks = trial_block.shape[1]
    back_first, fore_first = tables(width_first)
    back_second, fore_second = tables(width_second)
    back_third, fore_third = tables(width_third)
    along_third = "pqkc,qnabc->pnabk"
    along_second = "pqkb,qnabc->pnakc"
    along_first = "pqka,qnabc->pnkbc"
    trial_float = trial_block.astype(jnp.float32)
    filled = jnp.zeros((2, blocks, slab_rows * width_second * width_third), jnp.float32)
    filled = filled.at[:, :, wave_cells].set(trial_float)
    filled = filled.reshape(2, blocks, slab_rows, width_second, width_third)
    filled = transform(filled, back_third, along_third)
    filled = transform(filled, back_second, along_second)
    spatial = transform(
        lax.all_to_all(filled, "pw", split_axis=3, concat_axis=2, tiled=True),
        back_first,
        along_first,
    )
    power = spatial[0] * spatial[0] + spatial[1] * spatial[1]
    acted = transform(spatial * potential, fore_first, along_first)
    returned = lax.all_to_all(acted, "pw", split_axis=2, concat_axis=3, tiled=True)
    columns, power = (returned, power[None])
    columns = transform(columns, fore_second, along_second)
    columns = transform(columns, fore_third, along_third)
    applied = columns.reshape(2, blocks, slab_rows * width_second * width_third)[:, :, wave_cells]
    weights = occupation.astype(jnp.float32)
    density_part = jnp.einsum("n,nabc->abc", weights, power[0], precision=HIGHEST)
    summed_density = lax.psum(density_part.astype(jnp.bfloat16), "band").astype(jnp.float32)
    share = width_first // lax.axis_size("band")
    block_density = lax.dynamic_slice_in_dim(
        summed_density, lax.axis_index("band") * share, share, 0
    )
    density = rest_density + block_density
    action = kinetic * trial_float + applied
    damping = 1.0 / (1.0 + kinetic)
    action_half = action.astype(jnp.bfloat16)
    damped = (action * damping).astype(jnp.bfloat16)
    softened = (trial_float * damping).astype(jnp.bfloat16)
    every_trial, every_action, every_damped, every_softened = (
        lax.all_gather(trial_block, "band", axis=1, tiled=True),
        lax.all_gather(action_half, "band", axis=1, tiled=True),
        lax.all_gather(damped, "band", axis=1, tiled=True),
        lax.all_gather(softened, "band", axis=1, tiled=True),
    )
    trial_wide = every_trial.astype(jnp.float32)
    numerator = jnp.sum(trial_wide * every_action.astype(jnp.float32), axis=(0, 2))
    denominator = jnp.sum(trial_wide * trial_wide, axis=(0, 2))
    correlation = inner(all_bands, every_action)
    correlation, numerator, denominator = lax.psum((correlation, numerator, denominator), "pw")
    rayleigh = numerator / (denominator + EPSILON)
    local_terms = inner(all_bands, every_damped) - rayleigh * inner(all_bands, every_softened)
    coefficients = lax.psum(local_terms, "pw")
    coefficient_half = coefficients.astype(jnp.bfloat16)
    real_piece = coefficient_half[0]
    imag_piece = coefficient_half[1]
    contract = (((0,), (0,)), ((), ()))
    real_real = lax.dot_general(
        real_piece, all_bands[0], contract, preferred_element_type=jnp.float32
    )
    imag_imag = lax.dot_general(
        imag_piece, all_bands[1], contract, preferred_element_type=jnp.float32
    )
    imag_real = lax.dot_general(
        imag_piece, all_bands[0], contract, preferred_element_type=jnp.float32
    )
    real_imag = lax.dot_general(
        real_piece, all_bands[1], contract, preferred_element_type=jnp.float32
    )
    projected = lax.psum_scatter(
        jnp.concatenate(
            [(real_real - imag_imag)[:, None], (imag_real + real_imag)[:, None]], axis=1
        ),
        "band",
        scatter_dimension=0,
        tiled=True,
    )
    own_ratio = lax.dynamic_slice_in_dim(rayleigh, lax.axis_index("band") * blocks, blocks, 0)
    real_correction = (
        damped[0].astype(jnp.float32)
        - own_ratio[:, None] * softened[0].astype(jnp.float32)
        - projected[:, 0]
    )
    imag_correction = (
        damped[1].astype(jnp.float32)
        - own_ratio[:, None] * softened[1].astype(jnp.float32)
        - projected[:, 1]
    )
    correction = jnp.stack([real_correction, imag_correction])
    return (correction, correlation, density)


def solution(mesh):
    placed = (
        P("ens", "band", "pw"),
        P("ens", "band", "pw"),
        P("ens", "pw", None),
        P(("ens", "band"), "pw", None),
        P("pw"),
        P("pw"),
        P(("ens", "band")),
    )
    results = (P("ens", "band", "pw"), P("ens", "band", None), P(("ens", "band"), "pw", None))

    def program(*arguments):
        body = in_waves if fits(arguments[0], arguments[2], mesh) else on_device
        return jax.shard_map(
            body, mesh=mesh, in_specs=placed, out_specs=results, check_vma=False
        )(*arguments)

    return program
```

```python
import functools
import math

import jax
import jax.numpy as jnp
import numpy as np
from jax import lax
from jax.experimental import pallas as pl
from jax.experimental.pallas import tpu as pltpu
from jax.sharding import PartitionSpec as P

EPSILON = 1e-06
HIGHEST = lax.Precision.HIGHEST
BF16 = jnp.bfloat16
F32 = jnp.float32
LANES = 128


def split_pair(values):
    high = values.astype(BF16)
    low = (values - high.astype(np.float64)).astype(BF16)
    return high, low


def wave_tables(devices, rows, width_first, width_second, width_third):
    half = rows // 2
    second = np.arange(width_second)
    steps = np.outer(2 * np.arange(half) + 1, second) % (2 * width_second)
    angles = steps * (math.pi / width_second)
    near = np.concatenate([np.cos(angles), np.sin(angles)])
    blocks = []
    for device in range(devices):
        middle = 2 * rows * device + rows - 1
        turns = (middle * second % (2 * width_second)) * (math.pi / width_second)
        centre = np.stack([np.cos(turns), np.sin(turns)])
        high, low = split_pair(centre)
        blocks.append(np.concatenate([near.astype(BF16), high, low]))
    second_table = np.stack(blocks)
    missing = -second_table.shape[1] % 16
    second_table = np.pad(second_table, ((0, 0), (0, missing), (0, 0)))
    third = np.arange(width_third)
    angles = np.outer(third[: width_third // 2], third) % width_third * (2 * math.pi / width_third)
    factor = 1.0 / math.sqrt(width_second * width_third)
    values = np.concatenate([np.cos(angles), np.sin(angles)]) * factor
    third_table = np.concatenate(split_pair(values), axis=1)
    first = np.arange(width_first)
    angles = (np.outer(first, first) % width_first) * (2 * math.pi / width_first)
    cosines = np.cos(angles) / math.sqrt(width_first)
    sines = np.sin(angles) / math.sqrt(width_first)
    back = np.block([[cosines, -sines], [sines, cosines]]).astype(BF16)
    fore = np.block([[cosines, sines], [-sines, cosines]]).astype(BF16)
    return second_table, third_table, back, fore


def pack_kernel(bands, devices, width_second, width_third, trial_ref, cells_ref, packet_ref):
    cells = cells_ref[...].reshape(1, cells_ref.shape[0])
    first = lax.div(cells, width_second * width_third)
    second = lax.rem(lax.div(cells, width_third), width_second)
    third = lax.rem(cells, width_third)
    unused = jnp.zeros((packet_ref.shape[1] - 2 * bands - 3, cells.shape[1]), jnp.int32)
    place = jnp.concatenate([first, second, third, unused]).astype(F32)
    trial = [trial_ref[part].astype(F32) for part in range(2)]
    packet = jnp.concatenate([*trial, place]).astype(BF16)
    for p in range(devices):
        packet_ref[p] = packet


def grid_kernel(
    bands,
    waves_ref,
    second_ref,
    third_ref,
    back_ref,
    fore_ref,
    potential_in,
    kinetic_ref,
    occupation_ref,
    sent_ref,
    own_out,
    other_out,
    phase_s,
    select_s,
    slab_s,
    acted_s,
    coef_s,
    potential_ref,
    own_ref,
    other_ref,
    done,
):
    devices, _, count = waves_ref.shape
    fetch = pltpu.make_async_copy(potential_in, potential_ref, done.at[2])
    fetch.start()
    rows, width_first, width_third = potential_ref.shape
    slab = width_first // devices
    half = rows // 2
    share = width_first // 2
    me = lax.axis_index("pw")
    low_side = lax.axis_index("band") == 0
    nt = (((1,), (1,)), ((), ()))
    tn = (((0,), (0,)), ((), ()))
    near = second_ref[me]
    fold = width_third // 2
    full = rows * slab
    groups = bands // 2
    low_lanes = lax.broadcasted_iota(jnp.int32, (1, width_third), 1) < fold
    energies = [jnp.zeros((8, width_third), F32) for _ in range(groups)]
    weights = [
        jnp.where(
            low_lanes, occupation_ref[2 * g].astype(F32), occupation_ref[2 * g + 1].astype(F32)
        )
        for g in range(groups)
    ]
    centres = []

    squares = []

    def place(p):
        waves = waves_ref[p].astype(F32)
        place = waves[2 * bands : 2 * bands + 8].astype(jnp.int32)
        first, second, third = place[0:1], place[1:2], place[2:3]
        line = lax.broadcasted_iota(jnp.int32, (LANES, count), 0)
        pick = jnp.where(line == second, 1.0, 0.0).astype(BF16)
        turn = jnp.dot(near, pick, preferred_element_type=F32)
        pick = jnp.where(line == third, 1.0, 0.0).astype(BF16)
        phase_s[p] = jnp.dot(
            third_ref[...], jnp.concatenate([pick, pick]), preferred_element_type=F32
        )
        centre = turn[rows : rows + 2] + turn[rows + 2 : rows + 4]
        centres.append(centre)
        real, imag = waves[:bands], waves[bands : 2 * bands]
        squares.append(real * real + imag * imag)
        turned_real = real * centre[0:1] - imag * centre[1:2]
        turned_imag = real * centre[1:2] + imag * centre[0:1]
        inside = lax.broadcasted_iota(jnp.int32, (slab, count), 0) == first
        sign = jnp.where(lax.rem(third, 2) == 0, 1.0, -1.0)
        near_turn, far_turn = turn[:rows], turn[:rows] * sign
        for k in range(rows):
            at = slice(k * slab, (k + 1) * slab)
            select_s[p, at, :] = jnp.where(inside, near_turn[k : k + 1], 0.0).astype(BF16)
            at = slice(full + k * slab, full + (k + 1) * slab)
            select_s[p, at, :] = jnp.where(inside, far_turn[k : k + 1], 0.0).astype(BF16)
        return turned_real, turned_imag

    def weigh(p, g, turned):
        turned_real, turned_imag = turned
        cosines, sines = phase_s[p, :fold], phase_s[p, fold:]
        slot = (p * groups + g) % 2
        for i, n in enumerate((2 * g, 2 * g + 1)):
            a, b = turned_real[n : n + 1], turned_imag[n : n + 1]
            real_rows = slice(i * fold, (i + 1) * fold)
            imag_rows = slice(width_third + i * fold, width_third + (i + 1) * fold)
            coef_s[slot, real_rows, :] = (a * cosines - b * sines).astype(BF16)
            coef_s[slot, imag_rows, :] = (a * sines + b * cosines).astype(BF16)

    def spread(p, g):
        planes = lax.dot_general(
            select_s[p], coef_s[(p * groups + g) % 2], nt, preferred_element_type=F32
        )
        for h in range(2):
            even = planes[h * full : h * full + full // 2]
            odd = planes[h * full + full // 2 : (h + 1) * full]
            even_real, even_imag = even[:, :width_third], even[:, width_third:]
            odd_real, odd_imag = odd[:, :width_third], odd[:, width_third:]
            plus_real = (even_real - odd_imag).astype(BF16)
            plus_imag = (even_imag + odd_real).astype(BF16)
            minus_real = (even_real + odd_imag).astype(BF16)
            minus_imag = (even_imag - odd_real).astype(BF16)
            real_rows = slice(p * slab, (p + 1) * slab)
            imag_rows = slice(width_first + p * slab, width_first + (p + 1) * slab)
            to = slice((2 * g + h) * width_third, (2 * g + h + 1) * width_third)
            for k in range(half):
                part = slice(k * slab, (k + 1) * slab)
                slab_s[half + k, real_rows, to] = plus_real[part]
                slab_s[half + k, imag_rows, to] = plus_imag[part]
                slab_s[half - 1 - k, real_rows, to] = minus_real[part]
                slab_s[half - 1 - k, imag_rows, to] = minus_imag[part]

    steps = [(p, g) for p in range(devices) for g in range(groups)]
    turned = {0: place(0)}
    weigh(0, 0, turned[0])
    for i, (p, g) in enumerate(steps):
        if g == 0 and p + 1 < devices:
            turned[p + 1] = place(p + 1)
        if i + 1 < len(steps):
            weigh(*steps[i + 1], turned[steps[i + 1][0]])
        spread(p, g)
    square = sum(squares)

    fetch.wait()
    blocks = [slice(h * width_third, (h + 1) * width_third) for h in range(2)]
    for k in range(half):
        densities = [[0.0, 0.0], [0.0, 0.0]]
        locals_ = []
        for row in (half + k, half - 1 - k):
            values = potential_ref[row]
            other = pltpu.roll(values, fold, 1)
            locals_.append(
                (jnp.where(low_lanes, values, other), jnp.where(low_lanes, other, values))
            )
        for g in range(groups):
            at = slice(2 * g * width_third, (2 * g + 2) * width_third)
            results = []
            for side, row in enumerate((half + k, half - 1 - k)):
                spatial = jnp.dot(back_ref[...], slab_s[row, :, at], preferred_element_type=F32)
                moved_real, moved_imag = [], []
                for h in range(2):
                    local = locals_[side][h]
                    real = spatial[:width_first, blocks[h]]
                    imag = spatial[width_first:, blocks[h]]
                    power = real * real + imag * imag
                    densities[side][h] = densities[side][h] + weights[g] * power
                    energy = (power * local).reshape(width_first // 8, 8, width_third)
                    energies[g] = energies[g] + jnp.sum(energy, axis=0)
                    moved_real.append((real * local).astype(BF16))
                    moved_imag.append((imag * local).astype(BF16))
                moved = jnp.concatenate(
                    [jnp.concatenate(moved_real, axis=1), jnp.concatenate(moved_imag, axis=1)]
                )
                results.append(jnp.dot(fore_ref[...], moved, preferred_element_type=F32))
            plus, minus = results
            total = (plus + minus).astype(BF16)
            gap = plus - minus
            gap_real = gap[width_first:].astype(BF16)
            gap_imag = (-gap[:width_first]).astype(BF16)
            to_real = slice(2 * g * width_third, (2 * g + 1) * width_third)
            to_imag = slice((2 * g + 1) * width_third, (2 * g + 2) * width_third)
            for p in range(devices):
                mine = slice(p * slab, (p + 1) * slab)
                mine_imag = slice(width_first + p * slab, width_first + (p + 1) * slab)
                for h in range(2):
                    even_rows = slice(h * full + k * slab, h * full + (k + 1) * slab)
                    start = h * full + full // 2 + k * slab
                    odd_rows = slice(start, start + slab)
                    acted_s[p, even_rows, to_real] = total[mine, blocks[h]]
                    acted_s[p, even_rows, to_imag] = total[mine_imag, blocks[h]]
                    acted_s[p, odd_rows, to_real] = gap_real[mine, blocks[h]]
                    acted_s[p, odd_rows, to_imag] = gap_imag[mine, blocks[h]]
        for side, row in enumerate((half + k, half - 1 - k)):
            folded = [d + pltpu.roll(d, fold, 1) for d in densities[side]]
            density = jnp.where(low_lanes, *folded)
            low, high = density[:share], density[share:]
            own_ref[row] = jnp.where(low_side, low, high)
            other_ref[row] = jnp.where(low_side, high, low).astype(BF16)

    stores = [
        pltpu.make_async_copy(own_ref, own_out, done.at[0]),
        pltpu.make_async_copy(other_ref, other_out, done.at[1]),
    ]
    for store in stores:
        store.start()

    waves = waves_ref[me].astype(F32)
    real, imag = waves[:bands], waves[bands : 2 * bands]
    kinetic = kinetic_ref[...].reshape(1, count)
    moving = jnp.sum((real * real + imag * imag) * kinetic, axis=1, keepdims=True)
    energy = []
    for values in energies:
        for part in (jnp.where(low_lanes, values, 0.0), jnp.where(low_lanes, 0.0, values)):
            energy.append(jnp.sum(part, axis=(0, 1), keepdims=True))
    energy = jnp.concatenate(energy)
    numerator = moving + energy
    denominator = jnp.sum(square, axis=1, keepdims=True) * (1.0 / devices)
    scalars = []
    for value in (numerator, denominator):
        high = value.astype(BF16)
        low = (value - high.astype(F32)).astype(BF16)
        both = jnp.concatenate([high.astype(F32), low.astype(F32)])
        scalars.append(jnp.broadcast_to(both, (2 * bands, LANES)))
    scalars = jnp.concatenate(scalars, axis=1).astype(BF16)

    for p in range(devices):
        cosines, sines = phase_s[p, :fold], phase_s[p, fold:]
        reals, imags = [], []
        for g in range(groups):
            at = slice(2 * g * width_third, 2 * (g + 1) * width_third)
            found = lax.dot_general(acted_s[p, :, at], select_s[p], tn, preferred_element_type=F32)
            for i in range(2):
                real = found[i * fold : (i + 1) * fold]
                imag = found[width_third + i * fold : width_third + (i + 1) * fold]
                reals.append(
                    jnp.sum(real * cosines, axis=0, keepdims=True)
                    + jnp.sum(imag * sines, axis=0, keepdims=True)
                )
                imags.append(
                    jnp.sum(imag * cosines, axis=0, keepdims=True)
                    - jnp.sum(real * sines, axis=0, keepdims=True)
                )
        real, imag = jnp.concatenate(reals), jnp.concatenate(imags)
        cosine, sine = centres[p][0:1], centres[p][1:2]
        result = jnp.concatenate([real * cosine + imag * sine, imag * cosine - real * sine])
        sent_ref[p, :, :count] = result.astype(BF16)
        sent_ref[p, :, count:] = scalars

    for store in stores:
        store.wait()


def on_grid(waves, potential, kinetic, occupation, bands, width_second):
    devices, _, count = waves.shape
    rows, width_first, width_third = potential.shape
    slab = width_first // devices
    tables = wave_tables(devices, rows, width_first, width_second, width_third)
    vmem = pl.BlockSpec(memory_space=pltpu.VMEM)
    smem = pl.BlockSpec(memory_space=pltpu.SMEM)
    anywhere = pl.BlockSpec(memory_space=pl.ANY)
    planes = (rows, width_first // 2, width_third)
    return pl.pallas_call(
        functools.partial(grid_kernel, bands),
        out_shape=(
            jax.ShapeDtypeStruct((devices, 2 * bands, count + 2 * LANES), BF16),
            jax.ShapeDtypeStruct(planes, F32),
            jax.ShapeDtypeStruct(planes, BF16),
        ),
        in_specs=[vmem] * 5 + [anywhere, vmem, smem],
        out_specs=(vmem, anywhere, anywhere),
        scratch_shapes=[
            pltpu.VMEM((devices, width_third, count), F32),
            pltpu.VMEM((devices, 2 * rows * slab, count), BF16),
            pltpu.VMEM((rows, 2 * width_first, bands * width_third), BF16),
            pltpu.VMEM((devices, 2 * rows * slab, bands * width_third), BF16),
            pltpu.VMEM((2, 2 * width_third, count), BF16),
            pltpu.VMEM(potential.shape, F32),
            pltpu.VMEM(planes, F32),
            pltpu.VMEM(planes, BF16),
            pltpu.SemaphoreType.DMA((3,)),
        ],
        compiler_params=pltpu.CompilerParams(vmem_limit_bytes=56 * 1024 * 1024),
    )(waves, *[jnp.asarray(t) for t in tables], potential, kinetic, occupation)


def action_kernel(bands, arrived_ref, trial_ref, kinetic_ref, rows_ref, rest_ref):
    devices = arrived_ref.shape[0]
    count = kinetic_ref.shape[0]
    block = 2 * bands
    total = sum(arrived_ref[p].astype(F32) for p in range(devices))
    applied = total[:, :count]
    scalars = total[:bands, count:] + total[bands:, count:]
    ratio = scalars[:, 0:1] / (scalars[:, LANES : LANES + 1] + EPSILON)
    kinetic = kinetic_ref[...].reshape(1, count)
    damping = 1.0 / (1.0 + kinetic)
    trial = jnp.concatenate([trial_ref[part].astype(F32) for part in range(2)])
    action = kinetic * trial + applied
    damped = (action * damping).astype(BF16).astype(F32)
    soft = (trial * damping).astype(BF16).astype(F32)
    both = jnp.concatenate([ratio, ratio])
    rest_ref[...] = damped - both * soft
    high = ratio.astype(BF16).astype(F32)
    pair = jnp.broadcast_to(jnp.concatenate([high, ratio - high]), (block, LANES))
    unused = jnp.zeros((block, count), F32)
    rows = jnp.concatenate([action, damped, soft, unused])
    tail = jnp.concatenate([pair, pair, pair, pair])
    rows_ref[...] = jnp.concatenate([rows, tail], axis=1).astype(BF16)


def inner_kernel(bands, mine_ref, theirs_ref, all_ref, received_ref, sent_ref, passed_ref):
    count = all_ref.shape[2]
    block = 2 * bands
    first = lax.axis_index("band") == 0
    nt = (((1,), (1,)), ((), ()))
    mine, theirs = mine_ref[...].astype(F32), theirs_ref[...].astype(F32)
    low, high = jnp.where(first, mine, theirs), jnp.where(first, theirs, mine)
    pieces = []
    for at in range(0, 3 * block, bands):
        pieces += [low[at : at + bands], high[at : at + bands]]
    pair = pieces[0][:, count:] + pieces[2][:, count:], pieces[1][:, count:] + pieces[3][:, count:]
    ratio = jnp.concatenate(pair)[:, 0:1]
    rows = jnp.concatenate(pieces)[:, :count].astype(BF16)
    one = lax.dot_general(rows, all_ref[0], nt, preferred_element_type=F32)
    two = lax.dot_general(rows, all_ref[1], nt, preferred_element_type=F32)

    def inner(at):
        real = one[at : at + block] + two[at + block : at + 2 * block]
        imag = one[at + block : at + 2 * block] - two[at : at + block]
        return real, imag

    correlation = inner(0)
    damped = inner(2 * block)
    soft = inner(4 * block)
    coefficients = [d - ratio * s for d, s in zip(damped, soft)]
    sent_ref[...] = jnp.concatenate([*correlation, *coefficients]).astype(BF16)


def project_kernel(bands, parts, *refs):
    terms, (all_ref, rest_ref, _, correlation_ref, own_ref, sent_ref) = refs[:parts], refs[parts:]
    block = 2 * bands
    first = lax.axis_index("band") == 0
    total = sum(term[...].astype(F32) for term in terms)
    correlation_ref[...] = total[: 2 * block]
    coefficients = total[2 * block :].astype(BF16)
    one = jnp.dot(coefficients, all_ref[0], preferred_element_type=F32)
    two = jnp.dot(coefficients, all_ref[1], preferred_element_type=F32)
    real = one[:block] - two[block:]
    imag = one[block:] + two[:block]
    for part, value in enumerate((real, imag)):
        low, high = value[:bands], value[bands:]
        rest = rest_ref[part * bands : (part + 1) * bands]
        own_ref[part] = rest - jnp.where(first, low, high)
        sent_ref[part] = jnp.where(first, high, low)


def swap(values, axis, bit):
    size = lax.axis_size(axis)
    return lax.ppermute(values, axis, [(i, i ^ bit) for i in range(size)])


def in_waves(trial_block, all_bands, potential, rest_density, wave_cells, kinetic, occupation):
    devices = lax.axis_size("pw")
    _, rows, width_third = potential.shape
    width_second = rows * devices
    _, bands, count = trial_block.shape
    states = all_bands.shape[1]
    block = 2 * bands
    vmem = pl.BlockSpec(memory_space=pltpu.VMEM)
    anywhere = pl.BlockSpec(memory_space=pl.ANY)
    params = pltpu.CompilerParams(vmem_limit_bytes=16 * 1024 * 1024)
    packets = pl.pallas_call(
        functools.partial(pack_kernel, bands, devices, width_second, width_third),
        out_shape=jax.ShapeDtypeStruct((devices, 16, count), BF16),
        in_specs=[vmem] * 2,
        out_specs=vmem,
        compiler_params=pltpu.CompilerParams(vmem_limit_bytes=56 * 1024 * 1024),
    )(trial_block, wave_cells)
    waves = lax.all_to_all(packets, "pw", split_axis=0, concat_axis=0, tiled=True)
    partial, density_own, density_other = on_grid(
        waves, potential.transpose(1, 0, 2), kinetic, occupation, bands, width_second
    )
    arrived = lax.all_to_all(partial, "pw", split_axis=0, concat_axis=0, tiled=True)
    received = swap(density_other, "band", 1)
    mine, rest = pl.pallas_call(
        functools.partial(action_kernel, bands),
        out_shape=(
            jax.ShapeDtypeStruct((4 * block, count + LANES), BF16),
            jax.ShapeDtypeStruct((block, count), F32),
        ),
        in_specs=[vmem] * 3,
        out_specs=(vmem, vmem),
        compiler_params=params,
    )(arrived, trial_block, kinetic)
    theirs = swap(mine, "band", 1)
    sums, received = pl.pallas_call(
        functools.partial(inner_kernel, bands),
        out_shape=(
            jax.ShapeDtypeStruct((4 * block, states), BF16),
            jax.ShapeDtypeStruct(received.shape, received.dtype),
        ),
        in_specs=[vmem] * 3 + [anywhere],
        out_specs=(vmem, anywhere),
        input_output_aliases={3: 1},
        compiler_params=params,
    )(mine, theirs, all_bands, received)
    density = rest_density + (density_own + received.astype(F32)).transpose(1, 0, 2)
    near = sums + swap(sums, "pw", 1)
    terms = [near] + [swap(near, "pw", step) for step in range(2, devices, 2)]
    correlation, own, sent = pl.pallas_call(
        functools.partial(project_kernel, bands, len(terms)),
        out_shape=(
            jax.ShapeDtypeStruct((2 * block, states), F32),
            jax.ShapeDtypeStruct((2, bands, count), F32),
            jax.ShapeDtypeStruct((2, bands, count), F32),
        ),
        in_specs=[vmem] * (len(terms) + 2) + [anywhere],
        out_specs=(vmem, vmem, vmem),
        compiler_params=params,
    )(*terms, all_bands, rest, density)
    correction = own - swap(sent, "band", 1)
    correlation = correlation.reshape(2, block, states).transpose(0, 2, 1)
    return (correction, correlation, density)


def fits(trial_block, potential, mesh):
    devices = mesh.shape["pw"]
    width_first, width_second, width_third = potential.shape[0] // mesh.shape["ens"], *potential.shape[1:]
    slab, rows = width_first // devices, width_second // devices
    bands = trial_block.shape[1] // mesh.shape["band"]
    return (
        mesh.shape["band"] == 2
        and devices >= 2
        and devices & (devices - 1) == 0
        and slab % 16 == 0
        and rows % 16 == 0
        and width_first % LANES == 0
        and width_second == LANES
        and width_third == LANES
        and bands == 4
        and trial_block.shape[2] // devices % LANES == 0
    )


def tables(length):
    positions = jnp.arange(length, dtype=jnp.int32)
    products = positions[:, None] * positions[None, :] % length
    angles = products.astype(jnp.float32) * (2.0 * math.pi / length)
    factor = 1.0 / math.sqrt(length)
    cosines = jnp.cos(angles) * factor
    sines = jnp.sin(angles) * factor
    backward = jnp.stack([jnp.stack([cosines, -sines]), jnp.stack([sines, cosines])])
    forward = jnp.stack([jnp.stack([cosines, sines]), jnp.stack([-sines, cosines])])
    return (backward, forward)


def transform(fields, table, formula):
    return jnp.einsum(formula, table, fields, precision=HIGHEST)


def inner(left, right):
    contract = (((1,), (1,)), ((), ()))
    first = lax.dot_general(left[0], right[0], contract, preferred_element_type=jnp.float32)
    second = lax.dot_general(left[1], right[1], contract, preferred_element_type=jnp.float32)
    cross_one = lax.dot_general(left[0], right[1], contract, preferred_element_type=jnp.float32)
    cross_two = lax.dot_general(left[1], right[0], contract, preferred_element_type=jnp.float32)
    return jnp.stack([first + second, cross_one - cross_two])


def on_device(trial_block, all_bands, potential, rest_density, wave_cells, kinetic, occupation):
    devices = lax.axis_size("pw")
    width_first, rows_second, width_third = potential.shape
    width_second = rows_second * devices
    slab_rows = width_first // devices
    blocks = trial_block.shape[1]
    back_first, fore_first = tables(width_first)
    back_second, fore_second = tables(width_second)
    back_third, fore_third = tables(width_third)
    along_third = "pqkc,qnabc->pnabk"
    along_second = "pqkb,qnabc->pnakc"
    along_first = "pqka,qnabc->pnkbc"
    trial_float = trial_block.astype(jnp.float32)
    filled = jnp.zeros((2, blocks, slab_rows * width_second * width_third), jnp.float32)
    filled = filled.at[:, :, wave_cells].set(trial_float)
    filled = filled.reshape(2, blocks, slab_rows, width_second, width_third)
    filled = transform(filled, back_third, along_third)
    filled = transform(filled, back_second, along_second)
    spatial = transform(
        lax.all_to_all(filled, "pw", split_axis=3, concat_axis=2, tiled=True),
        back_first,
        along_first,
    )
    power = spatial[0] * spatial[0] + spatial[1] * spatial[1]
    acted = transform(spatial * potential, fore_first, along_first)
    returned = lax.all_to_all(acted, "pw", split_axis=2, concat_axis=3, tiled=True)
    columns, power = (returned, power[None])
    columns = transform(columns, fore_second, along_second)
    columns = transform(columns, fore_third, along_third)
    applied = columns.reshape(2, blocks, slab_rows * width_second * width_third)[:, :, wave_cells]
    weights = occupation.astype(jnp.float32)
    density_part = jnp.einsum("n,nabc->abc", weights, power[0], precision=HIGHEST)
    summed_density = lax.psum(density_part.astype(jnp.bfloat16), "band").astype(jnp.float32)
    share = width_first // lax.axis_size("band")
    block_density = lax.dynamic_slice_in_dim(
        summed_density, lax.axis_index("band") * share, share, 0
    )
    density = rest_density + block_density
    action = kinetic * trial_float + applied
    damping = 1.0 / (1.0 + kinetic)
    action_half = action.astype(jnp.bfloat16)
    damped = (action * damping).astype(jnp.bfloat16)
    softened = (trial_float * damping).astype(jnp.bfloat16)
    every_trial, every_action, every_damped, every_softened = (
        lax.all_gather(trial_block, "band", axis=1, tiled=True),
        lax.all_gather(action_half, "band", axis=1, tiled=True),
        lax.all_gather(damped, "band", axis=1, tiled=True),
        lax.all_gather(softened, "band", axis=1, tiled=True),
    )
    trial_wide = every_trial.astype(jnp.float32)
    numerator = jnp.sum(trial_wide * every_action.astype(jnp.float32), axis=(0, 2))
    denominator = jnp.sum(trial_wide * trial_wide, axis=(0, 2))
    correlation = inner(all_bands, every_action)
    correlation, numerator, denominator = lax.psum((correlation, numerator, denominator), "pw")
    rayleigh = numerator / (denominator + EPSILON)
    local_terms = inner(all_bands, every_damped) - rayleigh * inner(all_bands, every_softened)
    coefficients = lax.psum(local_terms, "pw")
    coefficient_half = coefficients.astype(jnp.bfloat16)
    real_piece = coefficient_half[0]
    imag_piece = coefficient_half[1]
    contract = (((0,), (0,)), ((), ()))
    real_real = lax.dot_general(
        real_piece, all_bands[0], contract, preferred_element_type=jnp.float32
    )
    imag_imag = lax.dot_general(
        imag_piece, all_bands[1], contract, preferred_element_type=jnp.float32
    )
    imag_real = lax.dot_general(
        imag_piece, all_bands[0], contract, preferred_element_type=jnp.float32
    )
    real_imag = lax.dot_general(
        real_piece, all_bands[1], contract, preferred_element_type=jnp.float32
    )
    projected = lax.psum_scatter(
        jnp.concatenate(
            [(real_real - imag_imag)[:, None], (imag_real + real_imag)[:, None]], axis=1
        ),
        "band",
        scatter_dimension=0,
        tiled=True,
    )
    own_ratio = lax.dynamic_slice_in_dim(rayleigh, lax.axis_index("band") * blocks, blocks, 0)
    real_correction = (
        damped[0].astype(jnp.float32)
        - own_ratio[:, None] * softened[0].astype(jnp.float32)
        - projected[:, 0]
    )
    imag_correction = (
        damped[1].astype(jnp.float32)
        - own_ratio[:, None] * softened[1].astype(jnp.float32)
        - projected[:, 1]
    )
    correction = jnp.stack([real_correction, imag_correction])
    return (correction, correlation, density)


def solution(mesh):
    placed = (
        P("ens", "band", "pw"),
        P("ens", "band", "pw"),
        P("ens", "pw", None),
        P(("ens", "band"), "pw", None),
        P("pw"),
        P("pw"),
        P(("ens", "band")),
    )
    results = (P("ens", "band", "pw"), P("ens", "band", None), P(("ens", "band"), "pw", None))

    def program(*arguments):
        body = in_waves if fits(arguments[0], arguments[2], mesh) else on_device
        return jax.shard_map(
            body, mesh=mesh, in_specs=placed, out_specs=results, check_vma=False
        )(*arguments)

    return program
```

```python
import functools
import math

import jax
import jax.numpy as jnp
import numpy as np
from jax import lax
from jax.experimental import pallas as pl
from jax.experimental.pallas import tpu as pltpu
from jax.sharding import PartitionSpec as P

EPSILON = 1e-06
HIGHEST = lax.Precision.HIGHEST
BF16 = jnp.bfloat16
F32 = jnp.float32
LANES = 128


def split_pair(values):
    high = values.astype(BF16)
    low = (values - high.astype(np.float64)).astype(BF16)
    return high, low


def wave_tables(devices, rows, width_first, width_second, width_third):
    half = rows // 2
    second = np.arange(width_second)
    steps = np.outer(2 * np.arange(half) + 1, second) % (2 * width_second)
    angles = steps * (math.pi / width_second)
    near = np.concatenate([np.cos(angles), np.sin(angles)])
    blocks = []
    for device in range(devices):
        middle = 2 * rows * device + rows - 1
        turns = (middle * second % (2 * width_second)) * (math.pi / width_second)
        centre = np.stack([np.cos(turns), np.sin(turns)])
        high, low = split_pair(centre)
        blocks.append(np.concatenate([near.astype(BF16), high, low]))
    second_table = np.stack(blocks)
    missing = -second_table.shape[1] % 16
    second_table = np.pad(second_table, ((0, 0), (0, missing), (0, 0)))
    third = np.arange(width_third)
    angles = np.outer(third[: width_third // 2], third) % width_third * (2 * math.pi / width_third)
    factor = 1.0 / math.sqrt(width_second * width_third)
    values = np.concatenate([np.cos(angles), np.sin(angles)]) * factor
    third_table = np.concatenate(split_pair(values), axis=1)
    first = np.arange(width_first)
    angles = (np.outer(first, first) % width_first) * (2 * math.pi / width_first)
    cosines = np.cos(angles) / math.sqrt(width_first)
    sines = np.sin(angles) / math.sqrt(width_first)
    back = np.block([[cosines, -sines], [sines, cosines]]).astype(BF16)
    fore = np.block([[cosines, sines], [-sines, cosines]]).astype(BF16)
    return second_table, third_table, back, fore


def pack_kernel(bands, devices, width_second, width_third, trial_ref, cells_ref, packet_ref):
    cells = cells_ref[...].reshape(1, cells_ref.shape[0])
    first = lax.div(cells, width_second * width_third)
    second = lax.rem(lax.div(cells, width_third), width_second)
    third = lax.rem(cells, width_third)
    middle = cells.shape[1] // 2
    halves = [part for row in (first, second, third) for part in (row[:, :middle], row[:, middle:])]
    unused = jnp.zeros((2 * bands - 6, middle), jnp.int32)
    place = jnp.concatenate([*halves, unused]).astype(F32)
    trial = jnp.concatenate([trial_ref[part].astype(F32) for part in range(2)])
    packet = jnp.concatenate([trial, place], axis=1).astype(BF16)
    for p in range(devices):
        packet_ref[p] = packet


def grid_kernel(
    bands,
    waves_ref,
    second_ref,
    third_ref,
    back_ref,
    fore_ref,
    potential_in,
    kinetic_ref,
    occupation_ref,
    sent_ref,
    own_out,
    other_out,
    phase_s,
    select_s,
    slab_s,
    acted_s,
    coef_s,
    potential_ref,
    own_ref,
    other_ref,
    done,
):
    devices, _, length = waves_ref.shape
    count = 2 * length // 3
    fetch = pltpu.make_async_copy(potential_in, potential_ref, done.at[2])
    fetch.start()
    rows, width_first, width_third = potential_ref.shape
    slab = width_first // devices
    half = rows // 2
    share = width_first // 2
    me = lax.axis_index("pw")
    low_side = lax.axis_index("band") == 0
    nt = (((1,), (1,)), ((), ()))
    tn = (((0,), (0,)), ((), ()))
    near = second_ref[me]
    fold = width_third // 2
    full = rows * slab
    groups = bands // 2
    low_lanes = lax.broadcasted_iota(jnp.int32, (1, width_third), 1) < fold
    energies = [jnp.zeros((8, width_third), F32) for _ in range(groups)]
    weights = [
        jnp.where(
            low_lanes, occupation_ref[2 * g].astype(F32), occupation_ref[2 * g + 1].astype(F32)
        )
        for g in range(groups)
    ]
    centres = []

    squares = []

    zero, one = jnp.zeros((), BF16), jnp.ones((), BF16)
    line = lax.broadcasted_iota(jnp.int32, (slab, count), 0).astype(F32).astype(BF16)

    def level(row):
        return jnp.broadcast_to(row, (slab, count)).astype(BF16)

    def one_hot(row):
        target = level(row)
        tiles = [line + jnp.asarray(at, BF16) == target for at in range(0, LANES, slab)]
        return jnp.concatenate([jnp.where(tile, one, zero) for tile in tiles])

    def place(p):
        waves = waves_ref[p].astype(F32)
        first, second, third = [
            jnp.concatenate([waves[i : i + 1, count:], waves[i + 1 : i + 2, count:]], axis=1)
            for i in (0, 2, 4)
        ]
        turn = jnp.dot(near, one_hot(second), preferred_element_type=F32)
        pick = one_hot(third)
        phase_s[p] = jnp.dot(
            third_ref[...], jnp.concatenate([pick, pick]), preferred_element_type=F32
        )
        centre = turn[rows : rows + 2] + turn[rows + 2 : rows + 4]
        centres.append(centre)
        real, imag = waves[:bands, :count], waves[bands:, :count]
        squares.append(real * real + imag * imag)
        turned_real = real * centre[0:1] - imag * centre[1:2]
        turned_imag = real * centre[1:2] + imag * centre[0:1]
        inside = line == level(first)
        sign = level(jnp.where(lax.rem(third.astype(jnp.int32), 2) == 0, 1.0, -1.0))
        for k in range(rows):
            chosen = jnp.where(inside, level(turn[k : k + 1]), zero)
            select_s[p, k * slab : (k + 1) * slab, :] = chosen
            select_s[p, full + k * slab : full + (k + 1) * slab, :] = chosen * sign
        return turned_real, turned_imag

    def weigh(p, g, turned):
        turned_real, turned_imag = turned
        cosines, sines = phase_s[p, :fold], phase_s[p, fold:]
        slot = (p * groups + g) % 2
        for i, n in enumerate((2 * g, 2 * g + 1)):
            a, b = turned_real[n : n + 1], turned_imag[n : n + 1]
            real_rows = slice(i * fold, (i + 1) * fold)
            imag_rows = slice(width_third + i * fold, width_third + (i + 1) * fold)
            coef_s[slot, real_rows, :] = (a * cosines - b * sines).astype(BF16)
            coef_s[slot, imag_rows, :] = (a * sines + b * cosines).astype(BF16)

    def spread(p, g):
        planes = lax.dot_general(
            select_s[p], coef_s[(p * groups + g) % 2], nt, preferred_element_type=F32
        )
        for h in range(2):
            even = planes[h * full : h * full + full // 2]
            odd = planes[h * full + full // 2 : (h + 1) * full]
            even_real, even_imag = even[:, :width_third], even[:, width_third:]
            odd_real, odd_imag = odd[:, :width_third], odd[:, width_third:]
            plus_real = (even_real - odd_imag).astype(BF16)
            plus_imag = (even_imag + odd_real).astype(BF16)
            minus_real = (even_real + odd_imag).astype(BF16)
            minus_imag = (even_imag - odd_real).astype(BF16)
            real_rows = slice(p * slab, (p + 1) * slab)
            imag_rows = slice(width_first + p * slab, width_first + (p + 1) * slab)
            to = slice((2 * g + h) * width_third, (2 * g + h + 1) * width_third)
            for k in range(half):
                part = slice(k * slab, (k + 1) * slab)
                slab_s[half + k, real_rows, to] = plus_real[part]
                slab_s[half + k, imag_rows, to] = plus_imag[part]
                slab_s[half - 1 - k, real_rows, to] = minus_real[part]
                slab_s[half - 1 - k, imag_rows, to] = minus_imag[part]

    steps = [(p, g) for p in range(devices) for g in range(groups)]
    turned = {0: place(0)}
    weigh(0, 0, turned[0])
    for i, (p, g) in enumerate(steps):
        if g == 0 and p + 1 < devices:
            turned[p + 1] = place(p + 1)
        if i + 1 < len(steps):
            weigh(*steps[i + 1], turned[steps[i + 1][0]])
        spread(p, g)
    square = sum(squares)

    fetch.wait()
    blocks = [slice(h * width_third, (h + 1) * width_third) for h in range(2)]
    for k in range(half):
        densities = [[0.0, 0.0], [0.0, 0.0]]
        locals_ = []
        for row in (half + k, half - 1 - k):
            values = potential_ref[row]
            other = pltpu.roll(values, fold, 1)
            locals_.append(
                (jnp.where(low_lanes, values, other), jnp.where(low_lanes, other, values))
            )
        for g in range(groups):
            at = slice(2 * g * width_third, (2 * g + 2) * width_third)
            results = []
            for side, row in enumerate((half + k, half - 1 - k)):
                spatial = jnp.dot(back_ref[...], slab_s[row, :, at], preferred_element_type=F32)
                moved_real, moved_imag = [], []
                for h in range(2):
                    local = locals_[side][h]
                    real = spatial[:width_first, blocks[h]]
                    imag = spatial[width_first:, blocks[h]]
                    power = real * real + imag * imag
                    densities[side][h] = densities[side][h] + weights[g] * power
                    energy = (power * local).reshape(width_first // 8, 8, width_third)
                    energies[g] = energies[g] + jnp.sum(energy, axis=0)
                    moved_real.append((real * local).astype(BF16))
                    moved_imag.append((imag * local).astype(BF16))
                moved = jnp.concatenate(
                    [jnp.concatenate(moved_real, axis=1), jnp.concatenate(moved_imag, axis=1)]
                )
                results.append(jnp.dot(fore_ref[...], moved, preferred_element_type=F32))
            plus, minus = results
            total = (plus + minus).astype(BF16)
            gap = plus - minus
            gap_real = gap[width_first:].astype(BF16)
            gap_imag = (-gap[:width_first]).astype(BF16)
            to_real = slice(2 * g * width_third, (2 * g + 1) * width_third)
            to_imag = slice((2 * g + 1) * width_third, (2 * g + 2) * width_third)
            for p in range(devices):
                mine = slice(p * slab, (p + 1) * slab)
                mine_imag = slice(width_first + p * slab, width_first + (p + 1) * slab)
                for h in range(2):
                    even_rows = slice(h * full + k * slab, h * full + (k + 1) * slab)
                    start = h * full + full // 2 + k * slab
                    odd_rows = slice(start, start + slab)
                    acted_s[p, even_rows, to_real] = total[mine, blocks[h]]
                    acted_s[p, even_rows, to_imag] = total[mine_imag, blocks[h]]
                    acted_s[p, odd_rows, to_real] = gap_real[mine, blocks[h]]
                    acted_s[p, odd_rows, to_imag] = gap_imag[mine, blocks[h]]
        for side, row in enumerate((half + k, half - 1 - k)):
            folded = [d + pltpu.roll(d, fold, 1) for d in densities[side]]
            density = jnp.where(low_lanes, *folded)
            low, high = density[:share], density[share:]
            own_ref[row] = jnp.where(low_side, low, high)
            other_ref[row] = jnp.where(low_side, high, low).astype(BF16)

    stores = [
        pltpu.make_async_copy(own_ref, own_out, done.at[0]),
        pltpu.make_async_copy(other_ref, other_out, done.at[1]),
    ]
    for store in stores:
        store.start()

    waves = waves_ref[me].astype(F32)
    real, imag = waves[:bands, :count], waves[bands:, :count]
    kinetic = kinetic_ref[...].reshape(1, count)
    moving = jnp.sum((real * real + imag * imag) * kinetic, axis=1, keepdims=True)
    energy = []
    for values in energies:
        for part in (jnp.where(low_lanes, values, 0.0), jnp.where(low_lanes, 0.0, values)):
            energy.append(jnp.sum(part, axis=(0, 1), keepdims=True))
    energy = jnp.concatenate(energy)
    numerator = moving + energy
    denominator = jnp.sum(square, axis=1, keepdims=True) * (1.0 / devices)
    scalars = []
    for value in (numerator, denominator):
        high = value.astype(BF16)
        low = (value - high.astype(F32)).astype(BF16)
        both = jnp.concatenate([high.astype(F32), low.astype(F32)])
        scalars.append(jnp.broadcast_to(both, (2 * bands, LANES)))
    scalars = jnp.where(low_lanes, *scalars).astype(BF16)

    for p in range(devices):
        cosines, sines = phase_s[p, :fold], phase_s[p, fold:]
        reals, imags = [], []
        for g in range(groups):
            at = slice(2 * g * width_third, 2 * (g + 1) * width_third)
            found = lax.dot_general(acted_s[p, :, at], select_s[p], tn, preferred_element_type=F32)
            for i in range(2):
                real = found[i * fold : (i + 1) * fold]
                imag = found[width_third + i * fold : width_third + (i + 1) * fold]
                reals.append(
                    jnp.sum(real * cosines, axis=0, keepdims=True)
                    + jnp.sum(imag * sines, axis=0, keepdims=True)
                )
                imags.append(
                    jnp.sum(imag * cosines, axis=0, keepdims=True)
                    - jnp.sum(real * sines, axis=0, keepdims=True)
                )
        real, imag = jnp.concatenate(reals), jnp.concatenate(imags)
        cosine, sine = centres[p][0:1], centres[p][1:2]
        result = jnp.concatenate([real * cosine + imag * sine, imag * cosine - real * sine])
        sent_ref[p, :, :count] = result.astype(BF16)
        sent_ref[p, :, count : count + LANES] = scalars
        sent_ref[p, :, count + LANES :] = jnp.zeros_like(scalars)

    for store in stores:
        store.wait()


def on_grid(waves, potential, kinetic, occupation, bands, width_second):
    devices, _, length = waves.shape
    count = 2 * length // 3
    rows, width_first, width_third = potential.shape
    slab = width_first // devices
    tables = wave_tables(devices, rows, width_first, width_second, width_third)
    vmem = pl.BlockSpec(memory_space=pltpu.VMEM)
    smem = pl.BlockSpec(memory_space=pltpu.SMEM)
    anywhere = pl.BlockSpec(memory_space=pl.ANY)
    planes = (rows, width_first // 2, width_third)
    return pl.pallas_call(
        functools.partial(grid_kernel, bands),
        out_shape=(
            jax.ShapeDtypeStruct((devices, 2 * bands, count + 2 * LANES), BF16),
            jax.ShapeDtypeStruct(planes, F32),
            jax.ShapeDtypeStruct(planes, BF16),
        ),
        in_specs=[vmem] * 5 + [anywhere, vmem, smem],
        out_specs=(vmem, anywhere, anywhere),
        scratch_shapes=[
            pltpu.VMEM((devices, width_third, count), F32),
            pltpu.VMEM((devices, 2 * rows * slab, count), BF16),
            pltpu.VMEM((rows, 2 * width_first, bands * width_third), BF16),
            pltpu.VMEM((devices, 2 * rows * slab, bands * width_third), BF16),
            pltpu.VMEM((2, 2 * width_third, count), BF16),
            pltpu.VMEM(potential.shape, F32),
            pltpu.VMEM(planes, F32),
            pltpu.VMEM(planes, BF16),
            pltpu.SemaphoreType.DMA((3,)),
        ],
        compiler_params=pltpu.CompilerParams(vmem_limit_bytes=56 * 1024 * 1024),
    )(waves, *[jnp.asarray(t) for t in tables], potential, kinetic, occupation)


def action_kernel(bands, arrived_ref, trial_ref, kinetic_ref, rows_ref, rest_ref):
    devices = arrived_ref.shape[0]
    count = kinetic_ref.shape[0]
    block = 2 * bands
    total = sum(arrived_ref[p].astype(F32) for p in range(devices))
    applied = total[:, :count]
    scalars = total[:bands, count:] + total[bands:, count:]
    ratio = scalars[:, 0:1] / (scalars[:, LANES // 2 : LANES // 2 + 1] + EPSILON)
    kinetic = kinetic_ref[...].reshape(1, count)
    damping = 1.0 / (1.0 + kinetic)
    trial = jnp.concatenate([trial_ref[part].astype(F32) for part in range(2)])
    action = kinetic * trial + applied
    damped = (action * damping).astype(BF16).astype(F32)
    soft = (trial * damping).astype(BF16).astype(F32)
    both = jnp.concatenate([ratio, ratio])
    rest_ref[...] = damped - both * soft
    high = ratio.astype(BF16).astype(F32)
    pair = jnp.broadcast_to(jnp.concatenate([high, ratio - high]), (block, LANES))
    unused = jnp.zeros((block, count), F32)
    rows = jnp.concatenate([action, damped, soft, unused])
    tail = jnp.concatenate([pair, pair, pair, pair])
    rows_ref[...] = jnp.concatenate([rows, tail], axis=1).astype(BF16)


def inner_kernel(bands, mine_ref, theirs_ref, all_ref, received_ref, sent_ref, passed_ref):
    count = all_ref.shape[2]
    block = 2 * bands
    first = lax.axis_index("band") == 0
    nt = (((1,), (1,)), ((), ()))
    mine, theirs = mine_ref[...].astype(F32), theirs_ref[...].astype(F32)
    low, high = jnp.where(first, mine, theirs), jnp.where(first, theirs, mine)
    pieces = []
    for at in range(0, 3 * block, bands):
        pieces += [low[at : at + bands], high[at : at + bands]]
    pair = pieces[0][:, count:] + pieces[2][:, count:], pieces[1][:, count:] + pieces[3][:, count:]
    ratio = jnp.concatenate(pair)[:, 0:1]
    rows = jnp.concatenate(pieces)[:, :count].astype(BF16)
    one = lax.dot_general(rows, all_ref[0], nt, preferred_element_type=F32)
    two = lax.dot_general(rows, all_ref[1], nt, preferred_element_type=F32)

    def inner(at):
        real = one[at : at + block] + two[at + block : at + 2 * block]
        imag = one[at + block : at + 2 * block] - two[at : at + block]
        return real, imag

    correlation = inner(0)
    damped = inner(2 * block)
    soft = inner(4 * block)
    coefficients = [d - ratio * s for d, s in zip(damped, soft)]
    sent_ref[...] = jnp.concatenate([*correlation, *coefficients]).astype(BF16)


def project_kernel(bands, parts, *refs):
    terms, (all_ref, rest_ref, _, correlation_ref, own_ref, sent_ref) = refs[:parts], refs[parts:]
    block = 2 * bands
    first = lax.axis_index("band") == 0
    total = sum(term[...].astype(F32) for term in terms)
    correlation_ref[...] = total[: 2 * block]
    coefficients = total[2 * block :].astype(BF16)
    one = jnp.dot(coefficients, all_ref[0], preferred_element_type=F32)
    two = jnp.dot(coefficients, all_ref[1], preferred_element_type=F32)
    real = one[:block] - two[block:]
    imag = one[block:] + two[:block]
    for part, value in enumerate((real, imag)):
        low, high = value[:bands], value[bands:]
        rest = rest_ref[part * bands : (part + 1) * bands]
        own_ref[part] = rest - jnp.where(first, low, high)
        sent_ref[part] = jnp.where(first, high, low)


def swap(values, axis, bit):
    size = lax.axis_size(axis)
    return lax.ppermute(values, axis, [(i, i ^ bit) for i in range(size)])


def in_waves(trial_block, all_bands, potential, rest_density, wave_cells, kinetic, occupation):
    devices = lax.axis_size("pw")
    _, rows, width_third = potential.shape
    width_second = rows * devices
    _, bands, count = trial_block.shape
    states = all_bands.shape[1]
    block = 2 * bands
    vmem = pl.BlockSpec(memory_space=pltpu.VMEM)
    anywhere = pl.BlockSpec(memory_space=pl.ANY)
    params = pltpu.CompilerParams(vmem_limit_bytes=16 * 1024 * 1024)
    packets = pl.pallas_call(
        functools.partial(pack_kernel, bands, devices, width_second, width_third),
        out_shape=jax.ShapeDtypeStruct((devices, block, 3 * count // 2), BF16),
        in_specs=[vmem] * 2,
        out_specs=vmem,
        compiler_params=pltpu.CompilerParams(vmem_limit_bytes=56 * 1024 * 1024),
    )(trial_block, wave_cells)
    waves = lax.all_to_all(packets, "pw", split_axis=0, concat_axis=0, tiled=True)
    partial, density_own, density_other = on_grid(
        waves, potential.transpose(1, 0, 2), kinetic, occupation, bands, width_second
    )
    arrived = lax.all_to_all(partial, "pw", split_axis=0, concat_axis=0, tiled=True)
    received = swap(density_other, "band", 1)
    mine, rest = pl.pallas_call(
        functools.partial(action_kernel, bands),
        out_shape=(
            jax.ShapeDtypeStruct((4 * block, count + LANES), BF16),
            jax.ShapeDtypeStruct((block, count), F32),
        ),
        in_specs=[vmem] * 3,
        out_specs=(vmem, vmem),
        compiler_params=params,
    )(arrived, trial_block, kinetic)
    theirs = swap(mine, "band", 1)
    sums, received = pl.pallas_call(
        functools.partial(inner_kernel, bands),
        out_shape=(
            jax.ShapeDtypeStruct((4 * block, states), BF16),
            jax.ShapeDtypeStruct(received.shape, received.dtype),
        ),
        in_specs=[vmem] * 3 + [anywhere],
        out_specs=(vmem, anywhere),
        input_output_aliases={3: 1},
        compiler_params=params,
    )(mine, theirs, all_bands, received)
    density = rest_density + (density_own + received.astype(F32)).transpose(1, 0, 2)
    near = sums + swap(sums, "pw", 1)
    terms = [near] + [swap(near, "pw", step) for step in range(2, devices, 2)]
    correlation, own, sent = pl.pallas_call(
        functools.partial(project_kernel, bands, len(terms)),
        out_shape=(
            jax.ShapeDtypeStruct((2 * block, states), F32),
            jax.ShapeDtypeStruct((2, bands, count), F32),
            jax.ShapeDtypeStruct((2, bands, count), F32),
        ),
        in_specs=[vmem] * (len(terms) + 2) + [anywhere],
        out_specs=(vmem, vmem, vmem),
        compiler_params=params,
    )(*terms, all_bands, rest, density)
    correction = own - swap(sent, "band", 1)
    correlation = correlation.reshape(2, block, states).transpose(0, 2, 1)
    return (correction, correlation, density)


def fits(trial_block, potential, mesh):
    devices = mesh.shape["pw"]
    width_first, width_second, width_third = potential.shape[0] // mesh.shape["ens"], *potential.shape[1:]
    slab, rows = width_first // devices, width_second // devices
    bands = trial_block.shape[1] // mesh.shape["band"]
    return (
        mesh.shape["band"] == 2
        and devices >= 2
        and devices & (devices - 1) == 0
        and slab % 16 == 0
        and rows % 16 == 0
        and width_first % LANES == 0
        and width_second == LANES
        and width_third == LANES
        and bands == 4
        and trial_block.shape[2] // devices % (2 * LANES) == 0
    )


def tables(length):
    positions = jnp.arange(length, dtype=jnp.int32)
    products = positions[:, None] * positions[None, :] % length
    angles = products.astype(jnp.float32) * (2.0 * math.pi / length)
    factor = 1.0 / math.sqrt(length)
    cosines = jnp.cos(angles) * factor
    sines = jnp.sin(angles) * factor
    backward = jnp.stack([jnp.stack([cosines, -sines]), jnp.stack([sines, cosines])])
    forward = jnp.stack([jnp.stack([cosines, sines]), jnp.stack([-sines, cosines])])
    return (backward, forward)


def transform(fields, table, formula):
    return jnp.einsum(formula, table, fields, precision=HIGHEST)


def inner(left, right):
    contract = (((1,), (1,)), ((), ()))
    first = lax.dot_general(left[0], right[0], contract, preferred_element_type=jnp.float32)
    second = lax.dot_general(left[1], right[1], contract, preferred_element_type=jnp.float32)
    cross_one = lax.dot_general(left[0], right[1], contract, preferred_element_type=jnp.float32)
    cross_two = lax.dot_general(left[1], right[0], contract, preferred_element_type=jnp.float32)
    return jnp.stack([first + second, cross_one - cross_two])


def on_device(trial_block, all_bands, potential, rest_density, wave_cells, kinetic, occupation):
    devices = lax.axis_size("pw")
    width_first, rows_second, width_third = potential.shape
    width_second = rows_second * devices
    slab_rows = width_first // devices
    blocks = trial_block.shape[1]
    back_first, fore_first = tables(width_first)
    back_second, fore_second = tables(width_second)
    back_third, fore_third = tables(width_third)
    along_third = "pqkc,qnabc->pnabk"
    along_second = "pqkb,qnabc->pnakc"
    along_first = "pqka,qnabc->pnkbc"
    trial_float = trial_block.astype(jnp.float32)
    filled = jnp.zeros((2, blocks, slab_rows * width_second * width_third), jnp.float32)
    filled = filled.at[:, :, wave_cells].set(trial_float)
    filled = filled.reshape(2, blocks, slab_rows, width_second, width_third)
    filled = transform(filled, back_third, along_third)
    filled = transform(filled, back_second, along_second)
    spatial = transform(
        lax.all_to_all(filled, "pw", split_axis=3, concat_axis=2, tiled=True),
        back_first,
        along_first,
    )
    power = spatial[0] * spatial[0] + spatial[1] * spatial[1]
    acted = transform(spatial * potential, fore_first, along_first)
    returned = lax.all_to_all(acted, "pw", split_axis=2, concat_axis=3, tiled=True)
    columns, power = (returned, power[None])
    columns = transform(columns, fore_second, along_second)
    columns = transform(columns, fore_third, along_third)
    applied = columns.reshape(2, blocks, slab_rows * width_second * width_third)[:, :, wave_cells]
    weights = occupation.astype(jnp.float32)
    density_part = jnp.einsum("n,nabc->abc", weights, power[0], precision=HIGHEST)
    summed_density = lax.psum(density_part.astype(jnp.bfloat16), "band").astype(jnp.float32)
    share = width_first // lax.axis_size("band")
    block_density = lax.dynamic_slice_in_dim(
        summed_density, lax.axis_index("band") * share, share, 0
    )
    density = rest_density + block_density
    action = kinetic * trial_float + applied
    damping = 1.0 / (1.0 + kinetic)
    action_half = action.astype(jnp.bfloat16)
    damped = (action * damping).astype(jnp.bfloat16)
    softened = (trial_float * damping).astype(jnp.bfloat16)
    every_trial, every_action, every_damped, every_softened = (
        lax.all_gather(trial_block, "band", axis=1, tiled=True),
        lax.all_gather(action_half, "band", axis=1, tiled=True),
        lax.all_gather(damped, "band", axis=1, tiled=True),
        lax.all_gather(softened, "band", axis=1, tiled=True),
    )
    trial_wide = every_trial.astype(jnp.float32)
    numerator = jnp.sum(trial_wide * every_action.astype(jnp.float32), axis=(0, 2))
    denominator = jnp.sum(trial_wide * trial_wide, axis=(0, 2))
    correlation = inner(all_bands, every_action)
    correlation, numerator, denominator = lax.psum((correlation, numerator, denominator), "pw")
    rayleigh = numerator / (denominator + EPSILON)
    local_terms = inner(all_bands, every_damped) - rayleigh * inner(all_bands, every_softened)
    coefficients = lax.psum(local_terms, "pw")
    coefficient_half = coefficients.astype(jnp.bfloat16)
    real_piece = coefficient_half[0]
    imag_piece = coefficient_half[1]
    contract = (((0,), (0,)), ((), ()))
    real_real = lax.dot_general(
        real_piece, all_bands[0], contract, preferred_element_type=jnp.float32
    )
    imag_imag = lax.dot_general(
        imag_piece, all_bands[1], contract, preferred_element_type=jnp.float32
    )
    imag_real = lax.dot_general(
        imag_piece, all_bands[0], contract, preferred_element_type=jnp.float32
    )
    real_imag = lax.dot_general(
        real_piece, all_bands[1], contract, preferred_element_type=jnp.float32
    )
    projected = lax.psum_scatter(
        jnp.concatenate(
            [(real_real - imag_imag)[:, None], (imag_real + real_imag)[:, None]], axis=1
        ),
        "band",
        scatter_dimension=0,
        tiled=True,
    )
    own_ratio = lax.dynamic_slice_in_dim(rayleigh, lax.axis_index("band") * blocks, blocks, 0)
    real_correction = (
        damped[0].astype(jnp.float32)
        - own_ratio[:, None] * softened[0].astype(jnp.float32)
        - projected[:, 0]
    )
    imag_correction = (
        damped[1].astype(jnp.float32)
        - own_ratio[:, None] * softened[1].astype(jnp.float32)
        - projected[:, 1]
    )
    correction = jnp.stack([real_correction, imag_correction])
    return (correction, correlation, density)


def solution(mesh):
    placed = (
        P("ens", "band", "pw"),
        P("ens", "band", "pw"),
        P("ens", "pw", None),
        P(("ens", "band"), "pw", None),
        P("pw"),
        P("pw"),
        P(("ens", "band")),
    )
    results = (P("ens", "band", "pw"), P("ens", "band", None), P(("ens", "band"), "pw", None))

    def program(*arguments):
        body = in_waves if fits(arguments[0], arguments[2], mesh) else on_device
        return jax.shard_map(
            body, mesh=mesh, in_specs=placed, out_specs=results, check_vma=False
        )(*arguments)

    return program
```

```python
import functools
import math

import jax
import jax.numpy as jnp
import numpy as np
from jax import lax
from jax.experimental import pallas as pl
from jax.experimental.pallas import tpu as pltpu
from jax.sharding import PartitionSpec as P

EPSILON = 1e-06
HIGHEST = lax.Precision.HIGHEST
BF16 = jnp.bfloat16
F32 = jnp.float32
LANES = 128


def split_pair(values):
    high = values.astype(BF16)
    low = (values - high.astype(np.float64)).astype(BF16)
    return high, low


def wave_tables(devices, rows, width_first, width_second, width_third):
    half = rows // 2
    second = np.arange(width_second)
    steps = np.outer(2 * np.arange(half) + 1, second) % (2 * width_second)
    angles = steps * (math.pi / width_second)
    near = np.concatenate([np.cos(angles), np.sin(angles)])
    blocks = []
    for device in range(devices):
        middle = 2 * rows * device + rows - 1
        turns = (middle * second % (2 * width_second)) * (math.pi / width_second)
        centre = np.stack([np.cos(turns), np.sin(turns)])
        high, low = split_pair(centre)
        blocks.append(np.concatenate([near.astype(BF16), high, low]))
    second_table = np.stack(blocks)
    missing = -second_table.shape[1] % 16
    second_table = np.pad(second_table, ((0, 0), (0, missing), (0, 0)))
    third = np.arange(width_third)
    angles = np.outer(third[: width_third // 2], third) % width_third * (2 * math.pi / width_third)
    factor = 1.0 / math.sqrt(width_second * width_third)
    values = np.concatenate([np.cos(angles), np.sin(angles)]) * factor
    third_table = np.concatenate(split_pair(values), axis=1)
    first = np.arange(width_first)
    angles = (np.outer(first, first) % width_first) * (2 * math.pi / width_first)
    cosines = np.cos(angles) / math.sqrt(width_first)
    sines = np.sin(angles) / math.sqrt(width_first)
    back = np.block([[cosines, -sines], [sines, cosines]]).astype(BF16)
    fore = np.block([[cosines, sines], [-sines, cosines]]).astype(BF16)
    return second_table, third_table, back, fore


def pack_kernel(bands, devices, width_second, width_third, trial_ref, cells_ref, packet_ref):
    cells = cells_ref[...].reshape(1, cells_ref.shape[0])
    first = lax.div(cells, width_second * width_third)
    second = lax.rem(lax.div(cells, width_third), width_second)
    third = lax.rem(cells, width_third)
    middle = cells.shape[1] // 2
    halves = [part for row in (first, second, third) for part in (row[:, :middle], row[:, middle:])]
    unused = jnp.zeros((2 * bands - 6, middle), jnp.int32)
    place = jnp.concatenate([*halves, unused]).astype(F32)
    trial = jnp.concatenate([trial_ref[part].astype(F32) for part in range(2)])
    packet = jnp.concatenate([trial, place], axis=1).astype(BF16)
    for p in range(devices):
        packet_ref[p] = packet


def grid_kernel(
    bands,
    waves_ref,
    second_ref,
    third_ref,
    back_ref,
    fore_ref,
    potential_in,
    kinetic_ref,
    occupation_ref,
    sent_ref,
    own_out,
    other_out,
    phase_s,
    select_s,
    slab_s,
    acted_s,
    coef_s,
    potential_ref,
    own_ref,
    other_ref,
    done,
):
    devices, _, length = waves_ref.shape
    count = 2 * length // 3
    fetch = pltpu.make_async_copy(potential_in, potential_ref, done.at[2])
    fetch.start()
    rows, width_first, width_third = potential_ref.shape
    slab = width_first // devices
    half = rows // 2
    share = width_first // 2
    me = lax.axis_index("pw")
    low_side = lax.axis_index("band") == 0
    nt = (((1,), (1,)), ((), ()))
    tn = (((0,), (0,)), ((), ()))
    near = second_ref[me]
    fold = width_third // 2
    full = rows * slab
    groups = bands // 2
    low_lanes = lax.broadcasted_iota(jnp.int32, (1, width_third), 1) < fold
    energies = [jnp.zeros((8, width_third), F32) for _ in range(groups)]
    weights = [
        jnp.where(
            low_lanes, occupation_ref[2 * g].astype(F32), occupation_ref[2 * g + 1].astype(F32)
        )
        for g in range(groups)
    ]
    centres = []

    squares = []

    zero, one = jnp.zeros((), BF16), jnp.ones((), BF16)
    line = lax.broadcasted_iota(jnp.int32, (slab, count), 0).astype(F32).astype(BF16)

    def level(row):
        return jnp.broadcast_to(row, (slab, count)).astype(BF16)

    def one_hot(row):
        target = level(row)
        tiles = [line + jnp.asarray(at, BF16) == target for at in range(0, LANES, slab)]
        return jnp.concatenate([jnp.where(tile, one, zero) for tile in tiles])

    def place(p):
        waves = waves_ref[p].astype(F32)
        first, second, third = [
            jnp.concatenate([waves[i : i + 1, count:], waves[i + 1 : i + 2, count:]], axis=1)
            for i in (0, 2, 4)
        ]
        turn = jnp.dot(near, one_hot(second), preferred_element_type=F32)
        pick = one_hot(third)
        phase_s[p] = jnp.dot(
            third_ref[...], jnp.concatenate([pick, pick]), preferred_element_type=F32
        )
        centre = turn[rows : rows + 2] + turn[rows + 2 : rows + 4]
        centres.append(centre)
        real, imag = waves[:bands, :count], waves[bands:, :count]
        squares.append(real * real + imag * imag)
        turned_real = real * centre[0:1] - imag * centre[1:2]
        turned_imag = real * centre[1:2] + imag * centre[0:1]
        inside = line == level(first)
        sign = level(jnp.where(lax.rem(third.astype(jnp.int32), 2) == 0, 1.0, -1.0))
        for k in range(rows):
            chosen = jnp.where(inside, level(turn[k : k + 1]), zero)
            select_s[p, k * slab : (k + 1) * slab, :] = chosen
            select_s[p, full + k * slab : full + (k + 1) * slab, :] = chosen * sign
        return turned_real, turned_imag

    def weigh(p, g, turned):
        turned_real, turned_imag = turned
        cosines, sines = phase_s[p, :fold], phase_s[p, fold:]
        slot = (p * groups + g) % 2
        for i, n in enumerate((2 * g, 2 * g + 1)):
            a, b = turned_real[n : n + 1], turned_imag[n : n + 1]
            real_rows = slice(i * fold, (i + 1) * fold)
            imag_rows = slice(width_third + i * fold, width_third + (i + 1) * fold)
            coef_s[slot, real_rows, :] = (a * cosines - b * sines).astype(BF16)
            coef_s[slot, imag_rows, :] = (a * sines + b * cosines).astype(BF16)

    def spread(p, g):
        planes = lax.dot_general(
            select_s[p], coef_s[(p * groups + g) % 2], nt, preferred_element_type=F32
        )
        for h in range(2):
            even = planes[h * full : h * full + full // 2]
            odd = planes[h * full + full // 2 : (h + 1) * full]
            even_real, even_imag = even[:, :width_third], even[:, width_third:]
            odd_real, odd_imag = odd[:, :width_third], odd[:, width_third:]
            plus_real = (even_real - odd_imag).astype(BF16)
            plus_imag = (even_imag + odd_real).astype(BF16)
            minus_real = (even_real + odd_imag).astype(BF16)
            minus_imag = (even_imag - odd_real).astype(BF16)
            real_rows = slice(p * slab, (p + 1) * slab)
            imag_rows = slice(width_first + p * slab, width_first + (p + 1) * slab)
            to = slice((2 * g + h) * width_third, (2 * g + h + 1) * width_third)
            for k in range(half):
                part = slice(k * slab, (k + 1) * slab)
                slab_s[half + k, real_rows, to] = plus_real[part]
                slab_s[half + k, imag_rows, to] = plus_imag[part]
                slab_s[half - 1 - k, real_rows, to] = minus_real[part]
                slab_s[half - 1 - k, imag_rows, to] = minus_imag[part]

    steps = [(p, g) for p in range(devices) for g in range(groups)]
    turned = {0: place(0)}
    weigh(0, 0, turned[0])
    for i, (p, g) in enumerate(steps):
        if g == 0 and p + 1 < devices:
            turned[p + 1] = place(p + 1)
        if i + 1 < len(steps):
            weigh(*steps[i + 1], turned[steps[i + 1][0]])
        spread(p, g)
    square = sum(squares)

    fetch.wait()
    blocks = [slice(h * width_third, (h + 1) * width_third) for h in range(2)]
    for k in range(half):
        densities = [[0.0, 0.0], [0.0, 0.0]]
        locals_ = []
        for row in (half + k, half - 1 - k):
            values = potential_ref[row]
            other = pltpu.roll(values, fold, 1)
            locals_.append(
                (jnp.where(low_lanes, values, other), jnp.where(low_lanes, other, values))
            )
        for g in range(groups):
            at = slice(2 * g * width_third, (2 * g + 2) * width_third)
            results = []
            for side, row in enumerate((half + k, half - 1 - k)):
                spatial = jnp.dot(back_ref[...], slab_s[row, :, at], preferred_element_type=F32)
                moved_real, moved_imag = [], []
                for h in range(2):
                    local = locals_[side][h]
                    real = spatial[:width_first, blocks[h]]
                    imag = spatial[width_first:, blocks[h]]
                    power = real * real + imag * imag
                    densities[side][h] = densities[side][h] + weights[g] * power
                    energy = (power * local).reshape(width_first // 8, 8, width_third)
                    energies[g] = energies[g] + jnp.sum(energy, axis=0)
                    moved_real.append((real * local).astype(BF16))
                    moved_imag.append((imag * local).astype(BF16))
                moved = jnp.concatenate(
                    [jnp.concatenate(moved_real, axis=1), jnp.concatenate(moved_imag, axis=1)]
                )
                results.append(jnp.dot(fore_ref[...], moved, preferred_element_type=F32))
            plus, minus = results
            total = (plus + minus).astype(BF16)
            gap = plus - minus
            gap_real = gap[width_first:].astype(BF16)
            gap_imag = (-gap[:width_first]).astype(BF16)
            to_real = slice(2 * g * width_third, (2 * g + 1) * width_third)
            to_imag = slice((2 * g + 1) * width_third, (2 * g + 2) * width_third)
            for p in range(devices):
                mine = slice(p * slab, (p + 1) * slab)
                mine_imag = slice(width_first + p * slab, width_first + (p + 1) * slab)
                for h in range(2):
                    even_rows = slice(h * full + k * slab, h * full + (k + 1) * slab)
                    start = h * full + full // 2 + k * slab
                    odd_rows = slice(start, start + slab)
                    acted_s[p, even_rows, to_real] = total[mine, blocks[h]]
                    acted_s[p, even_rows, to_imag] = total[mine_imag, blocks[h]]
                    acted_s[p, odd_rows, to_real] = gap_real[mine, blocks[h]]
                    acted_s[p, odd_rows, to_imag] = gap_imag[mine, blocks[h]]
        for side, row in enumerate((half + k, half - 1 - k)):
            folded = [d + pltpu.roll(d, fold, 1) for d in densities[side]]
            density = jnp.where(low_lanes, *folded)
            low, high = density[:share], density[share:]
            own_ref[row] = jnp.where(low_side, low, high)
            other_ref[row] = jnp.where(low_side, high, low).astype(BF16)

    stores = [
        pltpu.make_async_copy(own_ref, own_out, done.at[0]),
        pltpu.make_async_copy(other_ref, other_out, done.at[1]),
    ]
    for store in stores:
        store.start()

    waves = waves_ref[me].astype(F32)
    real, imag = waves[:bands, :count], waves[bands:, :count]
    kinetic = kinetic_ref[...].reshape(1, count)
    moving = jnp.sum((real * real + imag * imag) * kinetic, axis=1, keepdims=True)
    energy = []
    for values in energies:
        for part in (jnp.where(low_lanes, values, 0.0), jnp.where(low_lanes, 0.0, values)):
            energy.append(jnp.sum(part, axis=(0, 1), keepdims=True))
    energy = jnp.concatenate(energy)
    numerator = moving + energy
    denominator = jnp.sum(square, axis=1, keepdims=True) * (1.0 / devices)
    scalars = []
    for value in (numerator, denominator):
        high = value.astype(BF16)
        low = (value - high.astype(F32)).astype(BF16)
        both = jnp.concatenate([high.astype(F32), low.astype(F32)])
        scalars.append(jnp.broadcast_to(both, (2 * bands, LANES)))
    scalars = jnp.where(low_lanes, *scalars).astype(BF16)

    for p in range(devices):
        cosines, sines = phase_s[p, :fold], phase_s[p, fold:]
        reals, imags = [], []
        for g in range(groups):
            at = slice(2 * g * width_third, 2 * (g + 1) * width_third)
            found = lax.dot_general(acted_s[p, :, at], select_s[p], tn, preferred_element_type=F32)
            for i in range(2):
                real = found[i * fold : (i + 1) * fold]
                imag = found[width_third + i * fold : width_third + (i + 1) * fold]
                reals.append(
                    jnp.sum(real * cosines, axis=0, keepdims=True)
                    + jnp.sum(imag * sines, axis=0, keepdims=True)
                )
                imags.append(
                    jnp.sum(imag * cosines, axis=0, keepdims=True)
                    - jnp.sum(real * sines, axis=0, keepdims=True)
                )
        real, imag = jnp.concatenate(reals), jnp.concatenate(imags)
        cosine, sine = centres[p][0:1], centres[p][1:2]
        result = jnp.concatenate([real * cosine + imag * sine, imag * cosine - real * sine])
        sent_ref[p, :, :count] = result.astype(BF16)
        sent_ref[p, :, count : count + LANES] = scalars
        sent_ref[p, :, count + LANES :] = jnp.zeros_like(scalars)

    for store in stores:
        store.wait()


def on_grid(waves, potential, kinetic, occupation, bands, width_second):
    devices, _, length = waves.shape
    count = 2 * length // 3
    rows, width_first, width_third = potential.shape
    slab = width_first // devices
    tables = wave_tables(devices, rows, width_first, width_second, width_third)
    vmem = pl.BlockSpec(memory_space=pltpu.VMEM)
    smem = pl.BlockSpec(memory_space=pltpu.SMEM)
    anywhere = pl.BlockSpec(memory_space=pl.ANY)
    planes = (rows, width_first // 2, width_third)
    return pl.pallas_call(
        functools.partial(grid_kernel, bands),
        out_shape=(
            jax.ShapeDtypeStruct((devices, 2 * bands, count + 2 * LANES), BF16),
            jax.ShapeDtypeStruct(planes, F32),
            jax.ShapeDtypeStruct(planes, BF16),
        ),
        in_specs=[vmem] * 5 + [anywhere, vmem, smem],
        out_specs=(vmem, anywhere, anywhere),
        scratch_shapes=[
            pltpu.VMEM((devices, width_third, count), F32),
            pltpu.VMEM((devices, 2 * rows * slab, count), BF16),
            pltpu.VMEM((rows, 2 * width_first, bands * width_third), BF16),
            pltpu.VMEM((devices, 2 * rows * slab, bands * width_third), BF16),
            pltpu.VMEM((2, 2 * width_third, count), BF16),
            pltpu.VMEM(potential.shape, F32),
            pltpu.VMEM(planes, F32),
            pltpu.VMEM(planes, BF16),
            pltpu.SemaphoreType.DMA((3,)),
        ],
        compiler_params=pltpu.CompilerParams(vmem_limit_bytes=56 * 1024 * 1024),
    )(waves, *[jnp.asarray(t) for t in tables], potential, kinetic, occupation)


def action_kernel(bands, arrived_ref, trial_ref, kinetic_ref, rows_ref, rest_ref):
    devices = arrived_ref.shape[0]
    count = kinetic_ref.shape[0]
    block = 2 * bands
    total = sum(arrived_ref[p].astype(F32) for p in range(devices))
    applied = total[:, :count]
    scalars = total[:bands, count:] + total[bands:, count:]
    ratio = scalars[:, 0:1] / (scalars[:, LANES // 2 : LANES // 2 + 1] + EPSILON)
    kinetic = kinetic_ref[...].reshape(1, count)
    damping = 1.0 / (1.0 + kinetic)
    trial = jnp.concatenate([trial_ref[part].astype(F32) for part in range(2)])
    action = kinetic * trial + applied
    damped = (action * damping).astype(BF16).astype(F32)
    soft = (trial * damping).astype(BF16).astype(F32)
    both = jnp.concatenate([ratio, ratio])
    rest_ref[...] = damped - both * soft
    high = ratio.astype(BF16).astype(F32)
    pair = jnp.broadcast_to(jnp.concatenate([high, ratio - high]), (block, LANES))
    unused = jnp.zeros((block, count), F32)
    rows = jnp.concatenate([action, damped, soft, unused])
    tail = jnp.concatenate([pair, pair, pair, pair])
    rows_ref[...] = jnp.concatenate([rows, tail], axis=1).astype(BF16)


def inner_kernel(bands, mine_ref, theirs_ref, all_ref, received_ref, sent_ref, passed_ref):
    count = all_ref.shape[2]
    block = 2 * bands
    first = lax.axis_index("band") == 0
    nt = (((1,), (1,)), ((), ()))
    mine, theirs = mine_ref[...].astype(F32), theirs_ref[...].astype(F32)
    low, high = jnp.where(first, mine, theirs), jnp.where(first, theirs, mine)
    pieces = []
    for at in range(0, 3 * block, bands):
        pieces += [low[at : at + bands], high[at : at + bands]]
    pair = pieces[0][:, count:] + pieces[2][:, count:], pieces[1][:, count:] + pieces[3][:, count:]
    ratio = jnp.concatenate(pair)[:, 0:1]
    rows = jnp.concatenate(pieces)[:, :count].astype(BF16)
    one = lax.dot_general(rows, all_ref[0], nt, preferred_element_type=F32)
    two = lax.dot_general(rows, all_ref[1], nt, preferred_element_type=F32)

    def inner(at):
        real = one[at : at + block] + two[at + block : at + 2 * block]
        imag = one[at + block : at + 2 * block] - two[at : at + block]
        return real, imag

    correlation = inner(0)
    damped = inner(2 * block)
    soft = inner(4 * block)
    coefficients = [d - ratio * s for d, s in zip(damped, soft)]
    sent_ref[...] = jnp.concatenate([*correlation, *coefficients]).astype(BF16)


def project_kernel(bands, parts, *refs):
    terms, (all_ref, rest_ref, _, own_ref, sent_ref) = refs[:parts], refs[parts:]
    block = 2 * bands
    first = lax.axis_index("band") == 0
    total = sum(term[2 * block :].astype(F32) for term in terms)
    coefficients = total.astype(BF16)
    one = jnp.dot(coefficients, all_ref[0], preferred_element_type=F32)
    two = jnp.dot(coefficients, all_ref[1], preferred_element_type=F32)
    real = one[:block] - two[block:]
    imag = one[block:] + two[:block]
    for part, value in enumerate((real, imag)):
        low, high = value[:bands], value[bands:]
        rest = rest_ref[part * bands : (part + 1) * bands]
        own_ref[part] = rest - jnp.where(first, low, high)
        sent_ref[part] = jnp.where(first, high, low)


def swap(values, axis, bit):
    size = lax.axis_size(axis)
    return lax.ppermute(values, axis, [(i, i ^ bit) for i in range(size)])


def in_waves(trial_block, all_bands, potential, rest_density, wave_cells, kinetic, occupation):
    devices = lax.axis_size("pw")
    _, rows, width_third = potential.shape
    width_second = rows * devices
    _, bands, count = trial_block.shape
    states = all_bands.shape[1]
    block = 2 * bands
    vmem = pl.BlockSpec(memory_space=pltpu.VMEM)
    anywhere = pl.BlockSpec(memory_space=pl.ANY)
    params = pltpu.CompilerParams(vmem_limit_bytes=16 * 1024 * 1024)
    packets = pl.pallas_call(
        functools.partial(pack_kernel, bands, devices, width_second, width_third),
        out_shape=jax.ShapeDtypeStruct((devices, block, 3 * count // 2), BF16),
        in_specs=[vmem] * 2,
        out_specs=vmem,
        compiler_params=pltpu.CompilerParams(vmem_limit_bytes=56 * 1024 * 1024),
    )(trial_block, wave_cells)
    waves = lax.all_to_all(packets, "pw", split_axis=0, concat_axis=0, tiled=True)
    partial, density_own, density_other = on_grid(
        waves, potential.transpose(1, 0, 2), kinetic, occupation, bands, width_second
    )
    arrived = lax.all_to_all(partial, "pw", split_axis=0, concat_axis=0, tiled=True)
    received = swap(density_other, "band", 1)
    mine, rest = pl.pallas_call(
        functools.partial(action_kernel, bands),
        out_shape=(
            jax.ShapeDtypeStruct((4 * block, count + LANES), BF16),
            jax.ShapeDtypeStruct((block, count), F32),
        ),
        in_specs=[vmem] * 3,
        out_specs=(vmem, vmem),
        compiler_params=params,
    )(arrived, trial_block, kinetic)
    theirs = swap(mine, "band", 1)
    sums, received = pl.pallas_call(
        functools.partial(inner_kernel, bands),
        out_shape=(
            jax.ShapeDtypeStruct((4 * block, states), BF16),
            jax.ShapeDtypeStruct(received.shape, received.dtype),
        ),
        in_specs=[vmem] * 3 + [anywhere],
        out_specs=(vmem, anywhere),
        input_output_aliases={3: 1},
        compiler_params=params,
    )(mine, theirs, all_bands, received)
    density = rest_density + (density_own + received.astype(F32)).transpose(1, 0, 2)
    near = sums + swap(sums, "pw", 1)
    terms = [near] + [swap(near, "pw", step) for step in range(2, devices, 2)]
    correlation = sum(term[: 2 * block].astype(F32) for term in terms)
    own, sent = pl.pallas_call(
        functools.partial(project_kernel, bands, len(terms)),
        out_shape=(
            jax.ShapeDtypeStruct((2, bands, count), F32),
            jax.ShapeDtypeStruct((2, bands, count), F32),
        ),
        in_specs=[vmem] * (len(terms) + 2) + [anywhere],
        out_specs=(vmem, vmem),
        compiler_params=params,
    )(*terms, all_bands, rest, density)
    correction = own - swap(sent, "band", 1)
    correlation = correlation.reshape(2, block, states).transpose(0, 2, 1)
    return (correction, correlation, density)


def fits(trial_block, potential, mesh):
    devices = mesh.shape["pw"]
    width_first, width_second, width_third = potential.shape[0] // mesh.shape["ens"], *potential.shape[1:]
    slab, rows = width_first // devices, width_second // devices
    bands = trial_block.shape[1] // mesh.shape["band"]
    return (
        mesh.shape["band"] == 2
        and devices >= 2
        and devices & (devices - 1) == 0
        and slab % 16 == 0
        and rows % 16 == 0
        and width_first % LANES == 0
        and width_second == LANES
        and width_third == LANES
        and bands == 4
        and trial_block.shape[2] // devices % (2 * LANES) == 0
    )


def tables(length):
    positions = jnp.arange(length, dtype=jnp.int32)
    products = positions[:, None] * positions[None, :] % length
    angles = products.astype(jnp.float32) * (2.0 * math.pi / length)
    factor = 1.0 / math.sqrt(length)
    cosines = jnp.cos(angles) * factor
    sines = jnp.sin(angles) * factor
    backward = jnp.stack([jnp.stack([cosines, -sines]), jnp.stack([sines, cosines])])
    forward = jnp.stack([jnp.stack([cosines, sines]), jnp.stack([-sines, cosines])])
    return (backward, forward)


def transform(fields, table, formula):
    return jnp.einsum(formula, table, fields, precision=HIGHEST)


def inner(left, right):
    contract = (((1,), (1,)), ((), ()))
    first = lax.dot_general(left[0], right[0], contract, preferred_element_type=jnp.float32)
    second = lax.dot_general(left[1], right[1], contract, preferred_element_type=jnp.float32)
    cross_one = lax.dot_general(left[0], right[1], contract, preferred_element_type=jnp.float32)
    cross_two = lax.dot_general(left[1], right[0], contract, preferred_element_type=jnp.float32)
    return jnp.stack([first + second, cross_one - cross_two])


def on_device(trial_block, all_bands, potential, rest_density, wave_cells, kinetic, occupation):
    devices = lax.axis_size("pw")
    width_first, rows_second, width_third = potential.shape
    width_second = rows_second * devices
    slab_rows = width_first // devices
    blocks = trial_block.shape[1]
    back_first, fore_first = tables(width_first)
    back_second, fore_second = tables(width_second)
    back_third, fore_third = tables(width_third)
    along_third = "pqkc,qnabc->pnabk"
    along_second = "pqkb,qnabc->pnakc"
    along_first = "pqka,qnabc->pnkbc"
    trial_float = trial_block.astype(jnp.float32)
    filled = jnp.zeros((2, blocks, slab_rows * width_second * width_third), jnp.float32)
    filled = filled.at[:, :, wave_cells].set(trial_float)
    filled = filled.reshape(2, blocks, slab_rows, width_second, width_third)
    filled = transform(filled, back_third, along_third)
    filled = transform(filled, back_second, along_second)
    spatial = transform(
        lax.all_to_all(filled, "pw", split_axis=3, concat_axis=2, tiled=True),
        back_first,
        along_first,
    )
    power = spatial[0] * spatial[0] + spatial[1] * spatial[1]
    acted = transform(spatial * potential, fore_first, along_first)
    returned = lax.all_to_all(acted, "pw", split_axis=2, concat_axis=3, tiled=True)
    columns, power = (returned, power[None])
    columns = transform(columns, fore_second, along_second)
    columns = transform(columns, fore_third, along_third)
    applied = columns.reshape(2, blocks, slab_rows * width_second * width_third)[:, :, wave_cells]
    weights = occupation.astype(jnp.float32)
    density_part = jnp.einsum("n,nabc->abc", weights, power[0], precision=HIGHEST)
    summed_density = lax.psum(density_part.astype(jnp.bfloat16), "band").astype(jnp.float32)
    share = width_first // lax.axis_size("band")
    block_density = lax.dynamic_slice_in_dim(
        summed_density, lax.axis_index("band") * share, share, 0
    )
    density = rest_density + block_density
    action = kinetic * trial_float + applied
    damping = 1.0 / (1.0 + kinetic)
    action_half = action.astype(jnp.bfloat16)
    damped = (action * damping).astype(jnp.bfloat16)
    softened = (trial_float * damping).astype(jnp.bfloat16)
    every_trial, every_action, every_damped, every_softened = (
        lax.all_gather(trial_block, "band", axis=1, tiled=True),
        lax.all_gather(action_half, "band", axis=1, tiled=True),
        lax.all_gather(damped, "band", axis=1, tiled=True),
        lax.all_gather(softened, "band", axis=1, tiled=True),
    )
    trial_wide = every_trial.astype(jnp.float32)
    numerator = jnp.sum(trial_wide * every_action.astype(jnp.float32), axis=(0, 2))
    denominator = jnp.sum(trial_wide * trial_wide, axis=(0, 2))
    correlation = inner(all_bands, every_action)
    correlation, numerator, denominator = lax.psum((correlation, numerator, denominator), "pw")
    rayleigh = numerator / (denominator + EPSILON)
    local_terms = inner(all_bands, every_damped) - rayleigh * inner(all_bands, every_softened)
    coefficients = lax.psum(local_terms, "pw")
    coefficient_half = coefficients.astype(jnp.bfloat16)
    real_piece = coefficient_half[0]
    imag_piece = coefficient_half[1]
    contract = (((0,), (0,)), ((), ()))
    real_real = lax.dot_general(
        real_piece, all_bands[0], contract, preferred_element_type=jnp.float32
    )
    imag_imag = lax.dot_general(
        imag_piece, all_bands[1], contract, preferred_element_type=jnp.float32
    )
    imag_real = lax.dot_general(
        imag_piece, all_bands[0], contract, preferred_element_type=jnp.float32
    )
    real_imag = lax.dot_general(
        real_piece, all_bands[1], contract, preferred_element_type=jnp.float32
    )
    projected = lax.psum_scatter(
        jnp.concatenate(
            [(real_real - imag_imag)[:, None], (imag_real + real_imag)[:, None]], axis=1
        ),
        "band",
        scatter_dimension=0,
        tiled=True,
    )
    own_ratio = lax.dynamic_slice_in_dim(rayleigh, lax.axis_index("band") * blocks, blocks, 0)
    real_correction = (
        damped[0].astype(jnp.float32)
        - own_ratio[:, None] * softened[0].astype(jnp.float32)
        - projected[:, 0]
    )
    imag_correction = (
        damped[1].astype(jnp.float32)
        - own_ratio[:, None] * softened[1].astype(jnp.float32)
        - projected[:, 1]
    )
    correction = jnp.stack([real_correction, imag_correction])
    return (correction, correlation, density)


def solution(mesh):
    placed = (
        P("ens", "band", "pw"),
        P("ens", "band", "pw"),
        P("ens", "pw", None),
        P(("ens", "band"), "pw", None),
        P("pw"),
        P("pw"),
        P(("ens", "band")),
    )
    results = (P("ens", "band", "pw"), P("ens", "band", None), P(("ens", "band"), "pw", None))

    def program(*arguments):
        body = in_waves if fits(arguments[0], arguments[2], mesh) else on_device
        return jax.shard_map(
            body, mesh=mesh, in_specs=placed, out_specs=results, check_vma=False
        )(*arguments)

    return program
```

```python
import functools
import math

import jax
import jax.numpy as jnp
import numpy as np
from jax import lax
from jax.experimental import pallas as pl
from jax.experimental.pallas import tpu as pltpu
from jax.sharding import PartitionSpec as P

EPSILON = 1e-06
HIGHEST = lax.Precision.HIGHEST
BF16 = jnp.bfloat16
F32 = jnp.float32
LANES = 128


def split_pair(values):
    high = values.astype(BF16)
    low = (values - high.astype(np.float64)).astype(BF16)
    return high, low


def wave_tables(devices, rows, width_first, width_second, width_third):
    half = rows // 2
    second = np.arange(width_second)
    steps = np.outer(2 * np.arange(half) + 1, second) % (2 * width_second)
    angles = steps * (math.pi / width_second)
    near = np.concatenate([np.cos(angles), np.sin(angles)])
    blocks = []
    for device in range(devices):
        middle = 2 * rows * device + rows - 1
        turns = (middle * second % (2 * width_second)) * (math.pi / width_second)
        centre = np.stack([np.cos(turns), np.sin(turns)])
        high, low = split_pair(centre)
        blocks.append(np.concatenate([near.astype(BF16), high, low]))
    second_table = np.stack(blocks)
    missing = -second_table.shape[1] % 16
    second_table = np.pad(second_table, ((0, 0), (0, missing), (0, 0)))
    third = np.arange(width_third)
    angles = np.outer(third[: width_third // 2], third) % width_third * (2 * math.pi / width_third)
    factor = 1.0 / math.sqrt(width_second * width_third)
    values = np.concatenate([np.cos(angles), np.sin(angles)]) * factor
    third_table = np.concatenate(split_pair(values), axis=1)
    first = np.arange(width_first)
    angles = (np.outer(first, first) % width_first) * (2 * math.pi / width_first)
    cosines, sines = np.cos(angles), np.sin(angles)
    scale = 2.0 ** -math.ceil(math.log2(width_first) / 2)
    back = (np.block([[cosines, -sines], [sines, cosines]]) * scale).astype(BF16)
    scale = 1.0 / (width_first * scale)
    fore = (np.block([[cosines, sines], [-sines, cosines]]) * scale).astype(BF16)
    return second_table, third_table, back, fore


def pack_kernel(bands, devices, width_second, width_third, trial_ref, cells_ref, packet_ref):
    cells = cells_ref[...].reshape(1, cells_ref.shape[0])
    first = lax.div(cells, width_second * width_third)
    second = lax.rem(lax.div(cells, width_third), width_second)
    third = lax.rem(cells, width_third)
    middle = cells.shape[1] // 2
    halves = [part for row in (first, second, third) for part in (row[:, :middle], row[:, middle:])]
    unused = jnp.zeros((2 * bands - 6, middle), jnp.int32)
    place = jnp.concatenate([*halves, unused]).astype(F32)
    trial = jnp.concatenate([trial_ref[part].astype(F32) for part in range(2)])
    packet = jnp.concatenate([trial, place], axis=1).astype(BF16)
    for p in range(devices):
        packet_ref[p] = packet


def grid_kernel(
    bands,
    waves_ref,
    second_ref,
    third_ref,
    back_ref,
    fore_ref,
    potential_in,
    kinetic_ref,
    occupation_ref,
    sent_ref,
    own_out,
    other_out,
    phase_s,
    select_s,
    slab_s,
    acted_s,
    coef_s,
    potential_ref,
    own_ref,
    other_ref,
    done,
):
    devices, _, length = waves_ref.shape
    count = 2 * length // 3
    fetch = pltpu.make_async_copy(potential_in, potential_ref, done.at[2])
    fetch.start()
    rows, width_first, width_third = potential_ref.shape
    slab = width_first // devices
    half = rows // 2
    share = width_first // 2
    me = lax.axis_index("pw")
    low_side = lax.axis_index("band") == 0
    nt = (((1,), (1,)), ((), ()))
    tn = (((0,), (0,)), ((), ()))
    near = second_ref[me]
    fold = width_third // 2
    full = rows * slab
    groups = bands // 2
    low_lanes = lax.broadcasted_iota(jnp.int32, (1, width_third), 1) < fold
    lift = 2.0 ** (2 * math.ceil(math.log2(width_first) / 2)) / width_first
    energies = [jnp.zeros((8, width_third), F32) for _ in range(groups)]
    weights = [
        jnp.where(
            low_lanes, occupation_ref[2 * g].astype(F32), occupation_ref[2 * g + 1].astype(F32)
        )
        * lift
        for g in range(groups)
    ]
    centres = []

    squares = []

    zero, one = jnp.zeros((), BF16), jnp.ones((), BF16)
    line = lax.broadcasted_iota(jnp.int32, (slab, count), 0).astype(F32).astype(BF16)

    def level(row):
        return jnp.broadcast_to(row, (slab, count)).astype(BF16)

    def one_hot(row):
        target = level(row)
        tiles = [line + jnp.asarray(at, BF16) == target for at in range(0, LANES, slab)]
        return jnp.concatenate([jnp.where(tile, one, zero) for tile in tiles])

    def place(p):
        waves = waves_ref[p].astype(F32)
        first, second, third = [
            jnp.concatenate([waves[i : i + 1, count:], waves[i + 1 : i + 2, count:]], axis=1)
            for i in (0, 2, 4)
        ]
        turn = jnp.dot(near, one_hot(second), preferred_element_type=F32)
        pick = one_hot(third)
        phase_s[p] = jnp.dot(
            third_ref[...], jnp.concatenate([pick, pick]), preferred_element_type=F32
        )
        centre = turn[rows : rows + 2] + turn[rows + 2 : rows + 4]
        centres.append(centre)
        real, imag = waves[:bands, :count], waves[bands:, :count]
        squares.append(real * real + imag * imag)
        turned_real = real * centre[0:1] - imag * centre[1:2]
        turned_imag = real * centre[1:2] + imag * centre[0:1]
        inside = line == level(first)
        sign = level(jnp.where(lax.rem(third.astype(jnp.int32), 2) == 0, 1.0, -1.0))
        for k in range(rows):
            chosen = jnp.where(inside, level(turn[k : k + 1]), zero)
            select_s[p, k * slab : (k + 1) * slab, :] = chosen
            select_s[p, full + k * slab : full + (k + 1) * slab, :] = chosen * sign
        return turned_real, turned_imag

    def weigh(p, g, turned):
        turned_real, turned_imag = turned
        cosines, sines = phase_s[p, :fold], phase_s[p, fold:]
        slot = (p * groups + g) % 2
        for i, n in enumerate((2 * g, 2 * g + 1)):
            a, b = turned_real[n : n + 1], turned_imag[n : n + 1]
            real_rows = slice(i * fold, (i + 1) * fold)
            imag_rows = slice(width_third + i * fold, width_third + (i + 1) * fold)
            coef_s[slot, real_rows, :] = (a * cosines - b * sines).astype(BF16)
            coef_s[slot, imag_rows, :] = (a * sines + b * cosines).astype(BF16)

    def spread(p, g):
        planes = lax.dot_general(
            select_s[p], coef_s[(p * groups + g) % 2], nt, preferred_element_type=F32
        )
        for h in range(2):
            even = planes[h * full : h * full + full // 2]
            odd = planes[h * full + full // 2 : (h + 1) * full]
            even_real, even_imag = even[:, :width_third], even[:, width_third:]
            odd_real, odd_imag = odd[:, :width_third], odd[:, width_third:]
            plus_real = (even_real - odd_imag).astype(BF16)
            plus_imag = (even_imag + odd_real).astype(BF16)
            minus_real = (even_real + odd_imag).astype(BF16)
            minus_imag = (even_imag - odd_real).astype(BF16)
            real_rows = slice(p * slab, (p + 1) * slab)
            imag_rows = slice(width_first + p * slab, width_first + (p + 1) * slab)
            to = slice((2 * g + h) * width_third, (2 * g + h + 1) * width_third)
            for k in range(half):
                part = slice(k * slab, (k + 1) * slab)
                slab_s[half + k, real_rows, to] = plus_real[part]
                slab_s[half + k, imag_rows, to] = plus_imag[part]
                slab_s[half - 1 - k, real_rows, to] = minus_real[part]
                slab_s[half - 1 - k, imag_rows, to] = minus_imag[part]

    steps = [(p, g) for p in range(devices) for g in range(groups)]
    turned = {0: place(0)}
    weigh(0, 0, turned[0])
    for i, (p, g) in enumerate(steps):
        if g == 0 and p + 1 < devices:
            turned[p + 1] = place(p + 1)
        if i + 1 < len(steps):
            weigh(*steps[i + 1], turned[steps[i + 1][0]])
        spread(p, g)
    square = sum(squares)

    fetch.wait()
    blocks = [slice(h * width_third, (h + 1) * width_third) for h in range(2)]
    for k in range(half):
        densities = [[0.0, 0.0], [0.0, 0.0]]
        locals_ = []
        for row in (half + k, half - 1 - k):
            values = potential_ref[row]
            other = pltpu.roll(values, fold, 1)
            locals_.append(
                (jnp.where(low_lanes, values, other), jnp.where(low_lanes, other, values))
            )
        for g in range(groups):
            at = slice(2 * g * width_third, (2 * g + 2) * width_third)
            results = []
            for side, row in enumerate((half + k, half - 1 - k)):
                spatial = jnp.dot(back_ref[...], slab_s[row, :, at], preferred_element_type=F32)
                moved_real, moved_imag = [], []
                for h in range(2):
                    local = locals_[side][h]
                    real = spatial[:width_first, blocks[h]]
                    imag = spatial[width_first:, blocks[h]]
                    power = real * real + imag * imag
                    densities[side][h] = densities[side][h] + weights[g] * power
                    energy = (power * local).reshape(width_first // 8, 8, width_third)
                    energies[g] = energies[g] + jnp.sum(energy, axis=0)
                    moved_real.append((real * local).astype(BF16))
                    moved_imag.append((imag * local).astype(BF16))
                moved = jnp.concatenate(
                    [jnp.concatenate(moved_real, axis=1), jnp.concatenate(moved_imag, axis=1)]
                )
                results.append(jnp.dot(fore_ref[...], moved, preferred_element_type=F32))
            plus, minus = results
            total = (plus + minus).astype(BF16)
            gap = plus - minus
            gap_real = gap[width_first:].astype(BF16)
            gap_imag = (-gap[:width_first]).astype(BF16)
            to_real = slice(2 * g * width_third, (2 * g + 1) * width_third)
            to_imag = slice((2 * g + 1) * width_third, (2 * g + 2) * width_third)
            for p in range(devices):
                mine = slice(p * slab, (p + 1) * slab)
                mine_imag = slice(width_first + p * slab, width_first + (p + 1) * slab)
                for h in range(2):
                    even_rows = slice(h * full + k * slab, h * full + (k + 1) * slab)
                    start = h * full + full // 2 + k * slab
                    odd_rows = slice(start, start + slab)
                    acted_s[p, even_rows, to_real] = total[mine, blocks[h]]
                    acted_s[p, even_rows, to_imag] = total[mine_imag, blocks[h]]
                    acted_s[p, odd_rows, to_real] = gap_real[mine, blocks[h]]
                    acted_s[p, odd_rows, to_imag] = gap_imag[mine, blocks[h]]
        for side, row in enumerate((half + k, half - 1 - k)):
            folded = [d + pltpu.roll(d, fold, 1) for d in densities[side]]
            density = jnp.where(low_lanes, *folded)
            low, high = density[:share], density[share:]
            own_ref[row] = jnp.where(low_side, low, high)
            other_ref[row] = jnp.where(low_side, high, low).astype(BF16)

    stores = [
        pltpu.make_async_copy(own_ref, own_out, done.at[0]),
        pltpu.make_async_copy(other_ref, other_out, done.at[1]),
    ]
    for store in stores:
        store.start()

    waves = waves_ref[me].astype(F32)
    real, imag = waves[:bands, :count], waves[bands:, :count]
    kinetic = kinetic_ref[...].reshape(1, count)
    moving = jnp.sum((real * real + imag * imag) * kinetic, axis=1, keepdims=True)
    energy = []
    for values in energies:
        for part in (jnp.where(low_lanes, values, 0.0), jnp.where(low_lanes, 0.0, values)):
            energy.append(jnp.sum(part, axis=(0, 1), keepdims=True))
    energy = jnp.concatenate(energy)
    numerator = moving + lift * energy
    denominator = jnp.sum(square, axis=1, keepdims=True) * (1.0 / devices)
    scalars = []
    for value in (numerator, denominator):
        high = value.astype(BF16)
        low = (value - high.astype(F32)).astype(BF16)
        both = jnp.concatenate([high.astype(F32), low.astype(F32)])
        scalars.append(jnp.broadcast_to(both, (2 * bands, LANES)))
    scalars = jnp.where(low_lanes, *scalars).astype(BF16)

    for p in range(devices):
        cosines, sines = phase_s[p, :fold], phase_s[p, fold:]
        reals, imags = [], []
        for g in range(groups):
            at = slice(2 * g * width_third, 2 * (g + 1) * width_third)
            found = lax.dot_general(acted_s[p, :, at], select_s[p], tn, preferred_element_type=F32)
            for i in range(2):
                real = found[i * fold : (i + 1) * fold]
                imag = found[width_third + i * fold : width_third + (i + 1) * fold]
                reals.append(
                    jnp.sum(real * cosines, axis=0, keepdims=True)
                    + jnp.sum(imag * sines, axis=0, keepdims=True)
                )
                imags.append(
                    jnp.sum(imag * cosines, axis=0, keepdims=True)
                    - jnp.sum(real * sines, axis=0, keepdims=True)
                )
        real, imag = jnp.concatenate(reals), jnp.concatenate(imags)
        cosine, sine = centres[p][0:1], centres[p][1:2]
        result = jnp.concatenate([real * cosine + imag * sine, imag * cosine - real * sine])
        sent_ref[p, :, :count] = result.astype(BF16)
        sent_ref[p, :, count : count + LANES] = scalars
        sent_ref[p, :, count + LANES :] = jnp.zeros_like(scalars)

    for store in stores:
        store.wait()


def on_grid(waves, potential, kinetic, occupation, bands, width_second):
    devices, _, length = waves.shape
    count = 2 * length // 3
    rows, width_first, width_third = potential.shape
    slab = width_first // devices
    tables = wave_tables(devices, rows, width_first, width_second, width_third)
    vmem = pl.BlockSpec(memory_space=pltpu.VMEM)
    smem = pl.BlockSpec(memory_space=pltpu.SMEM)
    anywhere = pl.BlockSpec(memory_space=pl.ANY)
    planes = (rows, width_first // 2, width_third)
    return pl.pallas_call(
        functools.partial(grid_kernel, bands),
        out_shape=(
            jax.ShapeDtypeStruct((devices, 2 * bands, count + 2 * LANES), BF16),
            jax.ShapeDtypeStruct(planes, F32),
            jax.ShapeDtypeStruct(planes, BF16),
        ),
        in_specs=[vmem] * 5 + [anywhere, vmem, smem],
        out_specs=(vmem, anywhere, anywhere),
        scratch_shapes=[
            pltpu.VMEM((devices, width_third, count), F32),
            pltpu.VMEM((devices, 2 * rows * slab, count), BF16),
            pltpu.VMEM((rows, 2 * width_first, bands * width_third), BF16),
            pltpu.VMEM((devices, 2 * rows * slab, bands * width_third), BF16),
            pltpu.VMEM((2, 2 * width_third, count), BF16),
            pltpu.VMEM(potential.shape, F32),
            pltpu.VMEM(planes, F32),
            pltpu.VMEM(planes, BF16),
            pltpu.SemaphoreType.DMA((3,)),
        ],
        compiler_params=pltpu.CompilerParams(vmem_limit_bytes=56 * 1024 * 1024),
    )(waves, *[jnp.asarray(t) for t in tables], potential, kinetic, occupation)


def action_kernel(bands, arrived_ref, trial_ref, kinetic_ref, rows_ref, rest_ref):
    devices = arrived_ref.shape[0]
    count = kinetic_ref.shape[0]
    block = 2 * bands
    total = sum(arrived_ref[p].astype(F32) for p in range(devices))
    applied = total[:, :count]
    scalars = total[:bands, count:] + total[bands:, count:]
    ratio = scalars[:, 0:1] / (scalars[:, LANES // 2 : LANES // 2 + 1] + EPSILON)
    kinetic = kinetic_ref[...].reshape(1, count)
    damping = 1.0 / (1.0 + kinetic)
    trial = jnp.concatenate([trial_ref[part].astype(F32) for part in range(2)])
    action = kinetic * trial + applied
    damped = (action * damping).astype(BF16).astype(F32)
    soft = (trial * damping).astype(BF16).astype(F32)
    both = jnp.concatenate([ratio, ratio])
    rest_ref[...] = damped - both * soft
    high = ratio.astype(BF16).astype(F32)
    pair = jnp.broadcast_to(jnp.concatenate([high, ratio - high]), (block, LANES))
    unused = jnp.zeros((block, count), F32)
    rows = jnp.concatenate([action, damped, soft, unused])
    tail = jnp.concatenate([pair, pair, pair, pair])
    rows_ref[...] = jnp.concatenate([rows, tail], axis=1).astype(BF16)


def inner_kernel(bands, mine_ref, theirs_ref, all_ref, received_ref, sent_ref, passed_ref):
    count = all_ref.shape[2]
    block = 2 * bands
    first = lax.axis_index("band") == 0
    nt = (((1,), (1,)), ((), ()))
    mine, theirs = mine_ref[...].astype(F32), theirs_ref[...].astype(F32)
    low, high = jnp.where(first, mine, theirs), jnp.where(first, theirs, mine)
    pieces = []
    for at in range(0, 3 * block, bands):
        pieces += [low[at : at + bands], high[at : at + bands]]
    pair = pieces[0][:, count:] + pieces[2][:, count:], pieces[1][:, count:] + pieces[3][:, count:]
    ratio = jnp.concatenate(pair)[:, 0:1]
    rows = jnp.concatenate(pieces)[:, :count].astype(BF16)
    one = lax.dot_general(rows, all_ref[0], nt, preferred_element_type=F32)
    two = lax.dot_general(rows, all_ref[1], nt, preferred_element_type=F32)

    def inner(at):
        real = one[at : at + block] + two[at + block : at + 2 * block]
        imag = one[at + block : at + 2 * block] - two[at : at + block]
        return real, imag

    correlation = inner(0)
    damped = inner(2 * block)
    soft = inner(4 * block)
    coefficients = [d - ratio * s for d, s in zip(damped, soft)]
    sent_ref[...] = jnp.concatenate([*correlation, *coefficients]).astype(BF16)


def project_kernel(bands, parts, *refs):
    terms, (all_ref, rest_ref, _, own_ref, sent_ref) = refs[:parts], refs[parts:]
    block = 2 * bands
    first = lax.axis_index("band") == 0
    total = sum(term[2 * block :].astype(F32) for term in terms)
    coefficients = total.astype(BF16)
    one = jnp.dot(coefficients, all_ref[0], preferred_element_type=F32)
    two = jnp.dot(coefficients, all_ref[1], preferred_element_type=F32)
    real = one[:block] - two[block:]
    imag = one[block:] + two[:block]
    for part, value in enumerate((real, imag)):
        low, high = value[:bands], value[bands:]
        rest = rest_ref[part * bands : (part + 1) * bands]
        own_ref[part] = rest - jnp.where(first, low, high)
        sent_ref[part] = jnp.where(first, high, low)


def swap(values, axis, bit):
    size = lax.axis_size(axis)
    return lax.ppermute(values, axis, [(i, i ^ bit) for i in range(size)])


def in_waves(trial_block, all_bands, potential, rest_density, wave_cells, kinetic, occupation):
    devices = lax.axis_size("pw")
    _, rows, width_third = potential.shape
    width_second = rows * devices
    _, bands, count = trial_block.shape
    states = all_bands.shape[1]
    block = 2 * bands
    vmem = pl.BlockSpec(memory_space=pltpu.VMEM)
    anywhere = pl.BlockSpec(memory_space=pl.ANY)
    params = pltpu.CompilerParams(vmem_limit_bytes=16 * 1024 * 1024)
    packets = pl.pallas_call(
        functools.partial(pack_kernel, bands, devices, width_second, width_third),
        out_shape=jax.ShapeDtypeStruct((devices, block, 3 * count // 2), BF16),
        in_specs=[vmem] * 2,
        out_specs=vmem,
        compiler_params=pltpu.CompilerParams(vmem_limit_bytes=56 * 1024 * 1024),
    )(trial_block, wave_cells)
    waves = lax.all_to_all(packets, "pw", split_axis=0, concat_axis=0, tiled=True)
    partial, density_own, density_other = on_grid(
        waves, potential.transpose(1, 0, 2), kinetic, occupation, bands, width_second
    )
    arrived = lax.all_to_all(partial, "pw", split_axis=0, concat_axis=0, tiled=True)
    received = swap(density_other, "band", 1)
    mine, rest = pl.pallas_call(
        functools.partial(action_kernel, bands),
        out_shape=(
            jax.ShapeDtypeStruct((4 * block, count + LANES), BF16),
            jax.ShapeDtypeStruct((block, count), F32),
        ),
        in_specs=[vmem] * 3,
        out_specs=(vmem, vmem),
        compiler_params=params,
    )(arrived, trial_block, kinetic)
    theirs = swap(mine, "band", 1)
    sums, received = pl.pallas_call(
        functools.partial(inner_kernel, bands),
        out_shape=(
            jax.ShapeDtypeStruct((4 * block, states), BF16),
            jax.ShapeDtypeStruct(received.shape, received.dtype),
        ),
        in_specs=[vmem] * 3 + [anywhere],
        out_specs=(vmem, anywhere),
        input_output_aliases={3: 1},
        compiler_params=params,
    )(mine, theirs, all_bands, received)
    density = rest_density + (density_own + received.astype(F32)).transpose(1, 0, 2)
    near = sums + swap(sums, "pw", 1)
    terms = [near] + [swap(near, "pw", step) for step in range(2, devices, 2)]
    correlation = sum(term[: 2 * block].astype(F32) for term in terms)
    own, sent = pl.pallas_call(
        functools.partial(project_kernel, bands, len(terms)),
        out_shape=(
            jax.ShapeDtypeStruct((2, bands, count), F32),
            jax.ShapeDtypeStruct((2, bands, count), F32),
        ),
        in_specs=[vmem] * (len(terms) + 2) + [anywhere],
        out_specs=(vmem, vmem),
        compiler_params=params,
    )(*terms, all_bands, rest, density)
    correction = own - swap(sent, "band", 1)
    correlation = correlation.reshape(2, block, states).transpose(0, 2, 1)
    return (correction, correlation, density)


def fits(trial_block, potential, mesh):
    devices = mesh.shape["pw"]
    width_first, width_second, width_third = potential.shape[0] // mesh.shape["ens"], *potential.shape[1:]
    slab, rows = width_first // devices, width_second // devices
    bands = trial_block.shape[1] // mesh.shape["band"]
    return (
        mesh.shape["band"] == 2
        and devices >= 2
        and devices & (devices - 1) == 0
        and slab % 16 == 0
        and rows % 16 == 0
        and width_first % LANES == 0
        and width_second == LANES
        and width_third == LANES
        and bands == 4
        and trial_block.shape[2] // devices % (2 * LANES) == 0
    )


def tables(length):
    positions = jnp.arange(length, dtype=jnp.int32)
    products = positions[:, None] * positions[None, :] % length
    angles = products.astype(jnp.float32) * (2.0 * math.pi / length)
    factor = 1.0 / math.sqrt(length)
    cosines = jnp.cos(angles) * factor
    sines = jnp.sin(angles) * factor
    backward = jnp.stack([jnp.stack([cosines, -sines]), jnp.stack([sines, cosines])])
    forward = jnp.stack([jnp.stack([cosines, sines]), jnp.stack([-sines, cosines])])
    return (backward, forward)


def transform(fields, table, formula):
    return jnp.einsum(formula, table, fields, precision=HIGHEST)


def inner(left, right):
    contract = (((1,), (1,)), ((), ()))
    first = lax.dot_general(left[0], right[0], contract, preferred_element_type=jnp.float32)
    second = lax.dot_general(left[1], right[1], contract, preferred_element_type=jnp.float32)
    cross_one = lax.dot_general(left[0], right[1], contract, preferred_element_type=jnp.float32)
    cross_two = lax.dot_general(left[1], right[0], contract, preferred_element_type=jnp.float32)
    return jnp.stack([first + second, cross_one - cross_two])


def on_device(trial_block, all_bands, potential, rest_density, wave_cells, kinetic, occupation):
    devices = lax.axis_size("pw")
    width_first, rows_second, width_third = potential.shape
    width_second = rows_second * devices
    slab_rows = width_first // devices
    blocks = trial_block.shape[1]
    back_first, fore_first = tables(width_first)
    back_second, fore_second = tables(width_second)
    back_third, fore_third = tables(width_third)
    along_third = "pqkc,qnabc->pnabk"
    along_second = "pqkb,qnabc->pnakc"
    along_first = "pqka,qnabc->pnkbc"
    trial_float = trial_block.astype(jnp.float32)
    filled = jnp.zeros((2, blocks, slab_rows * width_second * width_third), jnp.float32)
    filled = filled.at[:, :, wave_cells].set(trial_float)
    filled = filled.reshape(2, blocks, slab_rows, width_second, width_third)
    filled = transform(filled, back_third, along_third)
    filled = transform(filled, back_second, along_second)
    spatial = transform(
        lax.all_to_all(filled, "pw", split_axis=3, concat_axis=2, tiled=True),
        back_first,
        along_first,
    )
    power = spatial[0] * spatial[0] + spatial[1] * spatial[1]
    acted = transform(spatial * potential, fore_first, along_first)
    returned = lax.all_to_all(acted, "pw", split_axis=2, concat_axis=3, tiled=True)
    columns, power = (returned, power[None])
    columns = transform(columns, fore_second, along_second)
    columns = transform(columns, fore_third, along_third)
    applied = columns.reshape(2, blocks, slab_rows * width_second * width_third)[:, :, wave_cells]
    weights = occupation.astype(jnp.float32)
    density_part = jnp.einsum("n,nabc->abc", weights, power[0], precision=HIGHEST)
    summed_density = lax.psum(density_part.astype(jnp.bfloat16), "band").astype(jnp.float32)
    share = width_first // lax.axis_size("band")
    block_density = lax.dynamic_slice_in_dim(
        summed_density, lax.axis_index("band") * share, share, 0
    )
    density = rest_density + block_density
    action = kinetic * trial_float + applied
    damping = 1.0 / (1.0 + kinetic)
    action_half = action.astype(jnp.bfloat16)
    damped = (action * damping).astype(jnp.bfloat16)
    softened = (trial_float * damping).astype(jnp.bfloat16)
    every_trial, every_action, every_damped, every_softened = (
        lax.all_gather(trial_block, "band", axis=1, tiled=True),
        lax.all_gather(action_half, "band", axis=1, tiled=True),
        lax.all_gather(damped, "band", axis=1, tiled=True),
        lax.all_gather(softened, "band", axis=1, tiled=True),
    )
    trial_wide = every_trial.astype(jnp.float32)
    numerator = jnp.sum(trial_wide * every_action.astype(jnp.float32), axis=(0, 2))
    denominator = jnp.sum(trial_wide * trial_wide, axis=(0, 2))
    correlation = inner(all_bands, every_action)
    correlation, numerator, denominator = lax.psum((correlation, numerator, denominator), "pw")
    rayleigh = numerator / (denominator + EPSILON)
    local_terms = inner(all_bands, every_damped) - rayleigh * inner(all_bands, every_softened)
    coefficients = lax.psum(local_terms, "pw")
    coefficient_half = coefficients.astype(jnp.bfloat16)
    real_piece = coefficient_half[0]
    imag_piece = coefficient_half[1]
    contract = (((0,), (0,)), ((), ()))
    real_real = lax.dot_general(
        real_piece, all_bands[0], contract, preferred_element_type=jnp.float32
    )
    imag_imag = lax.dot_general(
        imag_piece, all_bands[1], contract, preferred_element_type=jnp.float32
    )
    imag_real = lax.dot_general(
        imag_piece, all_bands[0], contract, preferred_element_type=jnp.float32
    )
    real_imag = lax.dot_general(
        real_piece, all_bands[1], contract, preferred_element_type=jnp.float32
    )
    projected = lax.psum_scatter(
        jnp.concatenate(
            [(real_real - imag_imag)[:, None], (imag_real + real_imag)[:, None]], axis=1
        ),
        "band",
        scatter_dimension=0,
        tiled=True,
    )
    own_ratio = lax.dynamic_slice_in_dim(rayleigh, lax.axis_index("band") * blocks, blocks, 0)
    real_correction = (
        damped[0].astype(jnp.float32)
        - own_ratio[:, None] * softened[0].astype(jnp.float32)
        - projected[:, 0]
    )
    imag_correction = (
        damped[1].astype(jnp.float32)
        - own_ratio[:, None] * softened[1].astype(jnp.float32)
        - projected[:, 1]
    )
    correction = jnp.stack([real_correction, imag_correction])
    return (correction, correlation, density)


def solution(mesh):
    placed = (
        P("ens", "band", "pw"),
        P("ens", "band", "pw"),
        P("ens", "pw", None),
        P(("ens", "band"), "pw", None),
        P("pw"),
        P("pw"),
        P(("ens", "band")),
    )
    results = (P("ens", "band", "pw"), P("ens", "band", None), P(("ens", "band"), "pw", None))

    def program(*arguments):
        body = in_waves if fits(arguments[0], arguments[2], mesh) else on_device
        return jax.shard_map(
            body, mesh=mesh, in_specs=placed, out_specs=results, check_vma=False
        )(*arguments)

    return program
```
